128 devices in a mesh: dp: 8 (over z, core), shard: 16 (over x, y).
Axes of the slice: x: 4, y: 4, z: 4, core: 2. Of those that a mesh axis runs over, the one named last changes fastest.
Arguments:
- tokens: bfloat16 [16, 2048, 1024], P('shard', 'dp'), may hold values from -6 to 6
- cotangent: bfloat16 [16, 2048, 1024], P('shard', 'dp'), may hold values from -6 to 6
- lengths: int32 [16, 4], P('shard'), may hold values from 1 to 1920, 2048 in all within a row
- weight_input: float32 [1024, 4096], P(('dp', 'shard')), may hold values from -0.1875 to 0.1875
- weight_output: float32 [2048, 1024], P(('dp', 'shard')), may hold values from -1 to 1
- weight_expand: float32 [1024, 6144], P(('dp', 'shard')), may hold values from -0.1875 to 0.1875
- weight_reduce: float32 [3072, 1024], P(('dp', 'shard')), may hold values from -0.109375 to 0.109375
- gains: float32 [2304], P(('dp', 'shard')), may hold values from 0.5 to 1.5
- first_input: float32 [1024, 4096], P(('dp', 'shard')), may hold values from -128 to 128
- first_output: float32 [2048, 1024], P(('dp', 'shard')), may hold values from -20 to 20
- first_expand: float32 [1024, 6144], P(('dp', 'shard')), may hold values from -64 to 64
- first_reduce: float32 [3072, 1024], P(('dp', 'shard')), may hold values from -64 to 64
- first_gains: float32 [2304], P(('dp', 'shard')), may hold values from -128 to 128
- second_input: float32 [1024, 4096], P(('dp', 'shard')), may hold values from 1723.5968 to 6881.28
- second_output: float32 [2048, 1024], P(('dp', 'shard')), may hold values from 49.152 to 196.608
- second_expand: float32 [1024, 6144], P(('dp', 'shard')), may hold values from 622.592 to 2490.368
- second_reduce: float32 [3072, 1024], P(('dp', 'shard')), may hold values from 622.592 to 2490.368
- second_gains: float32 [2304], P(('dp', 'shard')), may hold values from 1723.5968 to 6881.28
Outputs:
- block_out: bfloat16 [16, 2048, 1024], P('shard', 'dp')
- input_grad: float32 [16, 2048, 1024], P('shard', 'dp')
- new_input: float32 [1024, 4096], P(('dp', 'shard'))
- new_output: float32 [2048, 1024], P(('dp', 'shard'))
- new_expand: float32 [1024, 6144], P(('dp', 'shard'))
- new_reduce: float32 [3072, 1024], P(('dp', 'shard'))
- new_gains: float32 [2304], P(('dp', 'shard'))
- mean_input: float32 [1024, 4096], P(('dp', 'shard'))
- mean_output: float32 [2048, 1024], P(('dp', 'shard'))
- mean_expand: float32 [1024, 6144], P(('dp', 'shard'))
- mean_reduce: float32 [3072, 1024], P(('dp', 'shard'))
- mean_gains: float32 [2304], P(('dp', 'shard'))
- square_input: float32 [1024, 4096], P(('dp', 'shard'))
- square_output: float32 [2048, 1024], P(('dp', 'shard'))
- square_expand: float32 [1024, 6144], P(('dp', 'shard'))
- square_reduce: float32 [3072, 1024], P(('dp', 'shard'))
- square_gains: float32 [2304], P(('dp', 'shard'))
The draws below stay inside these ranges and needn't reach their ends.
Inputs may be any that keep to these rules, and one draw needn't show every extreme that they name: `lengths`: each row sums to 2048; the longest sequence of every row has exactly 1920 tokens.
All inputs are finite; a program needn't handle non-finite values.
Results may differ from the reference program's by a relative error of at most 0.015.
Values may be sent and summed in bfloat16 or wider, within the bound.
A program may use at most 192 MiB of HBM per device.

```python
import math
import jax
import jax.numpy as jnp
import numpy as np
from jax import lax

D = 1024
H = 16
KV = 8
HD = 128
FF = 3072
SEQS = 4
STEP = 10
GROUP = 2048
LONGEST = 1920
TOKENS = 32768
GAIN_ALL = 2304
N_SHARD = 16


def levels(own_key, shape, split, smallest, high):
    level = 1.0
    for dim, shards_of in split:
        steps = jax.random.uniform(jax.random.fold_in(jax.random.fold_in(own_key, 6), dim), (shards_of,), jnp.float32, smallest / len(split), high / len(split))
        level = level * jnp.repeat(jnp.exp(steps), shape[dim] // shards_of).reshape((-1,) + (1,) * (len(shape) - 1 - dim))
    return level


def split_up(number_of, total, most, lean):
    loads = [(1 << 20) // math.isqrt(rank ** lean) + 1 for rank in range(2, number_of + 1)]
    rest, given = total - most - (number_of - 1), [1] * (number_of - 1)
    while rest > 0:
        movable = [i for i in range(number_of - 1) if given[i] < most]
        mass, left = sum([loads[i] for i in movable]), rest
        for i in movable:
            more = min(most - given[i], max(1, left * loads[i] // mass), rest)
            given[i] = given[i] + more
            rest = rest - more
    return np.array([most] + given)


def ragged(stream_key, amount, total, limit, slope):
    if amount == 2:
        one = jax.random.randint(stream_key, (), max(1, total - limit), min(limit, total - 1) + 1)
        return jnp.stack([one, total - one])
    tallies = jnp.asarray(split_up(amount, total, limit, slope), jnp.int32)
    twos = (amount - 1) // 2
    donor, receiver = tallies[1:1 + 2 * twos:2], tallies[2:2 + 2 * twos:2]
    room = jnp.minimum(donor - 1, limit - receiver)
    shifted = jax.random.randint(jax.random.fold_in(stream_key, 1), (twos,), 0, 1 << 20) % (room + 1)
    tallies = tallies.at[1:1 + 2 * twos:2].set(donor - shifted).at[2:2 + 2 * twos:2].set(receiver + shifted)
    return tallies[jax.random.permutation(jax.random.fold_in(stream_key, 2), amount)]


def normal_values(rng, extent, scale, limit, shards=(), held_as=jnp.bfloat16):
    values = jax.random.normal(rng, extent, jnp.float32) * scale
    if len(shards) > 0:
        values = levels(rng, extent, shards, -0.22, 0.18) * values
    return jnp.clip(values, min=-limit, max=limit).astype(held_as)


def setup_inputs(seed: int = 0) -> dict:
    streams_of = jax.random.split(jax.random.key(seed), 19)
    return {
        "tokens": normal_values(streams_of[0], (N_SHARD, GROUP, D), 1.0, 6.0, ((0, 16), (1, 8))),
        "cotangent": normal_values(streams_of[1], (N_SHARD, GROUP, D), 1.0, 6.0, ((0, 16), (1, 8))),
        "lengths": jax.vmap(lambda own: ragged(own, SEQS, GROUP, LONGEST, 0))(jax.random.split(streams_of[2], N_SHARD)).reshape((N_SHARD, SEQS)).astype(jnp.int32),
        "weight_input": normal_values(streams_of[3], (D, (H + 2 * KV) * HD), D ** -0.5, 0.1875, ((0, 128),), jnp.float32),
        "weight_output": normal_values(streams_of[4], (H * HD, D), (H * HD // 64) ** -0.5, 1.0, ((0, 128),), jnp.float32),
        "weight_expand": normal_values(streams_of[5], (D, 2 * FF), D ** -0.5, 0.1875, ((0, 128),), jnp.float32),
        "weight_reduce": normal_values(streams_of[6], (FF, D), FF ** -0.5, 0.109375, ((0, 128),), jnp.float32),
        "gains": jnp.clip(1.0 + 0.1 * jax.random.normal(streams_of[7], (GAIN_ALL,), jnp.float32), 0.5, 1.5),
        "first_input": normal_values(streams_of[8], (D, (H + 2 * KV) * HD), (0.111 * TOKENS ** 0.5), 128.0, ((0, 128),), jnp.float32),
        "first_output": normal_values(streams_of[9], (H * HD, D), (0.019 * TOKENS ** 0.5), 20.0, ((0, 128),), jnp.float32),
        "first_expand": normal_values(streams_of[10], (D, 2 * FF), (0.067 * TOKENS ** 0.5), 64.0, ((0, 128),), jnp.float32),
        "first_reduce": normal_values(streams_of[11], (FF, D), (0.067 * TOKENS ** 0.5), 64.0, ((0, 128),), jnp.float32),
        "first_gains": normal_values(streams_of[12], (GAIN_ALL,), (0.111 * TOKENS ** 0.5), 128.0, ((0, 128),), jnp.float32),
        "second_input": jnp.clip(jnp.exp(math.log(6881.28) - 1.3843914 * jax.random.uniform(streams_of[13], (D, (H + 2 * KV) * HD), jnp.float32) ** levels(streams_of[13], (D, (H + 2 * KV) * HD), ((0, 128),), -0.2, 0.2)), 1723.5968, 6881.28),
        "second_output": jnp.clip(jnp.exp(math.log(196.608) - 1.3862944 * jax.random.uniform(streams_of[14], (H * HD, D), jnp.float32) ** levels(streams_of[14], (H * HD, D), ((0, 128),), -0.2, 0.2)), 49.152, 196.608),
        "second_expand": jnp.clip(jnp.exp(math.log(2490.368) - 1.3862944 * jax.random.uniform(streams_of[15], (D, 2 * FF), jnp.float32) ** levels(streams_of[15], (D, 2 * FF), ((0, 128),), -0.2, 0.2)), 622.592, 2490.368),
        "second_reduce": jnp.clip(jnp.exp(math.log(2490.368) - 1.3862944 * jax.random.uniform(streams_of[16], (FF, D), jnp.float32) ** levels(streams_of[16], (FF, D), ((0, 128),), -0.2, 0.2)), 622.592, 2490.368),
        "second_gains": jnp.clip(jnp.exp(math.log(6881.28) - 1.3843914 * jax.random.uniform(streams_of[17], (GAIN_ALL,), jnp.float32) ** levels(streams_of[17], (GAIN_ALL,), ((0, 128),), -0.2, 0.2)), 1723.5968, 6881.28),
    }


HIGH = lax.Precision.HIGHEST
norm_eps = 1e-06
rope_base = 1000000.0
beta_one = 0.9
beta_two = 0.95
adam_eps = 1e-08
matrix_rate = 0.1
gain_rate = 0.5
matrix_decay = 0.1
masked_score = -1e+30

@jax.custom_vjp
def low(v):
    return lax.optimization_barrier(v.astype(jnp.bfloat16)).astype(jnp.float32)

@jax.custom_vjp
def low_back(v):
    return v

def low_keep(v):
    return (low(v), None)

def low_pass(kept, grad):
    return (grad,)

def back_keep(v):
    return (v, None)

def back_low(kept, grad):
    return (low(grad),)
low.defvjp(low_keep, low_pass)
low_back.defvjp(back_keep, back_low)

def rms_scale(values, gain):
    return values * lax.rsqrt(lax.optimization_barrier(jnp.mean(values * values, axis=-1, keepdims=True)) + norm_eps) * gain

def rope_tables(positions, width):
    half = width // 2
    freq = rope_base ** (-(2.0 * jnp.arange(half, dtype=jnp.float32)) / width)
    angle = positions.astype(jnp.float32)[:, None] * freq[None, :]
    return (jnp.cos(angle), jnp.sin(angle))

def rotate(values, cosine, sine):
    half = values.shape[-1] // 2
    first = values[..., :half]
    second = values[..., half:]
    cos_b = cosine[:, None, :]
    sin_b = sine[:, None, :]
    return jnp.concatenate([first * cos_b - second * sin_b, second * cos_b + first * sin_b], axis=-1)

def seq_layout(lengths, count):
    ends = jnp.cumsum(lengths)
    starts = ends - lengths
    index = jnp.arange(count, dtype=jnp.int32)
    segment = lax.optimization_barrier(jnp.sum((index[:, None] >= ends[None, :]).astype(jnp.int32), axis=1))
    onehot = (segment[:, None] == jnp.arange(lengths.shape[0], dtype=jnp.int32)[None, :]).astype(jnp.int32)
    position = index - lax.optimization_barrier(jnp.sum(onehot * starts[None, :], axis=1))
    return (segment, position)

def adam_step(weight, grad, first, second, rate, decay):
    first_new = beta_one * first + (1.0 - beta_one) * grad
    second_new = beta_two * second + (1.0 - beta_two) * grad * grad
    fix_one = 1.0 - beta_one ** STEP
    fix_two = 1.0 - beta_two ** STEP
    direction = first_new / fix_one / (jnp.sqrt(second_new / fix_two) + adam_eps)
    return (weight - rate * (direction + decay * weight), first_new, second_new)

def group_layer(xg, lengths_g, w_in, w_out, w_exp, w_red, gains):
    count = xg.shape[0]
    group = H // KV
    segment, position = seq_layout(lengths_g, count)
    gain_in = gains[:D]
    gain_mid = gains[D:2 * D]
    gain_query = gains[2 * D:2 * D + HD]
    gain_key = gains[2 * D + HD:]
    normed = low(rms_scale(xg, gain_in))
    qkv = low_back(jnp.dot(normed, w_in, precision=HIGH))
    query = qkv[:, :H * HD].reshape(count, H, HD)
    key = qkv[:, H * HD:(H + KV) * HD].reshape(count, KV, HD)
    value = low(qkv[:, (H + KV) * HD:].reshape(count, KV, HD))
    cosine, sine = rope_tables(position, HD)
    query = low(rotate(rms_scale(query, gain_query), cosine, sine))
    key = low(rotate(rms_scale(key, gain_key), cosine, sine))
    index = jnp.arange(count, dtype=jnp.int32)
    allowed = (segment[:, None] == segment[None, :]) & (index[None, :] <= index[:, None])
    query_heads = query.reshape(count, KV, group, HD).transpose(1, 2, 0, 3)
    key_heads = key.transpose(1, 0, 2)
    value_heads = value.transpose(1, 0, 2)

    @jax.checkpoint
    def one_head(items):
        q_head, k_head, v_head = items
        scores = low_back(jnp.einsum('gqd,kd->gqk', q_head, k_head, precision=HIGH) * HD ** (-0.5))
        scores = jnp.where(allowed[None], scores, masked_score)
        top = lax.optimization_barrier(jnp.max(scores, axis=-1, keepdims=True))
        expo = jnp.exp(scores - top)
        probs = low(expo / lax.optimization_barrier(jnp.sum(expo, axis=-1, keepdims=True)))
        return jnp.einsum('gqk,kd->gqd', probs, v_head, precision=HIGH)
    mixed = lax.map(one_head, (query_heads, key_heads, value_heads))
    mixed = mixed.transpose(2, 0, 1, 3).reshape(count, H * HD)
    mixed = low(low_back(mixed))
    attended = low_back(jnp.dot(mixed, w_out, precision=HIGH))
    hidden = xg + attended
    normed_mid = low(rms_scale(hidden, gain_mid))
    gate_up = low_back(jnp.dot(normed_mid, w_exp, precision=HIGH))
    act = low(jax.nn.silu(gate_up[:, :FF]) * gate_up[:, FF:])
    return hidden + jnp.dot(act, w_red, precision=HIGH)

def reference(tokens, cotangent, lengths, weight_input, weight_output, weight_expand, weight_reduce, gains, first_input, first_output, first_expand, first_reduce, first_gains, second_input, second_output, second_expand, second_reduce, second_gains):
    start_x = tokens.astype(jnp.float32)

    def forward(inputs, w_in, w_out, w_exp, w_red, gain_all):
        low_in, low_out, low_exp, low_red = (low(w_in), low(w_out), low(w_exp), low(w_red))
        checked = jax.checkpoint(group_layer)

        def step(carry, item):
            xg, lengths_g = item
            return (carry, checked(xg, lengths_g, low_in, low_out, low_exp, low_red, gain_all))
        return lax.scan(step, jnp.zeros((), jnp.float32), (inputs, lengths))[1]
    result, pullback = jax.vjp(forward, start_x, weight_input, weight_output, weight_expand, weight_reduce, gains)
    grads = pullback(cotangent.astype(jnp.float32))
    new_input, mean_input, square_input = adam_step(weight_input, grads[1], first_input, second_input, matrix_rate, matrix_decay)
    new_output, mean_output, square_output = adam_step(weight_output, grads[2], first_output, second_output, matrix_rate, matrix_decay)
    new_expand, mean_expand, square_expand = adam_step(weight_expand, grads[3], first_expand, second_expand, matrix_rate, matrix_decay)
    new_reduce, mean_reduce, square_reduce = adam_step(weight_reduce, grads[4], first_reduce, second_reduce, matrix_rate, matrix_decay)
    new_gains, mean_gains, square_gains = adam_step(gains, grads[5], first_gains, second_gains, gain_rate, 0.0)
    return (result.astype(jnp.bfloat16), grads[0], new_input, new_output, new_expand, new_reduce, new_gains, mean_input, mean_output, mean_expand, mean_reduce, mean_gains, square_input, square_output, square_expand, square_reduce, square_gains)
```

```python
import jax
import jax.numpy as jnp
from jax import lax
from jax.sharding import PartitionSpec as P

D = 1024
H = 16
KV = 8
HD = 128
FF = 3072
STEP = 10


norm_eps = 1e-06
rope_base = 1000000.0
beta_one = 0.9
beta_two = 0.95
adam_eps = 1e-08
matrix_rate = 0.1
gain_rate = 0.5
matrix_decay = 0.1
masked_score = -1e30


def rms_scale(values, gain):
    return values * lax.rsqrt(jnp.mean(values * values, axis=-1, keepdims=True) + norm_eps) * gain


def rope_tables(positions, width):
    half = width // 2
    freq = rope_base ** (-(2.0 * jnp.arange(half, dtype=jnp.float32)) / width)
    angle = positions.astype(jnp.float32)[:, None] * freq[None, :]
    return (jnp.cos(angle), jnp.sin(angle))


def rotate(values, cosine, sine):
    half = values.shape[-1] // 2
    first = values[..., :half]
    second = values[..., half:]
    cos_b = cosine[:, None, :]
    sin_b = sine[:, None, :]
    return jnp.concatenate(
        [first * cos_b - second * sin_b, second * cos_b + first * sin_b], axis=-1
    )


def seq_layout(lengths, count):
    ends = jnp.cumsum(lengths)
    starts = ends - lengths
    index = jnp.arange(count, dtype=jnp.int32)
    segment = jnp.sum((index[:, None] >= ends[None, :]).astype(jnp.int32), axis=1)
    onehot = (segment[:, None] == jnp.arange(lengths.shape[0], dtype=jnp.int32)[None, :]).astype(
        jnp.int32
    )
    position = index - jnp.sum(onehot * starts[None, :], axis=1)
    return (segment, position)


def adam_step(weight, grad, first, second, rate, decay):
    first_new = beta_one * first + (1.0 - beta_one) * grad
    second_new = beta_two * second + (1.0 - beta_two) * grad * grad
    fix_one = 1.0 - beta_one**STEP
    fix_two = 1.0 - beta_two**STEP
    direction = first_new / fix_one / (jnp.sqrt(second_new / fix_two) + adam_eps)
    return (weight - rate * (direction + decay * weight), first_new, second_new)


def qk_prepare(query, key, gain_query, gain_key, cosine, sine):
    return (
        rotate(rms_scale(query, gain_query), cosine, sine),
        rotate(rms_scale(key, gain_key), cosine, sine),
    )


def swiglu(gate_up):
    return jax.nn.silu(gate_up[:, :FF]) * gate_up[:, FF:]


def split_columns(rows, widths):
    parts = []
    start = 0
    ranks = lax.axis_size("dp")
    for width in widths:
        part = rows[:, start : start + width]
        parts.append(part.reshape(rows.shape[0], ranks, width // ranks))
        start += width
    return jnp.concatenate(parts, axis=2).transpose(1, 0, 2)


def join_columns(blocks, widths):
    ranks = blocks.shape[0]
    parts = []
    start = 0
    for width in widths:
        part = blocks[:, :, start : start + width // ranks]
        parts.append(part.transpose(1, 0, 2).reshape(blocks.shape[1], width))
        start += width // ranks
    return jnp.concatenate(parts, axis=1)


IN_WIDTHS = (H * HD, KV * HD, KV * HD)
EXPAND_WIDTHS = (FF, FF)


def gather_columns(weight, widths):
    blocks = split_columns(weight.astype(jnp.bfloat16), widths)
    mine = lax.all_to_all(blocks, "dp", 0, 0)
    whole = lax.all_gather(mine, "shard", axis=1, tiled=True)
    return whole.reshape(-1, whole.shape[-1])


def gather_rows(weight):
    return lax.all_gather(weight.astype(jnp.bfloat16), "shard", axis=0, tiled=True)


def scatter_columns(grad, widths):
    ranks = lax.axis_size("dp")
    low = grad.astype(jnp.bfloat16).reshape(ranks, grad.shape[0] // ranks, grad.shape[1])
    mine = lax.psum_scatter(low, "shard", scatter_dimension=1, tiled=True)
    return join_columns(lax.all_to_all(mine, "dp", 0, 0).astype(jnp.float32), widths)


def scatter_rows(grad):
    return lax.psum_scatter(
        grad.astype(jnp.bfloat16), "shard", scatter_dimension=0, tiled=True
    ).astype(jnp.float32)


def gather_tokens(block):
    return lax.all_gather(block, "dp", axis=0, tiled=True)


def scatter_tokens(partial):
    return lax.psum_scatter(
        partial.astype(jnp.bfloat16), "dp", scatter_dimension=0, tiled=True
    ).astype(jnp.float32)


def dot(a, b):
    return jnp.dot(a, b, preferred_element_type=jnp.float32)


def dot_t(a, b):
    return lax.dot_general(a, b, (((1,), (1,)), ((), ())), preferred_element_type=jnp.float32)


def t_dot(a, b):
    return lax.dot_general(a, b, (((0,), (0,)), ((), ())), preferred_element_type=jnp.float32)


def body(
    tokens,
    cotangent,
    lengths,
    weight_input,
    weight_output,
    weight_expand,
    weight_reduce,
    gains,
    first_input,
    first_output,
    first_expand,
    first_reduce,
    first_gains,
    second_input,
    second_output,
    second_expand,
    second_reduce,
    second_gains,
):
    ranks = lax.axis_size("dp")
    count = tokens.shape[1]
    whole = count * ranks
    group = H // KV
    scale = HD ** (-0.5)
    half = FF // ranks
    x_val = tokens[0].astype(jnp.float32)
    all_gains = lax.all_gather(
        lax.all_gather(gains, "shard", axis=0, tiled=True), "dp", axis=0, tiled=True
    )
    gain_in = all_gains[:D]
    gain_mid = all_gains[D : 2 * D]
    gain_query = all_gains[2 * D : 2 * D + HD]
    gain_key = all_gains[2 * D + HD :]
    w_in = gather_columns(weight_input, IN_WIDTHS)
    w_out = gather_rows(weight_output)
    w_exp = gather_columns(weight_expand, EXPAND_WIDTHS)
    w_red = gather_rows(weight_reduce)

    segment, position = seq_layout(lengths[0], whole)
    index = jnp.arange(whole, dtype=jnp.int32)
    allowed = (segment[:, None] == segment[None, :]) & (index[None, :] <= index[:, None])
    cosine, sine = rope_tables(position, HD)

    normed = gather_tokens(rms_scale(x_val, gain_in).astype(jnp.bfloat16))
    qkv = dot(normed, w_in)
    query_raw = qkv[:, : group * HD].reshape(whole, group, HD)
    key_raw = qkv[:, group * HD : (group + 1) * HD].reshape(whole, 1, HD)
    value = qkv[:, (group + 1) * HD :].astype(jnp.bfloat16)
    query_rot, key_rot = qk_prepare(query_raw, key_raw, gain_query, gain_key, cosine, sine)
    query = query_rot.astype(jnp.bfloat16)
    key = key_rot.astype(jnp.bfloat16)[:, 0]

    def head_forward(q_head):
        scores = jnp.where(allowed, dot_t(q_head, key) * scale, masked_score)
        top = jnp.max(scores, axis=-1, keepdims=True)
        expo = jnp.exp(scores - top)
        total = jnp.sum(expo, axis=-1, keepdims=True)
        probs = (expo / total).astype(jnp.bfloat16)
        return (dot(probs, value), (top + jnp.log(total))[:, 0])

    mixed, log_totals = lax.map(head_forward, query.transpose(1, 0, 2))
    mixed_low = mixed.transpose(1, 0, 2).reshape(whole, group * HD).astype(jnp.bfloat16)
    hidden = x_val + scatter_tokens(dot(mixed_low, w_out))
    normed_mid = gather_tokens(rms_scale(hidden, gain_mid).astype(jnp.bfloat16))
    gate_up = dot(normed_mid, w_exp)

    def act_of(gu):
        return jax.nn.silu(gu[:, :half]) * gu[:, half:]

    act, act_pull = jax.vjp(act_of, gate_up)
    act_low = act.astype(jnp.bfloat16)
    block_out = (hidden + scatter_tokens(dot(act_low, w_red))).astype(jnp.bfloat16)[None]

    grad_val = cotangent[0].astype(jnp.float32)
    grad_all = gather_tokens(cotangent[0])
    grad_reduce = scatter_rows(t_dot(act_low, grad_all))
    d_gate_up = act_pull(dot_t(grad_all, w_red))[0].astype(jnp.bfloat16)
    grad_expand = scatter_columns(t_dot(normed_mid, d_gate_up), EXPAND_WIDTHS)
    d_normed_mid = scatter_tokens(dot_t(d_gate_up, w_exp))
    unused, mid_pull = jax.vjp(rms_scale, hidden, gain_mid)
    d_hidden_part, d_gain_mid = mid_pull(d_normed_mid)
    d_hidden = grad_val + d_hidden_part
    d_att = gather_tokens(d_hidden.astype(jnp.bfloat16))
    grad_output = scatter_rows(t_dot(mixed_low, d_att))
    d_mixed = dot_t(d_att, w_out).astype(jnp.bfloat16)

    def head_backward(items):
        q_head, d_head, log_total = items
        scores = dot_t(q_head, key) * scale
        probs = jnp.exp(jnp.where(allowed, scores - log_total[:, None], masked_score))
        d_probs = dot_t(d_head, value)
        inner = jnp.sum(probs * d_probs, axis=-1, keepdims=True)
        d_scores = (probs * (d_probs - inner)).astype(jnp.bfloat16)
        return (
            dot(d_scores, key) * scale,
            t_dot(d_scores, q_head) * scale,
            t_dot(probs.astype(jnp.bfloat16), d_head),
        )

    d_query, d_key, d_value = lax.map(
        head_backward,
        (query.transpose(1, 0, 2), d_mixed.reshape(whole, group, HD).transpose(1, 0, 2), log_totals),
    )

    def qk_only(query, key, gain_q, gain_k):
        return qk_prepare(query, key, gain_q, gain_k, cosine, sine)

    unused, qk_pull = jax.vjp(qk_only, query_raw, key_raw, gain_query, gain_key)
    d_query_raw, d_key_raw, d_gain_query, d_gain_key = qk_pull(
        (d_query.transpose(1, 0, 2), jnp.sum(d_key, axis=0)[:, None])
    )
    d_qkv = jnp.concatenate(
        [d_query_raw.reshape(whole, -1), d_key_raw.reshape(whole, -1), jnp.sum(d_value, axis=0)],
        axis=1,
    ).astype(jnp.bfloat16)
    grad_input = scatter_columns(t_dot(normed, d_qkv), IN_WIDTHS)
    d_normed = scatter_tokens(dot_t(d_qkv, w_in))
    unused, in_pull = jax.vjp(rms_scale, x_val, gain_in)
    d_x_part, d_gain_in = in_pull(d_normed)
    input_grad = (d_hidden + d_x_part)[None]
    gain_terms = jnp.concatenate([d_gain_in, d_gain_mid, d_gain_query, d_gain_key])
    grad_gains = lax.psum_scatter(gain_terms, ("dp", "shard"), scatter_dimension=0, tiled=True)
    new_input, mean_input, square_input = adam_step(
        weight_input, grad_input, first_input, second_input, matrix_rate, matrix_decay
    )
    new_output, mean_output, square_output = adam_step(
        weight_output, grad_output, first_output, second_output, matrix_rate, matrix_decay
    )
    new_expand, mean_expand, square_expand = adam_step(
        weight_expand, grad_expand, first_expand, second_expand, matrix_rate, matrix_decay
    )
    new_reduce, mean_reduce, square_reduce = adam_step(
        weight_reduce, grad_reduce, first_reduce, second_reduce, matrix_rate, matrix_decay
    )
    new_gains, mean_gains, square_gains = adam_step(
        gains, grad_gains, first_gains, second_gains, gain_rate, 0.0
    )
    return (
        block_out,
        input_grad,
        new_input,
        new_output,
        new_expand,
        new_reduce,
        new_gains,
        mean_input,
        mean_output,
        mean_expand,
        mean_reduce,
        mean_gains,
        square_input,
        square_output,
        square_expand,
        square_reduce,
        square_gains,
    )


def solution(mesh):
    placed = (
        P("shard", "dp", None),
        P("shard", "dp", None),
        P("shard", None),
        P(("dp", "shard"), None),
        P(("dp", "shard"), None),
        P(("dp", "shard"), None),
        P(("dp", "shard"), None),
        P(("dp", "shard")),
        P(("dp", "shard"), None),
        P(("dp", "shard"), None),
        P(("dp", "shard"), None),
        P(("dp", "shard"), None),
        P(("dp", "shard")),
        P(("dp", "shard"), None),
        P(("dp", "shard"), None),
        P(("dp", "shard"), None),
        P(("dp", "shard"), None),
        P(("dp", "shard")),
    )
    return jax.shard_map(
        body,
        mesh=mesh,
        in_specs=placed,
        out_specs=(
            P("shard", "dp", None),
            P("shard", "dp", None),
            P(("dp", "shard"), None),
            P(("dp", "shard"), None),
            P(("dp", "shard"), None),
            P(("dp", "shard"), None),
            P(("dp", "shard")),
            P(("dp", "shard"), None),
            P(("dp", "shard"), None),
            P(("dp", "shard"), None),
            P(("dp", "shard"), None),
            P(("dp", "shard")),
            P(("dp", "shard"), None),
            P(("dp", "shard"), None),
            P(("dp", "shard"), None),
            P(("dp", "shard"), None),
            P(("dp", "shard")),
        ),
        check_vma=False,
    )
```

```python
import math

import jax
import jax.numpy as jnp
from jax import lax
from jax.experimental import pallas as pl
from jax.experimental.pallas import tpu as pltpu
from jax.sharding import PartitionSpec as P

D = 1024
H = 16
KV = 8
HD = 128
FF = 3072
STEP = 10


norm_eps = 1e-06
rope_base = 1000000.0
beta_one = 0.9
beta_two = 0.95
adam_eps = 1e-08
matrix_rate = 0.1
gain_rate = 0.5
matrix_decay = 0.1
masked_score = -1e30


def rms_scale(values, gain):
    return values * lax.rsqrt(jnp.mean(values * values, axis=-1, keepdims=True) + norm_eps) * gain


def rope_tables(positions, width):
    half = width // 2
    freq = rope_base ** (-(2.0 * jnp.arange(half, dtype=jnp.float32)) / width)
    angle = positions.astype(jnp.float32)[:, None] * freq[None, :]
    return (jnp.cos(angle), jnp.sin(angle))


def rotate(values, cosine, sine):
    half = values.shape[-1] // 2
    first = values[..., :half]
    second = values[..., half:]
    cos_b = cosine[:, None, :]
    sin_b = sine[:, None, :]
    return jnp.concatenate(
        [first * cos_b - second * sin_b, second * cos_b + first * sin_b], axis=-1
    )


def seq_layout(lengths, count):
    ends = jnp.cumsum(lengths)
    starts = ends - lengths
    index = jnp.arange(count, dtype=jnp.int32)
    segment = jnp.sum((index[:, None] >= ends[None, :]).astype(jnp.int32), axis=1)
    onehot = (segment[:, None] == jnp.arange(lengths.shape[0], dtype=jnp.int32)[None, :]).astype(
        jnp.int32
    )
    position = index - jnp.sum(onehot * starts[None, :], axis=1)
    return (segment, position)


def adam_step(weight, grad, first, second, rate, decay):
    first_new = beta_one * first + (1.0 - beta_one) * grad
    second_new = beta_two * second + (1.0 - beta_two) * grad * grad
    fix_one = 1.0 - beta_one**STEP
    fix_two = 1.0 - beta_two**STEP
    direction = first_new / fix_one / (jnp.sqrt(second_new / fix_two) + adam_eps)
    return (weight - rate * (direction + decay * weight), first_new, second_new)


MESH = pl.DeviceIdType.MESH
F32 = jnp.float32
BF = jnp.bfloat16
VMEM = pl.BlockSpec(memory_space=pltpu.VMEM)
IN_COLS = (H + 2 * KV) * HD // 8
EXP_COLS = 2 * FF // 8
RED_ROWS = 32


def dot(a, b):
    return jnp.dot(a, b, preferred_element_type=F32)


def dot_t(a, b):
    return lax.dot_general(a, b, (((1,), (1,)), ((), ())), preferred_element_type=F32)


def t_dot(a, b):
    return lax.dot_general(a, b, (((0,), (0,)), ((), ())), preferred_element_type=F32)


def place():
    dp = lax.axis_index("dp")
    shard = lax.axis_index("shard")
    return dp // 2, lax.rem(dp, 2), shard // 4, lax.rem(shard, 4)


def device(z, core, x, y):
    return (lax.rem(z, 4) * 2 + core, lax.rem(x, 4) * 4 + lax.rem(y, 4))


def line_peers():
    z, core, x, y = place()
    return [device(z, 1 - core, x, y), device(z + 1, core, x, y), device(z + 3, core, x, y)]


def plane_peers():
    z, core, x, y = place()
    return [device(z, core, x + k, y) for k in (1, 2, 3)] + [
        device(z, core, x, y + k) for k in (1, 2, 3)
    ]


def dp_peers():
    dp = lax.axis_index("dp")
    shard = lax.axis_index("shard")
    return [(lax.rem(dp + k, 8), shard) for k in range(1, 8)]


def meet(peers):
    barrier = pltpu.get_barrier_semaphore()
    for peer in peers:
        pl.semaphore_signal(barrier, inc=1, device_id=peer, device_id_type=MESH)
    pl.semaphore_wait(barrier, len(peers))


def remote(src, dst, send, recv, peer):
    return pltpu.make_async_remote_copy(
        src_ref=src, dst_ref=dst, send_sem=send, recv_sem=recv, device_id=peer, device_id_type=MESH
    )


class LineGather:
    sems = 13

    def __init__(self, buf, send, recv):
        z, core, x, y = place()
        me, right, far, left = (lax.rem(z + k, 4) * 2 + core for k in range(4))
        to_right, to_left = device(z + 1, core, x, y), device(z + 3, core, x, y)
        sibling = device(z, 1 - core, x, y)
        plan = [
            (me, 0, to_right),
            (me, 1, to_right),
            (left, 0, to_right),
            (me, 1, to_left),
            (me, 0, to_left),
            (right, 1, to_left),
            (me, None, sibling),
            (left, 0, sibling),
            (right, 1, sibling),
            (left, 1, sibling),
            (right, 0, sibling),
            (far, 0, sibling),
            (far, 1, sibling),
        ]
        self.copies = []
        for k, (slot, half, peer) in enumerate(plan):
            ref = buf.at[slot] if half is None else buf.at[slot, half]
            self.copies.append(remote(ref, ref, send.at[k], recv.at[k], peer))

    def start(self, *which):
        for k in which:
            self.copies[k].start()

    def wait(self, *which):
        for k in which:
            self.copies[k].wait_recv()

    def begin(self):
        self.start(6, 0, 3, 1, 4)

    def pass_on(self):
        self.wait(0)
        self.start(2, 7)
        self.wait(3)
        self.start(5, 8)

    def second(self):
        self.wait(1)
        self.start(9)
        self.wait(4)
        self.start(10)

    def third(self):
        self.wait(2)
        self.start(11)
        self.wait(5)
        self.start(12)

    def sent(self):
        for copy in self.copies:
            copy.wait_send()


class PlaneGather:
    sems = 12

    def __init__(self, buf, send, recv):
        z, core, x, y = place()
        half = buf.shape[3] // 2
        low, high = pl.ds(0, half), pl.ds(half, half)
        self.copies = []
        refs = (
            (buf.at[x, y, :, low], 0),
            (buf.at[x, y, :, high], 1),
            (buf.at[:, y, :, low], 1),
            (buf.at[x, :, :, high], 0),
        )
        k = 0
        for ref, along_y in refs:
            for step in (1, 2, 3):
                peer = device(z, core, x, y + step) if along_y else device(z, core, x + step, y)
                self.copies.append(remote(ref, ref, send.at[k], recv.at[k], peer))
                k += 1

    def begin(self):
        for k in (0, 3, 1, 4, 2, 5):
            self.copies[k].start()

    def pass_on(self):
        for k in (0, 1, 2):
            self.copies[k].wait_recv()
        for k in (6, 7, 8):
            self.copies[k].start()
        for k in (3, 4, 5):
            self.copies[k].wait_recv()
        for k in (9, 10, 11):
            self.copies[k].start()

    def end(self):
        for k in range(6, 12):
            self.copies[k].wait_recv()

    def sent(self):
        for copy in self.copies:
            copy.wait_send()


class PlaneScatter:
    sems = 12

    def __init__(self, parts, got1, mid, got2, send, recv):
        z, core, x, y = place()
        self.parts, self.got1, self.mid, self.got2 = parts, got1, mid, got2
        half = parts.shape[3] // 2
        self.cols = (pl.ds(0, half), pl.ds(half, half))
        self.x, self.y = x, y
        self.copies = []
        k = 0
        for side in (0, 1):
            for step in (1, 2, 3):
                if side == 0:
                    ref = parts.at[:, lax.rem(y + step, 4), :, self.cols[0]]
                    peer = device(z, core, x, y + step)
                else:
                    ref = parts.at[lax.rem(x + step, 4), :, :, self.cols[1]]
                    peer = device(z, core, x + step, y)
                self.copies.append(remote(ref, got1.at[side, step - 1], send.at[k], recv.at[k], peer))
                k += 1
        for side in (0, 1):
            for step in (1, 2, 3):
                if side == 0:
                    ref = mid.at[0, lax.rem(x + step, 4)]
                    peer = device(z, core, x + step, y)
                else:
                    ref = mid.at[1, lax.rem(y + step, 4)]
                    peer = device(z, core, x, y + step)
                self.copies.append(remote(ref, got2.at[side, step - 1], send.at[k], recv.at[k], peer))
                k += 1

    def begin(self):
        for k in (0, 3, 1, 4, 2, 5):
            self.copies[k].start()

    def pass_on(self):
        for side in (0, 1):
            for k in range(3 * side, 3 * side + 3):
                self.copies[k].wait_recv()
            for j in range(4):
                if side == 0:
                    own = self.parts[j, self.y, :, self.cols[0]]
                else:
                    own = self.parts[self.x, j, :, self.cols[1]]
                total = own.astype(F32)
                for k in range(3):
                    total += self.got1[side, k, j].astype(F32)
                self.mid[side, j] = total.astype(BF)
            for k in range(6 + 3 * side, 9 + 3 * side):
                self.copies[k].start()

    def end(self, out):
        for side in (0, 1):
            for k in range(6 + 3 * side, 9 + 3 * side):
                self.copies[k].wait_recv()
            total = self.mid[side, self.x if side == 0 else self.y].astype(F32)
            for k in range(3):
                total += self.got2[side, k].astype(F32)
            out[:, self.cols[side]] = total

    def sent(self):
        for copy in self.copies:
            copy.wait_send()


def plane_scatter_scratch(rows, width):
    half = width // 2
    return [
        pltpu.VMEM((2, 3, 4, rows, half), BF),
        pltpu.VMEM((2, 4, rows, half), BF),
        pltpu.VMEM((2, 3, rows, half), BF),
        pltpu.SemaphoreType.DMA((12,)),
        pltpu.SemaphoreType.DMA((12,)),
    ]


class LineScatter:
    sems = 10

    def __init__(self, keep, give, took, out_z, in_z, send, recv):
        z, core, x, y = place()
        self.keep, self.took, self.out_z, self.in_z = keep, took, out_z, in_z
        to_right, to_left = device(z + 1, core, x, y), device(z + 3, core, x, y)
        sibling = device(z, 1 - core, x, y)
        self.swap = [remote(give.at[k], took.at[k], send.at[k], recv.at[k], sibling) for k in range(4)]
        self.copies = [
            remote(
                out_z.at[k], in_z.at[k], send.at[4 + k], recv.at[4 + k], to_right if k < 3 else to_left
            )
            for k in range(6)
        ]

    def give(self, offset):
        self.swap[offset].start()

    def take(self, offset):
        self.swap[offset].wait_recv()

    def half(self, offset, part):
        return self.keep[offset, part] + self.took[offset, part].astype(F32)

    def push(self, k, value):
        self.out_z[k] = value.astype(BF)
        self.copies[k].start()

    def far(self):
        self.take(2)
        self.push(0, self.half(2, 0))
        self.push(3, self.half(2, 1))

    def near(self):
        self.take(1)
        self.push(1, self.half(1, 1))
        self.take(3)
        self.push(4, self.half(3, 0))

    def last(self):
        self.copies[0].wait_recv()
        self.push(2, self.half(1, 0) + self.in_z[0].astype(F32))
        self.copies[3].wait_recv()
        self.push(5, self.half(3, 1) + self.in_z[3].astype(F32))

    def result(self):
        self.take(0)
        self.copies[1].wait_recv()
        self.copies[4].wait_recv()
        self.copies[2].wait_recv()
        first = self.half(0, 0) + self.in_z[4].astype(F32) + self.in_z[2].astype(F32)
        self.copies[5].wait_recv()
        second = self.half(0, 1) + self.in_z[1].astype(F32) + self.in_z[5].astype(F32)
        return first, second

    def sent(self):
        for copy in self.swap + self.copies:
            copy.wait_send()


def line_scatter_scratch(rows, width):
    return [
        pltpu.VMEM((4, 2, rows, width), F32),
        pltpu.VMEM((4, 2, rows, width), BF),
        pltpu.VMEM((4, 2, rows, width), BF),
        pltpu.VMEM((6, rows, width), BF),
        pltpu.VMEM((6, rows, width), BF),
        pltpu.SemaphoreType.DMA((10,)),
        pltpu.SemaphoreType.DMA((10,)),
    ]


def to_send(w_in, w_exp, gains, out):
    col = 0
    for ref, start, width in (
        (w_in, 0, 256),
        (w_in, H * HD, 128),
        (w_in, (H + KV) * HD, 128),
        (w_exp, 0, 384),
        (w_exp, FF, 384),
    ):
        for j in range(8):
            out[j, :, col : col + width] = ref[:, start + j * width : start + (j + 1) * width]
        col += width
    for j in range(8):
        out[j, :, col : col + 128] = gains[...]


def spread_gains(gbuf):
    wide = 128 * 18
    held = gbuf[:, :, :, 0:128].reshape(128, 128)
    n = lax.broadcasted_iota(jnp.int32, (128, wide), 1)
    r = lax.broadcasted_iota(jnp.int32, (128, wide), 0)
    nf = n.astype(F32)
    within = nf - 18.0 * jnp.floor((nf + 0.5) * (1.0 / 18.0))
    pick = jnp.where(within == r.astype(F32), 1.0, 0.0)
    spread = jnp.dot(held, pick, precision=lax.Precision.HIGHEST, preferred_element_type=F32)
    first = ((r & 7) * 16 + (r >> 3)) * 18
    return jnp.sum(jnp.where((n >= first) & (n < first + 18), spread, 0.0), axis=0, keepdims=True)


def fill_order(perm):
    def block(i, carry):
        n = lax.broadcasted_iota(jnp.int32, (128, D), 0)
        k = lax.broadcasted_iota(jnp.int32, (128, D), 1)
        goal = (n >> 3) * 64 + i * 8 + (n & 7)
        perm[pl.ds(pl.multiple_of(i * 128, 128), 128), :] = jnp.where(k == goal, 1.0, 0.0).astype(BF)
        return carry

    lax.fori_loop(0, 8, block, 0)


def normed_rows(values):
    return lax.rsqrt(jnp.mean(values * values, axis=-1, keepdims=True) + norm_eps)


def front_kernel(
    x_ref, w_in_ref, w_exp_ref, gains_ref, cos_ref, sin_ref, w_out_ref, w_red_ref,
    a_ref, raw_ref, q_ref, k_ref, v_ref, win_ref, wexp_ref, gain_ref, wout_all, wred_all,
    xall, wsend, wgot, gbuf, perm,
    line_send, line_recv, cols_send, cols_recv, win_send, win_recv, g_send, g_recv,
    o_send, o_recv, r_send, r_recv,
):
    z, core, x, y = place()
    dp = lax.axis_index("dp")
    peers = dp_peers()
    xall[dp] = x_ref[...].reshape(2, 128, D)
    to_send(w_in_ref, w_exp_ref, gains_ref, wsend)
    wout_all[x, y] = w_out_ref[...].astype(BF)
    wred_all[x, y] = jnp.concatenate([w_red_ref[...], jnp.zeros((8, D), F32)], axis=0).astype(BF)
    meet(peers + plane_peers())
    cols = [
        remote(
            wsend.at[lax.rem(dp + k, 8)], wgot.at[dp], cols_send.at[k - 1], cols_recv.at[k - 1], peers[k - 1]
        )
        for k in range(1, 8)
    ]
    for copy in cols:
        copy.start()
    line = LineGather(xall, line_send, line_recv)
    line.begin()
    wgot[dp] = wsend[dp]
    fill_order(perm)
    for copy in cols:
        copy.wait_recv()
    mine = wgot[:, :, 0 : IN_COLS + EXP_COLS].reshape(64, IN_COLS + EXP_COLS).astype(BF)
    win_ref[x, y] = mine[:, 0:IN_COLS]
    wexp_ref[...] = mine[:, IN_COLS:]
    own_gains = wgot[:, 0, IN_COLS + EXP_COLS :]
    gbuf[x, y, :, 0:128] = own_gains
    gbuf[x, y, :, 128:256] = own_gains
    plane_g = PlaneGather(gbuf, g_send, g_recv)
    plane_w = PlaneGather(win_ref, win_send, win_recv)
    plane_g.begin()
    plane_w.begin()
    plane_o = PlaneGather(wout_all, o_send, o_recv)
    plane_r = PlaneGather(wred_all, r_send, r_recv)
    plane_o.begin()
    plane_r.begin()
    plane_g.pass_on()
    line.pass_on()
    plane_w.pass_on()
    plane_g.end()
    gain_ref[...] = jnp.broadcast_to(spread_gains(gbuf), gain_ref.shape)
    plane_w.end()

    def rows_of(block, carry):
        rows = pl.ds(pl.multiple_of(block * 256, 256), 256)
        values = xall[block].reshape(256, D).astype(F32)
        a = (values * normed_rows(values) * gain_ref[0:1, 0:D]).astype(BF)
        a = dot(a, perm[...]).astype(BF)
        a_ref[rows, :] = a
        qkv = dot(a, win_ref[...].reshape(D, IN_COLS))
        raw_ref[rows, :] = qkv[:, 0:384]
        for part in range(3):
            u = qkv[:, part * HD : (part + 1) * HD]
            start = 2 * D + (HD if part == 2 else 0)
            u = u * normed_rows(u) * gain_ref[0:1, start : start + HD]
            u = (u * cos_ref[rows, :] + pltpu.roll(u, HD // 2, 1) * sin_ref[rows, :]).astype(BF)
            if part < 2:
                q_ref[rows, part * HD : (part + 1) * HD] = u
            else:
                k_ref[rows, :] = u
        v_ref[rows, :] = qkv[:, 384:512].astype(BF)
        return carry

    def chip(offset):
        first = lax.rem(z + offset, 4) * 2
        lax.fori_loop(first, first + 2, rows_of, 0)

    line.wait(6)
    chip(0)
    line.second()
    plane_o.pass_on()
    plane_r.pass_on()
    line.wait(7, 8, 9, 10)

    def near(t, carry):
        first = lax.rem(z + 1 + 2 * (t // 2), 4) * 2
        return rows_of(first + lax.rem(t, 2), carry)

    lax.fori_loop(0, 4, near, 0)
    line.third()
    line.wait(11, 12)
    chip(2)
    line.sent()
    plane_o.end()
    plane_r.end()
    plane_o.sent()
    plane_r.sent()
    plane_g.sent()
    plane_w.sent()
    for copy in cols:
        copy.wait_send()


def front(x, w_in, w_exp, gains, cos, sin, w_out, w_red):
    sh = jax.ShapeDtypeStruct
    return pl.pallas_call(
        front_kernel,
        out_shape=(
            sh((2048, D), BF),
            sh((2048, 384), F32),
            sh((2048, 256), BF),
            sh((2048, 128), BF),
            sh((2048, 128), BF),
            sh((4, 4, 64, IN_COLS), BF),
            sh((64, EXP_COLS), BF),
            sh((8, 2304), F32),
            sh((4, 4, 16, D), BF),
            sh((4, 4, RED_ROWS, D), BF),
        ),
        in_specs=[VMEM] * 8,
        out_specs=[VMEM] * 10,
        scratch_shapes=[
            pltpu.VMEM((8, 2, 128, D), BF),
            pltpu.VMEM((8, 8, IN_COLS + EXP_COLS + 128), F32),
            pltpu.VMEM((8, 8, IN_COLS + EXP_COLS + 128), F32),
            pltpu.VMEM((4, 4, 8, 256), F32),
            pltpu.VMEM((D, D), BF),
        ]
        + [pltpu.SemaphoreType.DMA((n,)) for n in (13, 13, 7, 7, 12, 12, 12, 12, 12, 12, 12, 12)],
        compiler_params=pltpu.CompilerParams(
            collective_id=1, has_side_effects=True, vmem_limit_bytes=56 * 2**20
        ),
        name="front",
    )(x, w_in, w_exp, gains, cos, sin, w_out, w_red)


def rope_full(lengths, whole):
    segment, position = seq_layout(lengths, whole)
    cosine, sine = rope_tables(position, HD)
    return (
        segment,
        jnp.concatenate([cosine, cosine], axis=1),
        jnp.concatenate([-sine, sine], axis=1),
    )


def padded_gains(gains):
    return jnp.broadcast_to(jnp.pad(gains, (0, 128 - gains.shape[0]))[None], (8, 128))


SCORE = HD**-0.5 * math.log2(math.e)
BLOCK = 256
BIG = 30000.0


def extra_columns(segment):
    lane = jnp.arange(128)[None, :]
    same = segment[:, None] == lane
    q_extra = jnp.where((lane < 4) & ~same, -BIG, 0.0).astype(BF)
    k_extra = jnp.where(lane < 4, same.astype(F32), jnp.where(lane < 7, 1.0, 0.0)).astype(BF)
    v_extra = jnp.broadcast_to((lane < 3).astype(BF), (segment.shape[0], 128))
    return q_extra, k_extra, v_extra


def block_rows(i):
    return pl.ds(pl.multiple_of(i * BLOCK, BLOCK), BLOCK)


def wide_rows(i):
    return pl.ds(pl.multiple_of(i * 2 * BLOCK, 2 * BLOCK), 2 * BLOCK)


def attend_block(i, q_ref, k_ref, v_ref, qx_ref, kx_ref, vx_ref, o_ref, lse_ref, acc, qs):
    rows = block_rows(i)
    for h in range(2):
        qs[h * BLOCK : (h + 1) * BLOCK, 0:HD] = q_ref[rows, h * HD : (h + 1) * HD]
        qs[h * BLOCK : (h + 1) * BLOCK, HD:] = qx_ref[rows, :]

    def keys(kr):
        return (
            jnp.concatenate([k_ref[kr, :], kx_ref[kr, :]], axis=1),
            jnp.concatenate([v_ref[kr, :], vx_ref[kr, :]], axis=1),
        )

    kk, vv = keys(rows)
    query = lax.broadcasted_iota(jnp.int32, (2 * BLOCK, BLOCK), 0) & (BLOCK - 1)
    index = lax.broadcasted_iota(jnp.int32, (2 * BLOCK, BLOCK), 1)
    e = jnp.where(index <= query, jnp.exp2(dot_t(qs[...], kk) * SCORE), 0.0)
    acc[...] = dot(e.astype(BF), vv)

    def step(kr):
        kk, vv = keys(kr)
        acc[...] += dot(jnp.exp2(dot_t(qs[...], kk) * SCORE).astype(BF), vv)

    def wide(j, carry):
        step(wide_rows(j))
        return carry

    def narrow(j, carry):
        step(block_rows(j))
        return carry

    lax.fori_loop(0, i // 2, wide, 0)
    lax.fori_loop(i // 2 * 2, i, narrow, 0)
    total = acc[:, HD : HD + 1]
    out = acc[:, 0:HD] * (1.0 / total)
    lse = jnp.log2(total) * (1.0 / SCORE)
    for h in range(2):
        part = slice(h * BLOCK, (h + 1) * BLOCK)
        o_ref[rows, h * HD : (h + 1) * HD] = out[part].astype(BF)
        lse_ref[rows, h : h + 1] = lse[part]


def attention_kernel(
    q_ref, k_ref, v_ref, qx_ref, kx_ref, vx_ref, wexp_ref, dy_ref,
    o_ref, lse_ref, wexp_all, dy_all,
    acc, qs, line_send, line_recv, w_send, w_recv,
):
    z, core, x, y = place()
    wexp_all[x, y] = wexp_ref[...]
    dy_all[lax.axis_index("dp")] = dy_ref[...].reshape(2, 128, D)
    meet(line_peers() + plane_peers())
    plane = PlaneGather(wexp_all, w_send, w_recv)
    line = LineGather(dy_all, line_send, line_recv)
    plane.begin()
    line.begin()

    def block(t, carry):
        attend_block(7 - t, q_ref, k_ref, v_ref, qx_ref, kx_ref, vx_ref, o_ref, lse_ref, acc, qs)

        @pl.when(t == 0)
        def _():
            plane.pass_on()

        @pl.when(t == 1)
        def _():
            line.pass_on()

        @pl.when(t == 3)
        def _():
            line.second()

        return carry

    lax.fori_loop(0, 8, block, 0)
    line.third()
    plane.end()
    line.wait(6, 7, 8, 9, 10, 11, 12)
    plane.sent()
    line.sent()


def attention(q, k, v, qx, kx, vx, wexp, dy):
    sh = jax.ShapeDtypeStruct
    return pl.pallas_call(
        attention_kernel,
        out_shape=(sh((2048, 256), BF), sh((2048, 128), F32), sh((4, 4, 64, EXP_COLS), BF), sh((8, 2, 128, D), BF)),
        in_specs=[VMEM] * 8,
        out_specs=[VMEM] * 4,
        scratch_shapes=[pltpu.VMEM((2 * BLOCK, 256), F32), pltpu.VMEM((2 * BLOCK, 256), BF)]
        + [pltpu.SemaphoreType.DMA((n,)) for n in (13, 13, 12, 12)],
        compiler_params=pltpu.CompilerParams(
            collective_id=2, has_side_effects=True, vmem_limit_bytes=56 * 2**20
        ),
        name="attention",
    )(q, k, v, qx, kx, vx, wexp, dy)


def rms_back(h, r, gain, d):
    dg = d * gain
    return r * dg - h * (r * r * r) * jnp.mean(h * dg, axis=-1, keepdims=True)


def unorder(values, perm):
    high = values.astype(BF)
    low = (values - high.astype(F32)).astype(BF)
    return dot_t(high, perm) + dot_t(low, perm)


def mid_kernel(
    x_ref, o_ref, wout_ref, wexp_ref, wred_ref, dy_ref, gain_ref,
    hid_ref, dhid_ref, act_ref, do_ref, gred_ref, gexp_ref, gout_ref, dgain_ref, wred_out,
    perm, ball, datt, dgu, dbk,
    keep, give, took, out_z, in_z,
    s1_send, s1_recv, b_send, b_recv, s2_send, s2_recv, d_send, d_recv,
):
    z, core, x, y = place()
    dp = lax.axis_index("dp")
    meet(line_peers())
    wout = wout_ref[...].reshape(256, D)
    scatter = LineScatter(keep, give, took, out_z, in_z, s1_send, s1_recv)

    def block_of(offset, own):
        return lax.rem(z + offset, 4) * 2 + (core if own else 1 - core)

    for offset in (2, 1, 3, 0):
        give[offset] = dot(o_ref[block_rows(block_of(offset, False)), :], wout).astype(BF).reshape(2, 128, D)
        scatter.give(offset)
        keep[offset] = dot(o_ref[block_rows(block_of(offset, True)), :], wout).reshape(2, 128, D)
    scatter.far()
    scatter.near()
    fill_order(perm)
    wred_out[...] = (
        wred_ref[...].astype(F32)[:, :, 0:24, :].reshape(FF // 8, D).astype(BF)
    )
    scatter.last()
    first, second = scatter.result()
    hid_ref[...] = x_ref[...].astype(F32) + jnp.concatenate([first, second], axis=0)
    gain = gain_ref[0:1, D : 2 * D]
    hid = hid_ref[...]
    b = (hid * normed_rows(hid) * gain).astype(BF)
    ball[dp] = dot(b, perm[...]).astype(BF).reshape(2, 128, D)
    line = LineGather(ball, b_send, b_recv)
    line.begin()
    scatter.sent()
    scatter = LineScatter(keep, give, took, out_z, in_z, s2_send, s2_recv)

    def mlp(block):
        rows = block_rows(block)
        wexp = wexp_ref[...].reshape(D, EXP_COLS)
        gu = dot(ball[block].reshape(256, D), wexp)
        gate, up = gu[:, : FF // 8], gu[:, FF // 8 :]
        sig = 1.0 / (1.0 + jnp.exp(-gate))
        silu = gate * sig
        act_ref[rows, :] = (silu * up).astype(BF)
        d_act = dot_t(dy_ref[block].reshape(256, D), wred_out[...])
        d_gate = d_act * up * (sig * (1.0 + gate * (1.0 - sig)))
        dgu[rows, 0 : FF // 8] = d_gate.astype(BF)
        dgu[rows, FF // 8 :] = (d_act * silu).astype(BF)
        return dot_t(dgu[rows, :], wexp).reshape(2, 128, D)

    def chip(offset):
        give[offset] = mlp(block_of(offset, False)).astype(BF)
        scatter.give(offset)
        keep[offset] = mlp(block_of(offset, True))

    line.wait(6)
    chip(0)
    line.pass_on()
    line.second()
    line.wait(7, 8, 9, 10)
    chip(1)
    chip(3)
    scatter.near()
    line.third()
    line.wait(11, 12)
    chip(2)
    scatter.far()
    gred_ref[...] = jnp.concatenate(
        [
            t_dot(act_ref[...], dy_ref[...].reshape(2048, D)).reshape(4, 4, 24, D),
            jnp.zeros((4, 4, 8, D), F32),
        ],
        axis=2,
    ).astype(BF)
    gexp_ref[...] = t_dot(ball[...].reshape(2048, D), dgu[...]).astype(BF).reshape(4, 4, 64, EXP_COLS)
    scatter.last()
    first, second = scatter.result()
    d_b = unorder(jnp.concatenate([first, second], axis=0), perm[...])
    hid = hid_ref[...]
    r = normed_rows(hid)
    dgain_ref[...] = jnp.broadcast_to(jnp.sum(d_b * hid * r, axis=0, keepdims=True), (8, D))
    d_hid = dy_ref[dp].reshape(256, D).astype(F32) + rms_back(hid, r, gain, d_b)
    dhid_ref[...] = d_hid
    datt[dp] = d_hid.astype(BF).reshape(2, 128, D)
    line.sent()
    line = LineGather(datt, d_send, d_recv)
    line.begin()
    scatter.sent()

    def back(block):
        do_ref[block_rows(block), :] = dot_t(datt[block].reshape(256, D), wout).astype(BF)

    def back_chip(offset):
        back(block_of(offset, False))
        back(block_of(offset, True))

    line.wait(6)
    back_chip(0)
    line.pass_on()
    line.second()
    line.wait(7, 8, 9, 10)
    back_chip(1)
    back_chip(3)
    line.third()
    line.wait(11, 12)
    back_chip(2)
    gout_ref[...] = t_dot(o_ref[...], datt[...].reshape(2048, D)).astype(BF).reshape(4, 4, 16, D)
    line.sent()


def mid(x, o, wout, wexp, wred, dy, gain):
    sh = jax.ShapeDtypeStruct
    return pl.pallas_call(
        mid_kernel,
        out_shape=(
            sh((256, D), F32),
            sh((256, D), F32),
            sh((2048, FF // 8), BF),
            sh((2048, 256), BF),
            sh((4, 4, RED_ROWS, D), BF),
            sh((4, 4, 64, EXP_COLS), BF),
            sh((4, 4, 16, D), BF),
            sh((8, D), F32),
            sh((FF // 8, D), BF),
        ),
        in_specs=[VMEM] * 7,
        out_specs=[VMEM] * 9,
        scratch_shapes=[
            pltpu.VMEM((D, D), BF),
            pltpu.VMEM((8, 2, 128, D), BF),
            pltpu.VMEM((8, 2, 128, D), BF),
            pltpu.VMEM((2048, EXP_COLS), BF),
            pltpu.VMEM((8, 128), F32),
        ]
        + line_scatter_scratch(128, D)[:5]
        + [pltpu.SemaphoreType.DMA((n,)) for n in (10, 10, 13, 13, 10, 10, 13, 13)],
        compiler_params=pltpu.CompilerParams(
            collective_id=3, has_side_effects=True, vmem_limit_bytes=60 * 2**20
        ),
        name="middle",
    )(x, o, wout, wexp, wred, dy, gain)


def in_three(values):
    high = values.astype(BF)
    rest = values - high.astype(F32)
    middle = rest.astype(BF)
    return high.astype(F32), middle.astype(F32), (rest - middle.astype(F32)).astype(BF).astype(F32)


def attend_back_block(
    i, q_ref, k_ref, v_ref, qx_ref, kx_ref, vx_ref, o_ref, lse_ref, do_ref,
    dq_ref, dk_ref, dv_ref, qs, dos, dqa,
):
    rows = block_rows(i)
    lane = lax.broadcasted_iota(jnp.int32, (BLOCK, HD), 1)
    for h in range(2):
        part = slice(h * BLOCK, (h + 1) * BLOCK)
        cols = slice(h * HD, (h + 1) * HD)
        qs[part, 0:HD] = q_ref[rows, cols]
        extra = qx_ref[rows, :].astype(F32)
        for k, term in enumerate(in_three(lse_ref[rows, h : h + 1])):
            extra = jnp.where(lane == 4 + k, -term, extra)
        qs[part, HD:] = extra.astype(BF)
        d = do_ref[rows, cols]
        dos[part, 0:HD] = d
        inner = jnp.sum(d.astype(F32) * o_ref[rows, cols].astype(F32), axis=1, keepdims=True)
        extra = jnp.zeros((BLOCK, HD), F32)
        for k, term in enumerate(in_three(inner)):
            extra = jnp.where(lane == k, -term, extra)
        dos[part, HD:] = extra.astype(BF)

    def step(kr, diagonal):
        kk = jnp.concatenate([k_ref[kr, :], kx_ref[kr, :]], axis=1)
        vv = jnp.concatenate([v_ref[kr, :], vx_ref[kr, :]], axis=1)
        p = jnp.exp2(dot_t(kk, qs[...]) * SCORE)
        if diagonal:
            index = lax.broadcasted_iota(jnp.int32, (BLOCK, 2 * BLOCK), 0)
            query = lax.broadcasted_iota(jnp.int32, (BLOCK, 2 * BLOCK), 1) & (BLOCK - 1)
            p = jnp.where(index <= query, p, 0.0)
        ds = (p * dot_t(vv, dos[...])).astype(BF)
        dv_ref[kr, :] += dot(p.astype(BF), dos[:, 0:HD])
        dk_ref[kr, :] += dot(ds, qs[:, 0:HD])
        dq = t_dot(ds, kk[:, 0:HD])
        if diagonal:
            dqa[...] = dq
        else:
            dqa[...] += dq

    step(rows, True)

    def wide(j, carry):
        step(wide_rows(j), False)
        return carry

    def narrow(j, carry):
        step(block_rows(j), False)
        return carry

    lax.fori_loop(0, i // 2, wide, 0)
    lax.fori_loop(i // 2 * 2, i, narrow, 0)
    for h in range(2):
        dq_ref[rows, h * HD : (h + 1) * HD] = dqa[h * BLOCK : (h + 1) * BLOCK, :] * HD**-0.5


def attention_back_kernel(
    q_ref, k_ref, v_ref, qx_ref, kx_ref, vx_ref, o_ref, lse_ref, do_ref,
    act_ref, wred_ref, hid_ref, pred_ref, pexp_ref, pout_ref,
    dq_ref, dk_ref, dv_ref, y_ref, gred_ref, gexp_ref, gout_ref,
    qs, dos, dqa, *rest,
):
    z, core, x, y = place()
    line_bufs, rest = rest[:7], rest[7:]
    planes = [
        PlaneScatter(part, *rest[5 * n : 5 * n + 5]) for n, part in enumerate((pred_ref, pexp_ref, pout_ref))
    ]
    scatter = LineScatter(*line_bufs)
    keep, give = line_bufs[0], line_bufs[1]
    meet(line_peers() + plane_peers())
    for plane in planes:
        plane.begin()
    for offset in (2, 1, 3, 0):
        chip = lax.rem(z + offset, 4) * 2
        give[offset] = (
            dot(act_ref[block_rows(chip + 1 - core), :], wred_ref[...]).astype(BF).reshape(2, 128, D)
        )
        scatter.give(offset)
        keep[offset] = dot(act_ref[block_rows(chip + core), :], wred_ref[...]).reshape(2, 128, D)
    scatter.far()
    scatter.near()
    dk_ref[...] = jnp.zeros_like(dk_ref)
    dv_ref[...] = jnp.zeros_like(dv_ref)

    def block(t, carry):
        attend_back_block(
            7 - t, q_ref, k_ref, v_ref, qx_ref, kx_ref, vx_ref, o_ref, lse_ref, do_ref,
            dq_ref, dk_ref, dv_ref, qs, dos, dqa,
        )

        @pl.when(t == 0)
        def _():
            scatter.last()

        @pl.when(t == 2)
        def _():
            for plane in planes:
                plane.pass_on()

        return carry

    lax.fori_loop(0, 8, block, 0)
    dk_ref[...] *= HD**-0.5
    first, second = scatter.result()
    y_ref[...] = (hid_ref[...] + jnp.concatenate([first, second], axis=0)).astype(BF)
    for plane, out in zip(planes, (gred_ref, gexp_ref, gout_ref)):
        plane.end(out)
        plane.sent()
    scatter.sent()


def attention_back(*args):
    sh = jax.ShapeDtypeStruct
    return pl.pallas_call(
        attention_back_kernel,
        out_shape=(
            sh((2048, 256), F32),
            sh((2048, 128), F32),
            sh((2048, 128), F32),
            sh((256, D), BF),
            sh((RED_ROWS, D), F32),
            sh((64, EXP_COLS), F32),
            sh((16, D), F32),
        ),
        in_specs=[VMEM] * 15,
        out_specs=[VMEM] * 7,
        scratch_shapes=[
            pltpu.VMEM((2 * BLOCK, 256), BF),
            pltpu.VMEM((2 * BLOCK, 256), BF),
            pltpu.VMEM((2 * BLOCK, HD), F32),
        ]
        + line_scatter_scratch(128, D)
        + plane_scatter_scratch(RED_ROWS, D)
        + plane_scatter_scratch(64, EXP_COLS)
        + plane_scatter_scratch(16, D),
        compiler_params=pltpu.CompilerParams(
            collective_id=4, has_side_effects=True, vmem_limit_bytes=60 * 2**20
        ),
        name="attention_back",
    )(*args)


def from_received(got, gin, gexp):
    col = 0
    for ref, start, width in (
        (gin, 0, 256),
        (gin, H * HD, 128),
        (gin, (H + KV) * HD, 128),
        (gexp, 0, 384),
        (gexp, FF, 384),
    ):
        for j in range(8):
            ref[:, start + j * width : start + (j + 1) * width] = got[j, :, col : col + width]
        col += width


def last_kernel(
    dq_ref, dk_ref, dv_ref, raw_ref, cos_ref, sin_ref, gain_ref, a_ref, win_ref, x_ref, dhid_ref, dmid_ref, gexp_ref,
    dx_ref, gin_out, gexp_out, dgain_ref,
    perm, dqkv, parts, gin, csend, cgot, gsum, gdp, gx, gy,
    keep, give, took, out_z, in_z, s_send, s_recv,
    got1, between, got2, p_send, p_recv, c_send, c_recv, g_send, g_recv,
):
    z, core, x, y = place()
    dp = lax.axis_index("dp")
    peers = dp_peers()
    meet(peers + plane_peers())
    scatter = LineScatter(keep, give, took, out_z, in_z, s_send, s_recv)
    plane = PlaneScatter(parts, got1, between, got2, p_send, p_recv)
    gsum[...] = jnp.zeros_like(gsum)

    def block(b):
        rows = block_rows(b)
        for part in range(3):
            cols = slice(part * HD, (part + 1) * HD)
            u = raw_ref[rows, cols]
            d = dq_ref[rows, cols] if part < 2 else dk_ref[rows, :]
            start = 2 * D + (HD if part == 2 else 0)
            gain = gain_ref[0:1, start : start + HD]
            d = d * cos_ref[rows, :] + pltpu.roll(d * sin_ref[rows, :], HD // 2, 1)
            r = normed_rows(u)
            row = 16 + part // 2
            gsum[row : row + 1, :] += jnp.sum(d * u * r, axis=0, keepdims=True)
            dqkv[rows, cols] = rms_back(u, r, gain, d).astype(BF)
        dqkv[rows, 384:512] = dv_ref[rows, :].astype(BF)
        return dot_t(dqkv[rows, :], win_ref[...].reshape(D, IN_COLS)).reshape(2, 128, D)

    for offset in (2, 1, 3, 0):
        chip = lax.rem(z + offset, 4) * 2
        give[offset] = block(chip + 1 - core).astype(BF)
        scatter.give(offset)
        keep[offset] = block(chip + core)
    scatter.far()
    scatter.near()
    parts[...] = t_dot(a_ref[...], dqkv[...]).astype(BF).reshape(4, 4, 64, IN_COLS)
    plane.begin()
    fill_order(perm)
    scatter.last()
    plane.pass_on()
    first, second = scatter.result()
    d_a = unorder(jnp.concatenate([first, second], axis=0), perm[...])
    values = x_ref[...].astype(F32)
    r = normed_rows(values)
    dx_ref[...] = dhid_ref[...] + rms_back(values, r, gain_ref[0:1, 0:D], d_a)
    d_in = jnp.sum(d_a * values * r, axis=0, keepdims=True)
    for k in range(8):
        gsum[k : k + 1, :] = d_in[:, k * 128 : (k + 1) * 128]
        gsum[8 + k : 9 + k, :] = dmid_ref[0:1, k * 128 : (k + 1) * 128]
    first_copies = [
        remote(gsum, gdp.at[k - 1], g_send.at[k - 1], g_recv.at[k - 1], peers[k - 1]) for k in range(1, 8)
    ]
    for copy in first_copies:
        copy.start()
    plane.end(gin)
    for d in range(8):
        csend[d, :, 0:IN_COLS] = gin[8 * d : 8 * d + 8, :]
        csend[d, :, IN_COLS:] = gexp_ref[8 * d : 8 * d + 8, :]
    cols = [
        remote(csend.at[lax.rem(dp + k, 8)], cgot.at[dp], c_send.at[k - 1], c_recv.at[k - 1], peers[k - 1])
        for k in range(1, 8)
    ]
    for copy in cols:
        copy.start()
    cgot[dp] = csend[dp]
    for copy in first_copies:
        copy.wait_recv()
    total = gsum[...]
    for k in range(7):
        total += gdp[k]
    gx[0] = total
    x_copies = [
        remote(gx.at[0], gx.at[k], g_send.at[6 + k], g_recv.at[6 + k], device(z, core, x + k, y)) for k in (1, 2, 3)
    ]
    for copy in x_copies:
        copy.start()
    for copy in x_copies:
        copy.wait_recv()
    gy[0] = gx[0] + gx[1] + gx[2] + gx[3]
    y_copies = [
        remote(gy.at[0], gy.at[k], g_send.at[9 + k], g_recv.at[9 + k], device(z, core, x, y + k)) for k in (1, 2, 3)
    ]
    for copy in y_copies:
        copy.start()
    for copy in cols:
        copy.wait_recv()
    from_received(cgot, gin_out, gexp_out)
    for copy in y_copies:
        copy.wait_recv()
    dgain_ref[...] = gy[0] + gy[1] + gy[2] + gy[3]
    for copy in first_copies + x_copies + y_copies + cols:
        copy.wait_send()
    scatter.sent()
    plane.sent()


def last(*args):
    sh = jax.ShapeDtypeStruct
    return pl.pallas_call(
        last_kernel,
        out_shape=(sh((256, D), F32), sh((8, 4096), F32), sh((8, 2 * FF), F32), sh((24, 128), F32)),
        in_specs=[VMEM] * 13,
        out_specs=[VMEM] * 4,
        scratch_shapes=[
            pltpu.VMEM((D, D), BF),
            pltpu.VMEM((2048, IN_COLS), BF),
            pltpu.VMEM((4, 4, 64, IN_COLS), BF),
            pltpu.VMEM((64, IN_COLS), F32),
            pltpu.VMEM((8, 8, IN_COLS + EXP_COLS), F32),
            pltpu.VMEM((8, 8, IN_COLS + EXP_COLS), F32),
            pltpu.VMEM((24, 128), F32),
            pltpu.VMEM((7, 24, 128), F32),
            pltpu.VMEM((4, 24, 128), F32),
            pltpu.VMEM((4, 24, 128), F32),
        ]
        + line_scatter_scratch(128, D)
        + plane_scatter_scratch(64, IN_COLS)
        + [pltpu.SemaphoreType.DMA((n,)) for n in (7, 7, 13, 13)],
        compiler_params=pltpu.CompilerParams(
            collective_id=5, has_side_effects=True, vmem_limit_bytes=60 * 2**20
        ),
        name="last",
    )(*args)


def body(
    tokens,
    cotangent,
    lengths,
    weight_input,
    weight_output,
    weight_expand,
    weight_reduce,
    gains,
    first_input,
    first_output,
    first_expand,
    first_reduce,
    first_gains,
    second_input,
    second_output,
    second_expand,
    second_reduce,
    second_gains,
):
    whole = tokens.shape[1] * lax.axis_size("dp")
    segment, cosine, sine = rope_full(lengths[0], whole)
    q_extra, k_extra, v_extra = extra_columns(segment)
    a, raw, q, k, v, win, wexp, gain, wout, wred = front(
        tokens[0],
        weight_input,
        weight_expand,
        padded_gains(gains),
        cosine,
        sine,
        weight_output,
        weight_reduce,
    )
    o, lse, wexp, dy = attention(q, k, v, q_extra, k_extra, v_extra, wexp, cotangent[0])
    hid, d_hid, act, d_o, part_red, part_exp, part_out, d_gain_mid, wred = mid(
        tokens[0], o, wout, wexp, wred, dy, gain
    )
    dq, dk, dv, block_out, sum_red, sum_exp, grad_output = attention_back(
        q, k, v, q_extra, k_extra, v_extra, o, lse, d_o, act, wred, hid, part_red, part_exp, part_out
    )
    input_grad, grad_input, grad_expand, grad_gains = last(
        dq, dk, dv, raw, cosine, sine, gain, a, win, tokens[0], d_hid, d_gain_mid, sum_exp
    )
    block_out = block_out[None]
    input_grad = input_grad[None]
    grad_reduce = sum_red[: weight_reduce.shape[0]]
    own = gains.shape[0]
    index = lax.axis_index("dp") * lax.axis_size("shard") + lax.axis_index("shard")
    grad_gains = lax.dynamic_slice_in_dim(grad_gains.reshape(-1), index * own, own)
    new_input, mean_input, square_input = adam_step(
        weight_input, grad_input, first_input, second_input, matrix_rate, matrix_decay
    )
    new_output, mean_output, square_output = adam_step(
        weight_output, grad_output, first_output, second_output, matrix_rate, matrix_decay
    )
    new_expand, mean_expand, square_expand = adam_step(
        weight_expand, grad_expand, first_expand, second_expand, matrix_rate, matrix_decay
    )
    new_reduce, mean_reduce, square_reduce = adam_step(
        weight_reduce, grad_reduce, first_reduce, second_reduce, matrix_rate, matrix_decay
    )
    new_gains, mean_gains, square_gains = adam_step(
        gains, grad_gains, first_gains, second_gains, gain_rate, 0.0
    )
    return (
        block_out,
        input_grad,
        new_input,
        new_output,
        new_expand,
        new_reduce,
        new_gains,
        mean_input,
        mean_output,
        mean_expand,
        mean_reduce,
        mean_gains,
        square_input,
        square_output,
        square_expand,
        square_reduce,
        square_gains,
    )


def solution(mesh):
    placed = (
        P("shard", "dp", None),
        P("shard", "dp", None),
        P("shard", None),
        P(("dp", "shard"), None),
        P(("dp", "shard"), None),
        P(("dp", "shard"), None),
        P(("dp", "shard"), None),
        P(("dp", "shard")),
        P(("dp", "shard"), None),
        P(("dp", "shard"), None),
        P(("dp", "shard"), None),
        P(("dp", "shard"), None),
        P(("dp", "shard")),
        P(("dp", "shard"), None),
        P(("dp", "shard"), None),
        P(("dp", "shard"), None),
        P(("dp", "shard"), None),
        P(("dp", "shard")),
    )
    return jax.shard_map(
        body,
        mesh=mesh,
        in_specs=placed,
        out_specs=(
            P("shard", "dp", None),
            P("shard", "dp", None),
            P(("dp", "shard"), None),
            P(("dp", "shard"), None),
            P(("dp", "shard"), None),
            P(("dp", "shard"), None),
            P(("dp", "shard")),
            P(("dp", "shard"), None),
            P(("dp", "shard"), None),
            P(("dp", "shard"), None),
            P(("dp", "shard"), None),
            P(("dp", "shard")),
            P(("dp", "shard"), None),
            P(("dp", "shard"), None),
            P(("dp", "shard"), None),
            P(("dp", "shard"), None),
            P(("dp", "shard")),
        ),
        check_vma=False,
    )
```

```python
import math

import jax
import jax.numpy as jnp
import numpy as np
from jax import lax
from jax.experimental import pallas as pl
from jax.experimental.pallas import tpu as pltpu
from jax.sharding import PartitionSpec as P

D = 1024
H = 16
KV = 8
HD = 128
FF = 3072
STEP = 10


norm_eps = 1e-06
rope_base = 1000000.0
beta_one = 0.9
beta_two = 0.95
adam_eps = 1e-08
matrix_rate = 0.1
gain_rate = 0.5
matrix_decay = 0.1
masked_score = -1e30


def adam_step(weight, grad, first, second, rate, decay):
    first_new = beta_one * first + (1.0 - beta_one) * grad
    second_new = beta_two * second + (1.0 - beta_two) * grad * grad
    fix_one = 1.0 - beta_one**STEP
    fix_two = 1.0 - beta_two**STEP
    direction = first_new / fix_one / (jnp.sqrt(second_new / fix_two) + adam_eps)
    return (weight - rate * (direction + decay * weight), first_new, second_new)


MESH = pl.DeviceIdType.MESH
F32 = jnp.float32
BF = jnp.bfloat16
VMEM = pl.BlockSpec(memory_space=pltpu.VMEM)
HBM = pl.BlockSpec(memory_space=pl.ANY)
SCORE = HD**-0.5 * math.log2(math.e)
BLOCK = 256
BIG = 30000.0
IN_COLS = (H + 2 * KV) * HD // 8
EXP_COLS = 2 * FF // 8
RED_ROWS = 32


def dot(a, b):
    return jnp.dot(a, b, preferred_element_type=F32)


def dot_t(a, b):
    return lax.dot_general(a, b, (((1,), (1,)), ((), ())), preferred_element_type=F32)


def t_dot(a, b):
    return lax.dot_general(a, b, (((0,), (0,)), ((), ())), preferred_element_type=F32)


def in_three(values):
    high = values.astype(BF)
    rest = values - high.astype(F32)
    middle = rest.astype(BF)
    return high.astype(F32), middle.astype(F32), (rest - middle.astype(F32)).astype(BF).astype(F32)


def block_rows(i):
    return pl.ds(pl.multiple_of(i * BLOCK, BLOCK), BLOCK)


def wide_rows(i):
    return pl.ds(pl.multiple_of(i * 2 * BLOCK, 2 * BLOCK), 2 * BLOCK)


def place():
    dp = lax.axis_index("dp")
    shard = lax.axis_index("shard")
    return dp // 2, lax.rem(dp, 2), shard // 4, lax.rem(shard, 4)


def device(z, core, x, y):
    return (lax.rem(z, 4) * 2 + core, lax.rem(x, 4) * 4 + lax.rem(y, 4))


def line_peers():
    z, core, x, y = place()
    return [device(z, 1 - core, x, y), device(z + 1, core, x, y), device(z + 3, core, x, y)]


def plane_peers():
    z, core, x, y = place()
    return [device(z, core, x + k, y) for k in (1, 2, 3)] + [
        device(z, core, x, y + k) for k in (1, 2, 3)
    ]


def dp_peers():
    dp = lax.axis_index("dp")
    shard = lax.axis_index("shard")
    return [(lax.rem(dp + k, 8), shard) for k in range(1, 8)]


def greet(peers):
    for peer in peers:
        pl.semaphore_signal(
            pltpu.get_barrier_semaphore(), inc=1, device_id=peer, device_id_type=MESH
        )


def meet(peers):
    pl.semaphore_wait(pltpu.get_barrier_semaphore(), len(peers))


def remote(src, dst, send, recv, peer):
    return pltpu.make_async_remote_copy(
        src_ref=src, dst_ref=dst, send_sem=send, recv_sem=recv, device_id=peer, device_id_type=MESH
    )


class LineGather:
    sems = 13

    def __init__(self, buf, send, recv):
        z, core, x, y = place()
        me, right, far, left = (lax.rem(z + k, 4) * 2 + core for k in range(4))
        to_right, to_left = device(z + 1, core, x, y), device(z + 3, core, x, y)
        sibling = device(z, 1 - core, x, y)
        plan = [
            (me, 0, to_right),
            (me, 1, to_right),
            (left, 0, to_right),
            (me, 1, to_left),
            (me, 0, to_left),
            (right, 1, to_left),
            (me, None, sibling),
            (left, 0, sibling),
            (right, 1, sibling),
            (left, 1, sibling),
            (right, 0, sibling),
            (far, 0, sibling),
            (far, 1, sibling),
        ]
        self.copies = []
        for k, (slot, half, peer) in enumerate(plan):
            ref = buf.at[slot] if half is None else buf.at[slot, half]
            self.copies.append(remote(ref, ref, send.at[k], recv.at[k], peer))

    def start(self, *which):
        for k in which:
            self.copies[k].start()

    def wait(self, *which):
        for k in which:
            self.copies[k].wait_recv()

    def begin(self):
        self.start(6, 0, 3, 1, 4)

    def pass_on(self):
        self.wait(0)
        self.start(2, 7)
        self.wait(3)
        self.start(5, 8)

    def second(self):
        self.wait(1)
        self.start(9)
        self.wait(4)
        self.start(10)

    def third(self):
        self.wait(2)
        self.start(11)
        self.wait(5)
        self.start(12)

    def sent(self):
        for copy in self.copies:
            copy.wait_send()


class PlaneGather:
    sems = 12

    def __init__(self, buf, send, recv):
        z, core, x, y = place()
        half = buf.shape[3] // 2
        low, high = pl.ds(0, half), pl.ds(half, half)
        self.copies = []
        refs = (
            (buf.at[x, y, :, low], 0),
            (buf.at[x, y, :, high], 1),
            (buf.at[:, y, :, low], 1),
            (buf.at[x, :, :, high], 0),
        )
        k = 0
        for ref, along_y in refs:
            for step in (1, 2, 3):
                peer = device(z, core, x, y + step) if along_y else device(z, core, x + step, y)
                self.copies.append(remote(ref, ref, send.at[k], recv.at[k], peer))
                k += 1

    def begin(self):
        for k in (0, 3, 1, 4, 2, 5):
            self.copies[k].start()

    def pass_on(self):
        for k in (0, 1, 2):
            self.copies[k].wait_recv()
        for k in (6, 7, 8):
            self.copies[k].start()
        for k in (3, 4, 5):
            self.copies[k].wait_recv()
        for k in (9, 10, 11):
            self.copies[k].start()

    def end(self):
        for k in range(6, 12):
            self.copies[k].wait_recv()

    def sent(self):
        for copy in self.copies:
            copy.wait_send()


class PlaneScatter:
    sems = 12

    def __init__(self, parts, got1, mid, got2, send, recv):
        z, core, x, y = place()
        self.parts, self.got1, self.mid, self.got2 = parts, got1, mid, got2
        half = parts.shape[3] // 2
        self.cols = (pl.ds(0, half), pl.ds(half, half))
        self.x, self.y = x, y
        self.copies = []
        k = 0
        for side in (0, 1):
            for step in (1, 2, 3):
                if side == 0:
                    ref = parts.at[:, lax.rem(y + step, 4), :, self.cols[0]]
                    peer = device(z, core, x, y + step)
                else:
                    ref = parts.at[lax.rem(x + step, 4), :, :, self.cols[1]]
                    peer = device(z, core, x + step, y)
                self.copies.append(remote(ref, got1.at[side, step - 1], send.at[k], recv.at[k], peer))
                k += 1
        for side in (0, 1):
            for step in (1, 2, 3):
                if side == 0:
                    ref = mid.at[0, lax.rem(x + step, 4)]
                    peer = device(z, core, x + step, y)
                else:
                    ref = mid.at[1, lax.rem(y + step, 4)]
                    peer = device(z, core, x, y + step)
                self.copies.append(remote(ref, got2.at[side, step - 1], send.at[k], recv.at[k], peer))
                k += 1

    def begin(self):
        for k in (0, 3, 1, 4, 2, 5):
            self.copies[k].start()

    def pass_on(self):
        for side in (0, 1):
            for k in range(3 * side, 3 * side + 3):
                self.copies[k].wait_recv()
            for j in range(4):
                if side == 0:
                    own = self.parts[j, self.y, :, self.cols[0]]
                else:
                    own = self.parts[self.x, j, :, self.cols[1]]
                total = own.astype(F32)
                for k in range(3):
                    total += self.got1[side, k, j].astype(F32)
                self.mid[side, j] = total.astype(BF)
            for k in range(6 + 3 * side, 9 + 3 * side):
                self.copies[k].start()

    def end(self, out):
        for side in (0, 1):
            for k in range(6 + 3 * side, 9 + 3 * side):
                self.copies[k].wait_recv()
            total = self.mid[side, self.x if side == 0 else self.y].astype(F32)
            for k in range(3):
                total += self.got2[side, k].astype(F32)
            out[:, self.cols[side]] = total

    def sent(self):
        for copy in self.copies:
            copy.wait_send()


def plane_scatter_scratch(rows, width):
    half = width // 2
    return [
        pltpu.VMEM((2, 3, 4, rows, half), BF),
        pltpu.VMEM((2, 4, rows, half), BF),
        pltpu.VMEM((2, 3, rows, half), BF),
        pltpu.SemaphoreType.DMA((12,)),
        pltpu.SemaphoreType.DMA((12,)),
    ]


class LineScatter:
    sems = 10

    def __init__(self, keep, give, took, out_z, in_z, send, recv):
        z, core, x, y = place()
        self.keep, self.took, self.out_z, self.in_z = keep, took, out_z, in_z
        to_right, to_left = device(z + 1, core, x, y), device(z + 3, core, x, y)
        sibling = device(z, 1 - core, x, y)
        self.exchange = lambda k: remote(give.at[k], took.at[k], send.at[k], recv.at[k], sibling)
        self.swap = [self.exchange(k) for k in range(4)]
        self.copies = [
            remote(
                out_z.at[k], in_z.at[k], send.at[4 + k], recv.at[4 + k], to_right if k < 3 else to_left
            )
            for k in range(6)
        ]

    def give(self, offset):
        self.swap[offset].start()

    def give_at(self, offset):
        self.exchange(offset).start()

    def take(self, offset):
        self.swap[offset].wait_recv()

    def half(self, offset, part):
        return self.keep[offset, part] + self.took[offset, part].astype(F32)

    def push(self, k, value):
        self.out_z[k] = value.astype(BF)
        self.copies[k].start()

    def far(self):
        self.take(2)
        self.push(0, self.half(2, 0))
        self.push(3, self.half(2, 1))

    def near_right(self):
        self.take(1)
        self.push(1, self.half(1, 1))

    def near_left(self):
        self.take(3)
        self.push(4, self.half(3, 0))

    def near(self):
        self.near_right()
        self.near_left()

    def last(self):
        self.copies[0].wait_recv()
        self.push(2, self.half(1, 0) + self.in_z[0].astype(F32))
        self.copies[3].wait_recv()
        self.push(5, self.half(3, 1) + self.in_z[3].astype(F32))

    def result(self):
        self.take(0)
        self.copies[1].wait_recv()
        self.copies[4].wait_recv()
        self.copies[2].wait_recv()
        first = self.half(0, 0) + self.in_z[4].astype(F32) + self.in_z[2].astype(F32)
        self.copies[5].wait_recv()
        second = self.half(0, 1) + self.in_z[1].astype(F32) + self.in_z[5].astype(F32)
        return first, second

    def sent(self):
        for copy in self.swap + self.copies:
            copy.wait_send()


def line_scatter_scratch(rows, width):
    return [
        pltpu.VMEM((4, 2, rows, width), F32),
        pltpu.VMEM((4, 2, rows, width), BF),
        pltpu.VMEM((4, 2, rows, width), BF),
        pltpu.VMEM((6, rows, width), BF),
        pltpu.VMEM((6, rows, width), BF),
        pltpu.SemaphoreType.DMA((10,)),
        pltpu.SemaphoreType.DMA((10,)),
    ]


def to_send(w_in, gains, out):
    col = 0
    for ref, start, width in ((w_in, 0, 256), (w_in, H * HD, 128), (w_in, (H + KV) * HD, 128)):
        for j in range(8):
            out[j, :, col : col + width] = ref[:, start + j * width : start + (j + 1) * width]
        col += width
    out[:, :, col : col + 128] = jnp.zeros((8, 8, 128), F32)
    for j in range(8):
        out[j, 0:1, col : col + 18] = gains[...]


def spread_gains(gbuf):
    wide = 128 * 18
    held = gbuf[:, :, :, 0:128].reshape(128, 128)
    n = lax.broadcasted_iota(jnp.int32, (128, wide), 1)
    r = lax.broadcasted_iota(jnp.int32, (128, wide), 0)
    nf = n.astype(F32)
    within = nf - 18.0 * jnp.floor((nf + 0.5) * (1.0 / 18.0))
    pick = jnp.where(within == r.astype(F32), 1.0, 0.0)
    spread = jnp.dot(held, pick, precision=lax.Precision.HIGHEST, preferred_element_type=F32)
    first = ((r & 7) * 16 + (r >> 3)) * 18
    return jnp.sum(jnp.where((n >= first) & (n < first + 18), spread, 0.0), axis=0, keepdims=True)


def fill_order(perm):
    def block(i, carry):
        n = lax.broadcasted_iota(jnp.int32, (128, D), 0)
        k = lax.broadcasted_iota(jnp.int32, (128, D), 1)
        goal = (n >> 3) * 64 + i * 8 + (n & 7)
        perm[pl.ds(pl.multiple_of(i * 128, 128), 128), :] = jnp.where(k == goal, 1.0, 0.0).astype(BF)
        return carry

    lax.fori_loop(0, 8, block, 0)


def normed_rows(values):
    return lax.rsqrt(jnp.mean(values * values, axis=-1, keepdims=True) + norm_eps)


def token_tables(block, lengths, freq, table, q_ref, k_ref, v_ref):
    rows = block_rows(block)
    end0 = lengths[0, 0]
    end1 = end0 + lengths[0, 1]
    end2 = end1 + lengths[0, 2]
    token = block * BLOCK + lax.broadcasted_iota(jnp.int32, (BLOCK, HD), 0)
    lane = lax.broadcasted_iota(jnp.int32, (BLOCK, HD), 1)
    start = jnp.where(token >= end2, end2, jnp.where(token >= end1, end1, jnp.where(token >= end0, end0, 0)))
    angle = (token - start).astype(F32) * freq[0:1, :]
    table[rows, :] = jnp.sin(angle + jnp.where(lane < HD // 2, math.pi / 2, 0.0))
    one = lambda test: jnp.where(test, 1, 0)
    segment = one(token >= end0) + one(token >= end1) + one(token >= end2)
    same = segment == lane
    q_ref[rows, 256:384] = jnp.where(lane < 4, jnp.where(same, 0.0, -BIG), 0.0).astype(BF)
    k_ref[rows, 128:256] = jnp.where(lane < 4, jnp.where(same, 1.0, 0.0), jnp.where(lane < 7, 1.0, 0.0)).astype(BF)
    v_ref[rows, 128:256] = jnp.where(lane < 3, 1.0, 0.0).astype(BF)


def both_tables(table):
    lane = lax.broadcasted_iota(jnp.int32, table.shape, 1)
    other = pltpu.roll(table, HD // 2, 1)
    return jnp.where(lane < HD // 2, table, other), jnp.where(lane < HD // 2, -other, table)


def front_kernel(
    x_ref, w_in_ref, w_exp_ref, gains_ref, freq_ref, w_out_ref, dy_ref, lengths,
    a_out, raw_out, q_out, k_out, v_out, table_out, win_out, wout_out, dy_out, wexp_ref, gain_ref,
    xall, raw, q_ref, k_ref, v_ref, table, win_ref, wout_all, dy_all,
    wsend, wgot, esend, egot, gbuf, perm, weight,
    line_send, line_recv, cols_send, cols_recv, e_send, e_recv, win_send, win_recv, g_send, g_recv,
    o_send, o_recv, dy_send, dy_recv, out_sem, w_sem,
):
    z, core, x, y = place()
    dp = lax.axis_index("dp")
    peers = dp_peers()
    greet(peers + plane_peers())
    to_send(w_in_ref, gains_ref, wsend)
    wout_all[x, y] = w_out_ref[...].astype(BF)
    dy_all[dp] = dy_ref[:, 0 : D // 2].reshape(2, 128, D // 2)
    fill_order(perm)
    values = x_ref[...].astype(F32)
    normed = (values * normed_rows(values)).astype(BF)
    xall[dp] = dot(normed, perm[...]).astype(BF).reshape(2, 128, D)
    meet(peers + plane_peers())

    def exchange(src, dst, send, recv):
        copies = [
            remote(src.at[lax.rem(dp + k, 8)], dst.at[dp], send.at[k - 1], recv.at[k - 1], peers[k - 1])
            for k in range(1, 8)
        ]
        for copy in copies:
            copy.start()
        return copies

    cols = exchange(wsend, wgot, cols_send, cols_recv)
    line = LineGather(xall, line_send, line_recv)
    line.begin()
    wgot[dp] = wsend[dp]
    for j in range(8):
        for part in range(2):
            start = part * FF + j * 384
            esend[j, :, part * 384 : (part + 1) * 384] = w_exp_ref[:, start : start + 384]
    for copy in cols:
        copy.wait_recv()
    win_ref[x, y] = wgot[:, :, 0:IN_COLS].reshape(64, IN_COLS).astype(BF)
    own_gains = wgot[:, 0, IN_COLS:]
    gbuf[x, y, :, 0:128] = own_gains
    gbuf[x, y, :, 128:256] = own_gains
    plane_g = PlaneGather(gbuf, g_send, g_recv)
    plane_w = PlaneGather(win_ref, win_send, win_recv)
    plane_g.begin()
    plane_w.begin()
    ecols = exchange(esend, egot, e_send, e_recv)
    egot[dp] = esend[dp]

    def tables(block, carry):
        token_tables(block, lengths, freq_ref, table, q_ref, k_ref, v_ref)
        return carry

    plane_g.pass_on()
    plane_w.pass_on()
    lax.fori_loop(0, 4, tables, 0)
    line.pass_on()
    plane_g.end()
    gains = spread_gains(gbuf)
    gain_ref[0:8, :] = jnp.broadcast_to(gains, (8, 2304))
    moved = jnp.zeros((8, D), F32)
    for term in in_three(gain_ref[0:8, 0:D]):
        moved += dot(term.astype(BF), perm[...])
    gain_ref[8:16, 0:D] = moved
    first = jnp.where(lax.broadcasted_iota(jnp.int32, (8, 128), 0) == 0, 1.0, 0.0)
    column = lax.dot_general(
        moved, first, (((0,), (0,)), ((), ())), precision=lax.Precision.HIGHEST, preferred_element_type=F32
    )[:, 0:1]
    plane_w.end()
    plane_o = PlaneGather(wout_all, o_send, o_recv)
    plane_o.begin()
    weight[...] = (win_ref[...].reshape(D, IN_COLS).astype(F32) * column).astype(BF)
    keep_weight = pltpu.make_async_copy(weight, win_out, w_sem.at[0])
    keep_weight.start()
    lax.fori_loop(4, 8, tables, 0)

    def rows_of(block, carry):
        rows = block_rows(block)
        qkv = dot(xall[block].reshape(256, D), weight[...])
        raw[rows, :] = qkv[:, 0:384]
        cos, sin = both_tables(table[rows, :])
        for part in range(3):
            u = qkv[:, part * HD : (part + 1) * HD]
            start = 2 * D + (HD if part == 2 else 0)
            u = u * normed_rows(u) * gain_ref[0:1, start : start + HD]
            u = (u * cos + pltpu.roll(u, HD // 2, 1) * sin).astype(BF)
            if part < 2:
                q_ref[rows, part * HD : (part + 1) * HD] = u
            else:
                k_ref[rows, 0:HD] = u
        v_ref[rows, 0:HD] = qkv[:, 384:512].astype(BF)
        return carry

    def chip(offset):
        first = lax.rem(z + offset, 4) * 2
        lax.fori_loop(first, first + 2, rows_of, 0)

    outs = []

    def write(offset):
        chip_at = lax.rem(z + offset, 4)
        rows = pl.ds(pl.multiple_of(chip_at * 512, 512), 512)
        blocks = pl.ds(chip_at * 2, 2)
        pairs = [(xall.at[blocks], a_out.at[blocks])]
        pairs += [
            (ref.at[rows, :], out.at[rows, :])
            for ref, out in ((raw, raw_out), (q_ref, q_out), (k_ref, k_out), (v_ref, v_out), (table, table_out))
        ]
        for n, (src, dst) in enumerate(pairs):
            copy = pltpu.make_async_copy(src, dst, out_sem.at[6 * offset + n])
            copy.start()
            outs.append(copy)

    line.wait(6)
    chip(0)
    write(0)
    line.second()
    line_dy = LineGather(dy_all, dy_send, dy_recv)
    line_dy.begin()
    plane_o.pass_on()
    line.wait(7, 8, 9, 10)

    def near(t, carry):
        first = lax.rem(z + 1 + 2 * (t // 2), 4) * 2
        return rows_of(first + lax.rem(t, 2), carry)

    lax.fori_loop(0, 4, near, 0)
    write(1)
    write(3)
    line.third()
    line.wait(11, 12)
    line_dy.pass_on()
    chip(2)
    write(2)
    line_dy.second()
    for copy in ecols:
        copy.wait_recv()
    wexp_ref[...] = egot[...].reshape(64, EXP_COLS).astype(BF)
    plane_o.end()
    line_dy.third()
    line_dy.wait(6, 7, 8, 9, 10, 11, 12)
    for n, (src, dst) in enumerate(((wout_all, wout_out), (dy_all, dy_out))):
        copy = pltpu.make_async_copy(src, dst, w_sem.at[1 + n])
        copy.start()
        outs.append(copy)
    line.sent()
    line_dy.sent()
    plane_o.sent()
    plane_g.sent()
    plane_w.sent()
    for copy in cols + ecols:
        copy.wait_send()
    for copy in [keep_weight] + outs:
        copy.wait()


def front(x, w_in, w_exp, gains, freq, w_out, dy, lengths):
    sh = jax.ShapeDtypeStruct
    held = [
        ((8, 2, 128, D), BF),
        ((2048, 384), F32),
        ((2048, 384), BF),
        ((2048, 256), BF),
        ((2048, 256), BF),
        ((2048, 128), F32),
    ]
    return pl.pallas_call(
        front_kernel,
        out_shape=tuple(sh(*one) for one in held)
        + (
            sh((D, IN_COLS), BF),
            sh((4, 4, 16, D), BF),
            sh((8, 2, 128, D // 2), BF),
            sh((64, EXP_COLS), BF),
            sh((16, 2304), F32),
        ),
        in_specs=[VMEM] * 7 + [pl.BlockSpec(memory_space=pltpu.SMEM)],
        out_specs=[HBM] * 9 + [VMEM] * 2,
        scratch_shapes=[pltpu.VMEM(*one) for one in held]
        + [
            pltpu.VMEM((4, 4, 64, IN_COLS), BF),
            pltpu.VMEM((4, 4, 16, D), BF),
            pltpu.VMEM((8, 2, 128, D // 2), BF),
            pltpu.VMEM((8, 8, IN_COLS + 128), F32),
            pltpu.VMEM((8, 8, IN_COLS + 128), F32),
            pltpu.VMEM((8, 8, EXP_COLS), F32),
            pltpu.VMEM((8, 8, EXP_COLS), F32),
            pltpu.VMEM((4, 4, 8, 256), F32),
            pltpu.VMEM((D, D), BF),
            pltpu.VMEM((D, IN_COLS), BF),
        ]
        + [pltpu.SemaphoreType.DMA((n,)) for n in (13, 13, 7, 7, 7, 7, 12, 12, 12, 12, 12, 12, 13, 13, 24, 3)],
        compiler_params=pltpu.CompilerParams(
            collective_id=1, has_side_effects=True, vmem_limit_bytes=56 * 2**20
        ),
        name="front",
    )(x, w_in, w_exp, gains, freq, w_out, dy, lengths)


def rope_rates():
    half = HD // 2
    rates = np.float32(rope_base) ** (-(2.0 * np.arange(half, dtype=np.float32)) / np.float32(HD))
    return jnp.asarray(np.tile(np.concatenate([rates, rates])[None], (8, 1)), F32)


def attend_block(i, q_ref, k_ref, v_ref, o_ref, lse_ref, acc, qs):
    rows = block_rows(i)
    for h in range(2):
        qs[h * BLOCK : (h + 1) * BLOCK, 0:HD] = q_ref[rows, h * HD : (h + 1) * HD]
        qs[h * BLOCK : (h + 1) * BLOCK, HD:] = q_ref[rows, 2 * HD :]

    query = lax.broadcasted_iota(jnp.int32, (2 * BLOCK, BLOCK), 0) & (BLOCK - 1)
    index = lax.broadcasted_iota(jnp.int32, (2 * BLOCK, BLOCK), 1)
    e = jnp.where(index <= query, jnp.exp2(dot_t(qs[...], k_ref[rows, :]) * SCORE), 0.0)
    acc[...] = dot(e.astype(BF), v_ref[rows, :])

    def step(kr):
        acc[...] += dot(jnp.exp2(dot_t(qs[...], k_ref[kr, :]) * SCORE).astype(BF), v_ref[kr, :])

    def wide(j, carry):
        step(wide_rows(j))
        return carry

    def narrow(j, carry):
        step(block_rows(j))
        return carry

    lax.fori_loop(0, i // 2, wide, 0)
    lax.fori_loop(i // 2 * 2, i, narrow, 0)
    total = acc[:, HD : HD + 1]
    out = acc[:, 0:HD] * (1.0 / total)
    lse = jnp.log2(total) * (1.0 / SCORE)
    for h in range(2):
        part = slice(h * BLOCK, (h + 1) * BLOCK)
        o_ref[rows, h * HD : (h + 1) * HD] = out[part].astype(BF)
        lse_ref[rows, h : h + 1] = lse[part]


def rms_back(h, r, dg):
    return r * dg - h * (r * r * r) * jnp.mean(h * dg, axis=-1, keepdims=True)


def unorder(values, perm):
    high = values.astype(BF)
    low = (values - high.astype(F32)).astype(BF)
    return dot_t(high, perm) + dot_t(low, perm)


def core_kernel(
    q_ref, k_ref, v_ref, x_ref, wout_ref, wexp_own, wred_own, dy_own, dy_left, gain_ref,
    o_out, lse_out, hid_ref, dhid_ref, act_out, do_out, gred_ref, gexp_ref, gout_ref, dgain_ref, wred_out,
    o_ref, lse_ref, act_ref, do_ref, wred,
    acc, qs, wexp, wred_all, dy_right, perm, ball, datt, dgu,
    keep, give, took, out_z, in_z,
    e_send, e_recv, r_send, r_recv, y_send, y_recv,
    s1_send, s1_recv, b_send, b_recv, s2_send, s2_recv, d_send, d_recv, out_sem,
):
    z, core, x, y = place()
    dp = lax.axis_index("dp")
    half = FF // 8
    greet(line_peers() + plane_peers())
    wexp[x, y] = wexp_own[...]
    wred_all[x, y] = jnp.concatenate([wred_own[...], jnp.zeros((8, D), F32)], axis=0).astype(BF)
    dy_right[dp] = dy_own[:, D // 2 :].reshape(2, 128, D // 2)
    meet(line_peers() + plane_peers())
    plane_e = PlaneGather(wexp, e_send, e_recv)
    plane_r = PlaneGather(wred_all, r_send, r_recv)
    line_y = LineGather(dy_right, y_send, y_recv)
    line_y.begin()
    plane_e.begin()
    plane_r.begin()
    scatter = LineScatter(keep, give, took, out_z, in_z, s1_send, s1_recv)
    wout = wout_ref[...].reshape(256, D)
    outs = []

    def write(src, dst):
        copy = pltpu.make_async_copy(src, dst, out_sem.at[len(outs)])
        copy.start()
        outs.append(copy)

    def attend(t, carry):
        pair = t // 2
        offset = jnp.where(pair == 0, 2, jnp.where(pair == 1, 1, jnp.where(pair == 2, 3, 0)))
        second = lax.rem(t, 2)
        block = lax.rem(z + offset, 4) * 2 + jnp.where(second == 1, core, 1 - core)
        attend_block(block, q_ref, k_ref, v_ref, o_ref, lse_ref, acc, qs)
        partial = dot(o_ref[block_rows(block), :], wout).reshape(2, 128, D)

        @pl.when(second == 0)
        def _():
            give[offset] = partial.astype(BF)
            scatter.give_at(offset)

        @pl.when(second == 1)
        def _():
            keep[offset] = partial

        @pl.when(t == 1)
        def _():
            scatter.far()
            plane_e.pass_on()
            plane_r.pass_on()
            line_y.pass_on()

        @pl.when(t == 3)
        def _():
            scatter.near_right()

        @pl.when(t == 4)
        def _():
            line_y.second()

        @pl.when(t == 5)
        def _():
            scatter.near_left()

        @pl.when(t == 6)
        def _():
            line_y.third()

        return carry

    lax.fori_loop(0, 8, attend, 0)
    write(o_ref, o_out)
    write(lse_ref, lse_out)
    scatter.last()
    fill_order(perm)
    plane_e.end()
    plane_r.end()
    wred[...] = wred_all[...].astype(F32)[:, :, 0:24, :].reshape(half, D).astype(BF)
    write(wred, wred_out)
    line_y.wait(6, 7, 8, 9, 10, 11, 12)
    first, second = scatter.result()
    hid_ref[...] = x_ref[...].astype(F32) + jnp.concatenate([first, second], axis=0)
    gain = gain_ref[0:1, D : 2 * D]
    hid = hid_ref[...]
    b = (hid * normed_rows(hid) * gain).astype(BF)
    ball[dp] = dot(b, perm[...]).astype(BF).reshape(2, 128, D)
    line_b = LineGather(ball, b_send, b_recv)
    line_b.begin()
    scatter.sent()
    scatter2 = LineScatter(keep, give, took, out_z, in_z, s2_send, s2_recv)

    def mlp(t, carry):
        pair = t // 2
        offset = jnp.where(pair == 0, 0, jnp.where(pair == 1, 1, jnp.where(pair == 2, 3, 2)))
        other = lax.rem(t, 2)
        block = lax.rem(z + offset, 4) * 2 + jnp.where(other == 0, core, 1 - core)
        rows = block_rows(block)

        @pl.when(t == 1)
        def _():
            line_b.wait(6)

        @pl.when(t == 2)
        def _():
            line_b.pass_on()
            line_b.second()
            line_b.wait(7, 8, 9, 10)

        @pl.when(t == 5)
        def _():
            line_b.third()

        @pl.when(t == 6)
        def _():
            line_b.wait(11, 12)

        weight = wexp[...].reshape(D, EXP_COLS)
        gu = dot(ball[block].reshape(256, D), weight)
        gate, up = gu[:, :half], gu[:, half:]
        sig = 1.0 / (1.0 + jnp.exp(-gate))
        silu = gate * sig
        act_ref[rows, :] = (silu * up).astype(BF)
        d_act = dot_t(dy_left[block].reshape(256, D // 2), wred[:, 0 : D // 2])
        d_act += dot_t(dy_right[block].reshape(256, D // 2), wred[:, D // 2 :])
        dgu[rows, 0:half] = (d_act * up * (sig * (1.0 + gate * (1.0 - sig)))).astype(BF)
        dgu[rows, half:] = (d_act * silu).astype(BF)
        partial = dot_t(dgu[rows, :], weight).reshape(2, 128, D)

        @pl.when(other == 1)
        def _():
            give[offset] = partial.astype(BF)
            scatter2.give_at(offset)

        @pl.when(other == 0)
        def _():
            keep[offset] = partial

        @pl.when(t == 3)
        def _():
            scatter2.near_right()

        @pl.when(t == 5)
        def _():
            scatter2.near_left()

        return carry

    lax.fori_loop(0, 8, mlp, 0)
    scatter2.far()
    write(act_ref, act_out)
    for side, dy in ((0, dy_left), (1, dy_right)):
        cols = pl.ds(side * (D // 2), D // 2)
        gred_ref[:, :, :, cols] = jnp.concatenate(
            [
                t_dot(act_ref[...], dy[...].reshape(2048, D // 2)).reshape(4, 4, 24, D // 2),
                jnp.zeros((4, 4, 8, D // 2), F32),
            ],
            axis=2,
        ).astype(BF)
    scatter2.last()
    gexp_ref[...] = t_dot(ball[...].reshape(2048, D), dgu[...]).astype(BF).reshape(4, 4, 64, EXP_COLS)
    first, second = scatter2.result()
    d_b = unorder(jnp.concatenate([first, second], axis=0), perm[...])
    hid = hid_ref[...]
    r = normed_rows(hid)
    dgain_ref[...] = jnp.broadcast_to(jnp.sum(d_b * hid * r, axis=0, keepdims=True), (8, D))
    d_hid = dy_own[...].astype(F32) + rms_back(hid, r, d_b * gain)
    dhid_ref[...] = d_hid
    datt[dp] = d_hid.astype(BF).reshape(2, 128, D)
    line_d = LineGather(datt, d_send, d_recv)
    line_d.begin()

    def back(t, carry):
        pair = t // 2
        offset = jnp.where(pair == 0, 0, jnp.where(pair == 1, 1, jnp.where(pair == 2, 3, 2)))
        block = lax.rem(z + offset, 4) * 2 + jnp.where(lax.rem(t, 2) == 0, core, 1 - core)

        @pl.when(t == 1)
        def _():
            line_d.wait(6)

        @pl.when(t == 2)
        def _():
            line_d.pass_on()
            line_d.second()
            line_d.wait(7, 8, 9, 10)

        @pl.when(t == 6)
        def _():
            line_d.third()
            line_d.wait(11, 12)

        do_ref[block_rows(block), :] = dot_t(datt[block].reshape(256, D), wout).astype(BF)
        return carry

    lax.fori_loop(0, 8, back, 0)
    write(do_ref, do_out)
    gout_ref[...] = t_dot(o_ref[...], datt[...].reshape(2048, D)).astype(BF).reshape(4, 4, 16, D)
    for one in (line_y, line_b, line_d, plane_e, plane_r, scatter2):
        one.sent()
    for copy in outs:
        copy.wait()


def core(*args):
    sh = jax.ShapeDtypeStruct
    held = [
        ((2048, 256), BF),
        ((2048, 128), F32),
        ((2048, FF // 8), BF),
        ((2048, 256), BF),
        ((FF // 8, D), BF),
    ]
    o, lse, act, d_o, wred = (sh(*one) for one in held)
    return pl.pallas_call(
        core_kernel,
        out_shape=(
            o,
            lse,
            sh((256, D), F32),
            sh((256, D), F32),
            act,
            d_o,
            sh((4, 4, RED_ROWS, D), BF),
            sh((4, 4, 64, EXP_COLS), BF),
            sh((4, 4, 16, D), BF),
            sh((8, D), F32),
            wred,
        ),
        in_specs=[VMEM] * 10,
        out_specs=[HBM, HBM, VMEM, VMEM, HBM, HBM, VMEM, VMEM, VMEM, VMEM, HBM],
        scratch_shapes=[pltpu.VMEM(*one) for one in held]
        + [
            pltpu.VMEM((2 * BLOCK, 256), F32),
            pltpu.VMEM((2 * BLOCK, 256), BF),
            pltpu.VMEM((4, 4, 64, EXP_COLS), BF),
            pltpu.VMEM((4, 4, RED_ROWS, D), BF),
            pltpu.VMEM((8, 2, 128, D // 2), BF),
            pltpu.VMEM((D, D), BF),
            pltpu.VMEM((8, 2, 128, D), BF),
            pltpu.VMEM((8, 2, 128, D), BF),
            pltpu.VMEM((2048, EXP_COLS), BF),
        ]
        + line_scatter_scratch(128, D)[:5]
        + [pltpu.SemaphoreType.DMA((n,)) for n in (12, 12, 12, 12, 13, 13, 10, 10, 13, 13, 10, 10, 13, 13, 5)],
        compiler_params=pltpu.CompilerParams(
            collective_id=2, has_side_effects=True, vmem_limit_bytes=60 * 2**20
        ),
        name="core",
    )(*args)


def attend_back_block(
    i, q_ref, k_ref, v_ref, o_ref, lse_ref, do_ref,
    dq_ref, dk_ref, dv_ref, qs, dos, dqa,
):
    rows = block_rows(i)
    lane = lax.broadcasted_iota(jnp.int32, (BLOCK, HD), 1)
    for h in range(2):
        part = slice(h * BLOCK, (h + 1) * BLOCK)
        cols = slice(h * HD, (h + 1) * HD)
        qs[part, 0:HD] = q_ref[rows, cols]
        extra = q_ref[rows, 2 * HD :].astype(F32)
        for k, term in enumerate(in_three(lse_ref[rows, h : h + 1])):
            extra = jnp.where(lane == 4 + k, -term, extra)
        qs[part, HD:] = extra.astype(BF)
        d = do_ref[rows, cols]
        dos[part, 0:HD] = d
        inner = jnp.sum(d.astype(F32) * o_ref[rows, cols].astype(F32), axis=1, keepdims=True)
        extra = jnp.zeros((BLOCK, HD), F32)
        for k, term in enumerate(in_three(inner)):
            extra = jnp.where(lane == k, -term, extra)
        dos[part, HD:] = extra.astype(BF)

    def step(kr, diagonal):
        p = jnp.exp2(dot_t(k_ref[kr, :], qs[...]) * SCORE)
        if diagonal:
            index = lax.broadcasted_iota(jnp.int32, (BLOCK, 2 * BLOCK), 0)
            query = lax.broadcasted_iota(jnp.int32, (BLOCK, 2 * BLOCK), 1) & (BLOCK - 1)
            p = jnp.where(index <= query, p, 0.0)
        ds = (p * dot_t(v_ref[kr, :], dos[...])).astype(BF)
        dv_ref[kr, :] += dot(p.astype(BF), dos[:, 0:HD])
        dk_ref[kr, :] += dot(ds, qs[:, 0:HD])
        dq = t_dot(ds, k_ref[kr, 0:HD])
        if diagonal:
            dqa[...] = dq
        else:
            dqa[...] += dq

    step(rows, True)

    def wide(j, carry):
        step(wide_rows(j), False)
        return carry

    def narrow(j, carry):
        step(block_rows(j), False)
        return carry

    lax.fori_loop(0, i // 2, wide, 0)
    lax.fori_loop(i // 2 * 2, i, narrow, 0)
    for h in range(2):
        dq_ref[rows, h * HD : (h + 1) * HD] = dqa[h * BLOCK : (h + 1) * BLOCK, :] * HD**-0.5


def attention_back_kernel(
    q_ref, k_ref, v_ref, o_ref, lse_ref, do_ref,
    act_ref, wred_ref, hid_ref, pred_ref, pexp_ref, pout_ref,
    dq_ref, dk_ref, dv_ref, y_ref, gred_ref, gexp_ref, gout_ref,
    qs, dos, dqa, *rest,
):
    z, core, x, y = place()
    line_bufs, rest = rest[:7], rest[7:]
    planes = [
        PlaneScatter(part, *rest[5 * n : 5 * n + 5]) for n, part in enumerate((pred_ref, pexp_ref, pout_ref))
    ]
    scatter = LineScatter(*line_bufs)
    keep, give = line_bufs[0], line_bufs[1]
    greet(line_peers() + plane_peers())
    meet(line_peers() + plane_peers())
    for plane in planes:
        plane.begin()
    for offset in (2, 1, 3, 0):
        chip = lax.rem(z + offset, 4) * 2
        give[offset] = (
            dot(act_ref[block_rows(chip + 1 - core), :], wred_ref[...]).astype(BF).reshape(2, 128, D)
        )
        scatter.give(offset)
        keep[offset] = dot(act_ref[block_rows(chip + core), :], wred_ref[...]).reshape(2, 128, D)
    scatter.far()
    scatter.near()
    dk_ref[...] = jnp.zeros_like(dk_ref)
    dv_ref[...] = jnp.zeros_like(dv_ref)

    def block(t, carry):
        attend_back_block(
            7 - t, q_ref, k_ref, v_ref, o_ref, lse_ref, do_ref,
            dq_ref, dk_ref, dv_ref, qs, dos, dqa,
        )

        @pl.when(t == 0)
        def _():
            scatter.last()

        @pl.when(t == 2)
        def _():
            for plane in planes:
                plane.pass_on()

        return carry

    lax.fori_loop(0, 8, block, 0)
    dk_ref[...] *= HD**-0.5
    first, second = scatter.result()
    y_ref[...] = (hid_ref[...] + jnp.concatenate([first, second], axis=0)).astype(BF)
    for plane, out in zip(planes, (gred_ref, gexp_ref, gout_ref)):
        plane.end(out)
        plane.sent()
    scatter.sent()


def attention_back(*args):
    sh = jax.ShapeDtypeStruct
    return pl.pallas_call(
        attention_back_kernel,
        out_shape=(
            sh((2048, 256), F32),
            sh((2048, 128), F32),
            sh((2048, 128), F32),
            sh((256, D), BF),
            sh((RED_ROWS, D), F32),
            sh((64, EXP_COLS), F32),
            sh((16, D), F32),
        ),
        in_specs=[VMEM] * 12,
        out_specs=[VMEM] * 7,
        scratch_shapes=[
            pltpu.VMEM((2 * BLOCK, 256), BF),
            pltpu.VMEM((2 * BLOCK, 256), BF),
            pltpu.VMEM((2 * BLOCK, HD), F32),
        ]
        + line_scatter_scratch(128, D)
        + plane_scatter_scratch(RED_ROWS, D)
        + plane_scatter_scratch(64, EXP_COLS)
        + plane_scatter_scratch(16, D),
        compiler_params=pltpu.CompilerParams(
            collective_id=4, has_side_effects=True, vmem_limit_bytes=60 * 2**20
        ),
        name="attention_back",
    )(*args)


def from_received(got, gin, gexp):
    col = 0
    for ref, start, width in (
        (gin, 0, 256),
        (gin, H * HD, 128),
        (gin, (H + KV) * HD, 128),
        (gexp, 0, 384),
        (gexp, FF, 384),
    ):
        for j in range(8):
            ref[:, start + j * width : start + (j + 1) * width] = got[j, :, col : col + width]
        col += width


def last_kernel(
    dq_ref, dk_ref, dv_ref, raw_ref, table_ref, gain_ref, a_ref, win_ref, x_ref, dhid_ref, dmid_ref, gexp_ref,
    dx_ref, gin_out, gexp_out, dgain_ref,
    perm, dqkv, parts, gin, csend, cgot, gsum, gdp, gx, gy,
    keep, give, took, out_z, in_z, s_send, s_recv,
    got1, between, got2, p_send, p_recv, c_send, c_recv, g_send, g_recv,
):
    z, core, x, y = place()
    dp = lax.axis_index("dp")
    peers = dp_peers()
    greet(peers + plane_peers())
    meet(peers + plane_peers())
    scatter = LineScatter(keep, give, took, out_z, in_z, s_send, s_recv)
    plane = PlaneScatter(parts, got1, between, got2, p_send, p_recv)
    gsum[...] = jnp.zeros_like(gsum)

    def block(b):
        rows = block_rows(b)
        cos, sin = both_tables(table_ref[rows, :])
        for part in range(3):
            cols = slice(part * HD, (part + 1) * HD)
            u = raw_ref[rows, cols]
            d = dq_ref[rows, cols] if part < 2 else dk_ref[rows, :]
            start = 2 * D + (HD if part == 2 else 0)
            gain = gain_ref[0:1, start : start + HD]
            d = d * cos + pltpu.roll(d * sin, HD // 2, 1)
            r = normed_rows(u)
            row = 16 + part // 2
            gsum[row : row + 1, :] += jnp.sum(d * u * r, axis=0, keepdims=True)
            dqkv[rows, cols] = rms_back(u, r, d * gain).astype(BF)
        dqkv[rows, 384:512] = dv_ref[rows, :].astype(BF)
        return dot_t(dqkv[rows, :], win_ref[...]).reshape(2, 128, D)

    for offset in (2, 1, 3, 0):
        chip = lax.rem(z + offset, 4) * 2
        give[offset] = block(chip + 1 - core).astype(BF)
        scatter.give(offset)
        keep[offset] = block(chip + core)
    scatter.far()
    scatter.near()
    first = jnp.where(lax.broadcasted_iota(jnp.int32, (8, 128), 0) == 0, 1.0, 0.0)
    column = lax.dot_general(
        gain_ref[8:16, 0:D],
        first,
        (((0,), (0,)), ((), ())),
        precision=lax.Precision.HIGHEST,
        preferred_element_type=F32,
    )[:, 0:1]
    grad = t_dot(a_ref[...].reshape(2048, D), dqkv[...]) * column
    parts[...] = grad.astype(BF).reshape(4, 4, 64, IN_COLS)
    plane.begin()
    fill_order(perm)
    scatter.last()
    plane.pass_on()
    first, second = scatter.result()
    d_a = unorder(jnp.concatenate([first, second], axis=0), perm[...])
    values = x_ref[...].astype(F32)
    r = normed_rows(values)
    dx_ref[...] = dhid_ref[...] + rms_back(values, r, d_a)
    d_in = jnp.sum(d_a * values * r, axis=0, keepdims=True) * (1.0 / gain_ref[0:1, 0:D])
    for k in range(8):
        gsum[k : k + 1, :] = d_in[:, k * 128 : (k + 1) * 128]
        gsum[8 + k : 9 + k, :] = dmid_ref[0:1, k * 128 : (k + 1) * 128]
    first_copies = [
        remote(gsum, gdp.at[k - 1], g_send.at[k - 1], g_recv.at[k - 1], peers[k - 1]) for k in range(1, 8)
    ]
    for copy in first_copies:
        copy.start()
    plane.end(gin)
    for d in range(8):
        csend[d, :, 0:IN_COLS] = gin[8 * d : 8 * d + 8, :]
        csend[d, :, IN_COLS:] = gexp_ref[8 * d : 8 * d + 8, :]
    cols = [
        remote(csend.at[lax.rem(dp + k, 8)], cgot.at[dp], c_send.at[k - 1], c_recv.at[k - 1], peers[k - 1])
        for k in range(1, 8)
    ]
    for copy in cols:
        copy.start()
    cgot[dp] = csend[dp]
    for copy in first_copies:
        copy.wait_recv()
    total = gsum[...]
    for k in range(7):
        total += gdp[k]
    gx[0] = total
    x_copies = [
        remote(gx.at[0], gx.at[k], g_send.at[6 + k], g_recv.at[6 + k], device(z, core, x + k, y)) for k in (1, 2, 3)
    ]
    for copy in x_copies:
        copy.start()
    for copy in x_copies:
        copy.wait_recv()
    gy[0] = gx[0] + gx[1] + gx[2] + gx[3]
    y_copies = [
        remote(gy.at[0], gy.at[k], g_send.at[9 + k], g_recv.at[9 + k], device(z, core, x, y + k)) for k in (1, 2, 3)
    ]
    for copy in y_copies:
        copy.start()
    for copy in cols:
        copy.wait_recv()
    from_received(cgot, gin_out, gexp_out)
    for copy in y_copies:
        copy.wait_recv()
    dgain_ref[...] = gy[0] + gy[1] + gy[2] + gy[3]
    for copy in first_copies + x_copies + y_copies + cols:
        copy.wait_send()
    scatter.sent()
    plane.sent()


def last(*args):
    sh = jax.ShapeDtypeStruct
    return pl.pallas_call(
        last_kernel,
        out_shape=(sh((256, D), F32), sh((8, 4096), F32), sh((8, 2 * FF), F32), sh((24, 128), F32)),
        in_specs=[VMEM] * 12,
        out_specs=[VMEM] * 4,
        scratch_shapes=[
            pltpu.VMEM((D, D), BF),
            pltpu.VMEM((2048, IN_COLS), BF),
            pltpu.VMEM((4, 4, 64, IN_COLS), BF),
            pltpu.VMEM((64, IN_COLS), F32),
            pltpu.VMEM((8, 8, IN_COLS + EXP_COLS), F32),
            pltpu.VMEM((8, 8, IN_COLS + EXP_COLS), F32),
            pltpu.VMEM((24, 128), F32),
            pltpu.VMEM((7, 24, 128), F32),
            pltpu.VMEM((4, 24, 128), F32),
            pltpu.VMEM((4, 24, 128), F32),
        ]
        + line_scatter_scratch(128, D)
        + plane_scatter_scratch(64, IN_COLS)
        + [pltpu.SemaphoreType.DMA((n,)) for n in (7, 7, 13, 13)],
        compiler_params=pltpu.CompilerParams(
            collective_id=5, has_side_effects=True, vmem_limit_bytes=60 * 2**20
        ),
        name="last",
    )(*args)


def update_kernel(*refs):
    weights, grads, firsts, seconds, news, means, squares = (refs[5 * n : 5 * n + 5] for n in range(7))
    for k in range(5):
        rate, decay = (gain_rate, 0.0) if k == 4 else (matrix_rate, matrix_decay)
        grad = grads[k][0 : weights[k].shape[0], :]
        news[k][...], means[k][...], squares[k][...] = adam_step(
            weights[k][...], grad, firsts[k][...], seconds[k][...], rate, decay
        )


def update(weights, grads, firsts, seconds):
    like = tuple(jax.ShapeDtypeStruct(w.shape, F32) for w in weights)
    return pl.pallas_call(
        update_kernel,
        out_shape=like * 3,
        in_specs=[VMEM] * 20,
        out_specs=[VMEM] * 15,
        compiler_params=pltpu.CompilerParams(vmem_limit_bytes=40 * 2**20),
        name="update",
    )(*weights, *grads, *firsts, *seconds)


def body(
    tokens,
    cotangent,
    lengths,
    weight_input,
    weight_output,
    weight_expand,
    weight_reduce,
    gains,
    first_input,
    first_output,
    first_expand,
    first_reduce,
    first_gains,
    second_input,
    second_output,
    second_expand,
    second_reduce,
    second_gains,
):
    a, raw, q, k, v, table, win, wout, dy_left, wexp, gain = front(
        tokens[0],
        weight_input,
        weight_expand,
        gains[None],
        rope_rates(),
        weight_output,
        cotangent[0],
        lengths,
    )
    o, lse, hid, d_hid, act, d_o, part_red, part_exp, part_out, d_gain_mid, wred = core(
        q, k, v, tokens[0], wout, wexp, weight_reduce, cotangent[0], dy_left, gain
    )
    dq, dk, dv, block_out, grad_reduce, sum_exp, grad_output = attention_back(
        q, k, v, o, lse, d_o, act, wred, hid, part_red, part_exp, part_out
    )
    input_grad, grad_input, grad_expand, grad_gains = last(
        dq, dk, dv, raw, table, gain, a, win, tokens[0], d_hid, d_gain_mid, sum_exp
    )
    own = gains.shape[0]
    index = lax.axis_index("dp") * lax.axis_size("shard") + lax.axis_index("shard")
    grad_gains = lax.dynamic_slice_in_dim(grad_gains.reshape(-1), index * own, own)
    done = update(
        (weight_input, weight_output, weight_expand, weight_reduce, gains[None]),
        (grad_input, grad_output, grad_expand, grad_reduce, grad_gains[None]),
        (first_input, first_output, first_expand, first_reduce, first_gains[None]),
        (second_input, second_output, second_expand, second_reduce, second_gains[None]),
    )
    done = [one[0] if n % 5 == 4 else one for n, one in enumerate(done)]
    return (block_out[None], input_grad[None], *done)


def solution(mesh):
    placed = (
        P("shard", "dp", None),
        P("shard", "dp", None),
        P("shard", None),
        P(("dp", "shard"), None),
        P(("dp", "shard"), None),
        P(("dp", "shard"), None),
        P(("dp", "shard"), None),
        P(("dp", "shard")),
        P(("dp", "shard"), None),
        P(("dp", "shard"), None),
        P(("dp", "shard"), None),
        P(("dp", "shard"), None),
        P(("dp", "shard")),
        P(("dp", "shard"), None),
        P(("dp", "shard"), None),
        P(("dp", "shard"), None),
        P(("dp", "shard"), None),
        P(("dp", "shard")),
    )
    return jax.shard_map(
        body,
        mesh=mesh,
        in_specs=placed,
        out_specs=(
            P("shard", "dp", None),
            P("shard", "dp", None),
            P(("dp", "shard"), None),
            P(("dp", "shard"), None),
            P(("dp", "shard"), None),
            P(("dp", "shard"), None),
            P(("dp", "shard")),
            P(("dp", "shard"), None),
            P(("dp", "shard"), None),
            P(("dp", "shard"), None),
            P(("dp", "shard"), None),
            P(("dp", "shard")),
            P(("dp", "shard"), None),
            P(("dp", "shard"), None),
            P(("dp", "shard"), None),
            P(("dp", "shard"), None),
            P(("dp", "shard")),
        ),
        check_vma=False,
    )
```

```python
import math

import jax
import jax.numpy as jnp
import numpy as np
from jax import lax
from jax.experimental import pallas as pl
from jax.experimental.pallas import tpu as pltpu
from jax.sharding import PartitionSpec as P

D = 1024
H = 16
KV = 8
HD = 128
FF = 3072
STEP = 10


norm_eps = 1e-06
rope_base = 1000000.0
beta_one = 0.9
beta_two = 0.95
adam_eps = 1e-08
matrix_rate = 0.1
gain_rate = 0.5
matrix_decay = 0.1
masked_score = -1e30


def adam_step(weight, grad, first, second, rate, decay):
    first_new = beta_one * first + (1.0 - beta_one) * grad
    second_new = beta_two * second + (1.0 - beta_two) * grad * grad
    fix_one = 1.0 - beta_one**STEP
    fix_two = 1.0 - beta_two**STEP
    direction = first_new / fix_one / (jnp.sqrt(second_new / fix_two) + adam_eps)
    return (weight - rate * (direction + decay * weight), first_new, second_new)


MESH = pl.DeviceIdType.MESH
F32 = jnp.float32
BF = jnp.bfloat16
VMEM = pl.BlockSpec(memory_space=pltpu.VMEM)
HBM = pl.BlockSpec(memory_space=pl.ANY)
SCORE = HD**-0.5 * math.log2(math.e)
BLOCK = 256
BIG = 30000.0
IN_COLS = (H + 2 * KV) * HD // 8
EXP_COLS = 2 * FF // 8
RED_ROWS = 32


def dot(a, b):
    return jnp.dot(a, b, preferred_element_type=F32)


def dot_t(a, b):
    return lax.dot_general(a, b, (((1,), (1,)), ((), ())), preferred_element_type=F32)


def t_dot(a, b):
    return lax.dot_general(a, b, (((0,), (0,)), ((), ())), preferred_element_type=F32)


def in_three(values):
    high = values.astype(BF)
    rest = values - high.astype(F32)
    middle = rest.astype(BF)
    return high.astype(F32), middle.astype(F32), (rest - middle.astype(F32)).astype(BF).astype(F32)


def block_rows(i):
    return pl.ds(pl.multiple_of(i * BLOCK, BLOCK), BLOCK)


def wide_rows(i):
    return pl.ds(pl.multiple_of(i * 2 * BLOCK, 2 * BLOCK), 2 * BLOCK)


def chip_rows(i):
    return pl.ds(pl.multiple_of(i * 2 * BLOCK, 2 * BLOCK), 2 * BLOCK)


def place():
    dp = lax.axis_index("dp")
    shard = lax.axis_index("shard")
    return dp // 2, lax.rem(dp, 2), shard // 4, lax.rem(shard, 4)


def device(z, core, x, y):
    return (lax.rem(z, 4) * 2 + core, lax.rem(x, 4) * 4 + lax.rem(y, 4))


def line_peers():
    z, core, x, y = place()
    return [device(z, 1 - core, x, y), device(z + 1, core, x, y), device(z + 3, core, x, y)]


def plane_peers():
    z, core, x, y = place()
    return [device(z, core, x + k, y) for k in (1, 2, 3)] + [
        device(z, core, x, y + k) for k in (1, 2, 3)
    ]


def dp_peers():
    dp = lax.axis_index("dp")
    shard = lax.axis_index("shard")
    return [(lax.rem(dp + k, 8), shard) for k in range(1, 8)]


def greet(peers):
    for peer in peers:
        pl.semaphore_signal(
            pltpu.get_barrier_semaphore(), inc=1, device_id=peer, device_id_type=MESH
        )


def meet(peers):
    pl.semaphore_wait(pltpu.get_barrier_semaphore(), len(peers))


def remote(src, dst, send, recv, peer):
    return pltpu.make_async_remote_copy(
        src_ref=src, dst_ref=dst, send_sem=send, recv_sem=recv, device_id=peer, device_id_type=MESH
    )


class LineGather:
    sems = 13

    def __init__(self, buf, send, recv):
        z, core, x, y = place()
        me, right, far, left = (lax.rem(z + k, 4) * 2 + core for k in range(4))
        to_right, to_left = device(z + 1, core, x, y), device(z + 3, core, x, y)
        sibling = device(z, 1 - core, x, y)
        plan = [
            (me, 0, to_right),
            (me, 1, to_right),
            (left, 0, to_right),
            (me, 1, to_left),
            (me, 0, to_left),
            (right, 1, to_left),
            (me, None, sibling),
            (left, 0, sibling),
            (right, 1, sibling),
            (left, 1, sibling),
            (right, 0, sibling),
            (far, 0, sibling),
            (far, 1, sibling),
        ]
        self.copies = []
        for k, (slot, half, peer) in enumerate(plan):
            ref = buf.at[slot] if half is None else buf.at[slot, half]
            self.copies.append(remote(ref, ref, send.at[k], recv.at[k], peer))

    def start(self, *which):
        for k in which:
            self.copies[k].start()

    def wait(self, *which):
        for k in which:
            self.copies[k].wait_recv()

    def begin(self):
        self.start(6, 0, 3, 1, 4)

    def pass_on(self):
        self.wait(0)
        self.start(2, 7)
        self.wait(3)
        self.start(5, 8)

    def second(self):
        self.wait(1)
        self.start(9)
        self.wait(4)
        self.start(10)

    def third(self):
        self.wait(2)
        self.start(11)
        self.wait(5)
        self.start(12)

    def sent(self):
        for copy in self.copies:
            copy.wait_send()


class PlaneGather:
    sems = 12

    def __init__(self, buf, send, recv):
        z, core, x, y = place()
        half = buf.shape[3] // 2
        low, high = pl.ds(0, half), pl.ds(half, half)
        self.copies = []
        refs = (
            (buf.at[x, y, :, low], 0),
            (buf.at[x, y, :, high], 1),
            (buf.at[:, y, :, low], 1),
            (buf.at[x, :, :, high], 0),
        )
        k = 0
        for ref, along_y in refs:
            for step in (1, 2, 3):
                peer = device(z, core, x, y + step) if along_y else device(z, core, x + step, y)
                self.copies.append(remote(ref, ref, send.at[k], recv.at[k], peer))
                k += 1

    def begin(self):
        for k in (0, 3, 1, 4, 2, 5):
            self.copies[k].start()

    def pass_on(self):
        for k in (0, 1, 2):
            self.copies[k].wait_recv()
        for k in (6, 7, 8):
            self.copies[k].start()
        for k in (3, 4, 5):
            self.copies[k].wait_recv()
        for k in (9, 10, 11):
            self.copies[k].start()

    def end(self):
        for k in range(6, 12):
            self.copies[k].wait_recv()

    def sent(self):
        for copy in self.copies:
            copy.wait_send()


class PlaneScatter:
    sems = 12

    def __init__(self, parts, got1, mid, got2, send, recv):
        z, core, x, y = place()
        self.parts, self.got1, self.mid, self.got2 = parts, got1, mid, got2
        half = parts.shape[3] // 2
        self.cols = (pl.ds(0, half), pl.ds(half, half))
        self.x, self.y = x, y
        self.copies = []
        k = 0
        for side in (0, 1):
            for step in (1, 2, 3):
                if side == 0:
                    ref = parts.at[:, lax.rem(y + step, 4), :, self.cols[0]]
                    peer = device(z, core, x, y + step)
                else:
                    ref = parts.at[lax.rem(x + step, 4), :, :, self.cols[1]]
                    peer = device(z, core, x + step, y)
                self.copies.append(remote(ref, got1.at[side, step - 1], send.at[k], recv.at[k], peer))
                k += 1
        for side in (0, 1):
            for step in (1, 2, 3):
                if side == 0:
                    ref = mid.at[0, lax.rem(x + step, 4)]
                    peer = device(z, core, x + step, y)
                else:
                    ref = mid.at[1, lax.rem(y + step, 4)]
                    peer = device(z, core, x, y + step)
                self.copies.append(remote(ref, got2.at[side, step - 1], send.at[k], recv.at[k], peer))
                k += 1

    def begin(self):
        for k in (0, 3, 1, 4, 2, 5):
            self.copies[k].start()

    def pass_on(self):
        for side in (0, 1):
            for k in range(3 * side, 3 * side + 3):
                self.copies[k].wait_recv()
            for j in range(4):
                if side == 0:
                    own = self.parts[j, self.y, :, self.cols[0]]
                else:
                    own = self.parts[self.x, j, :, self.cols[1]]
                total = own.astype(F32)
                for k in range(3):
                    total += self.got1[side, k, j].astype(F32)
                self.mid[side, j] = total.astype(BF)
            for k in range(6 + 3 * side, 9 + 3 * side):
                self.copies[k].start()

    def end(self, out):
        for side in (0, 1):
            for k in range(6 + 3 * side, 9 + 3 * side):
                self.copies[k].wait_recv()
            total = self.mid[side, self.x if side == 0 else self.y].astype(F32)
            for k in range(3):
                total += self.got2[side, k].astype(F32)
            out[:, self.cols[side]] = total

    def sent(self):
        for copy in self.copies:
            copy.wait_send()


def plane_scatter_scratch(rows, width):
    half = width // 2
    return [
        pltpu.VMEM((2, 3, 4, rows, half), BF),
        pltpu.VMEM((2, 4, rows, half), BF),
        pltpu.VMEM((2, 3, rows, half), BF),
        pltpu.SemaphoreType.DMA((12,)),
        pltpu.SemaphoreType.DMA((12,)),
    ]


class LineScatter:
    def __init__(self, parts, took, out_z, in_z, send, recv, kept=None):
        z, core, x, y = place()
        self.parts, self.kept, self.took, self.out_z, self.in_z = parts, kept, took, out_z, in_z
        to_right, to_left = device(z + 1, core, x, y), device(z + 3, core, x, y)
        sibling = device(z, 1 - core, x, y)
        self.exchange = lambda k: remote(parts.at[k, 0], took.at[k], send.at[k], recv.at[k], sibling)
        self.swap = [self.exchange(k) for k in range(4)]
        self.copies = [
            remote(
                out_z.at[k], in_z.at[k], send.at[4 + k], recv.at[4 + k], to_right if k < 3 else to_left
            )
            for k in range(6)
        ]

    def give(self, offset):
        self.swap[offset].start()

    def give_at(self, offset):
        self.exchange(offset).start()

    def take(self, offset):
        self.swap[offset].wait_recv()

    def half(self, offset, part):
        own = self.parts[offset, 1, part] if self.kept is None else self.kept[offset, part]
        return own.astype(F32) + self.took[offset, part].astype(F32)

    def push(self, k, value):
        self.out_z[k] = value.astype(BF)
        self.copies[k].start()

    def far(self):
        self.take(2)
        self.push(0, self.half(2, 0))
        self.push(3, self.half(2, 1))

    def near_right(self):
        self.take(1)
        self.push(1, self.half(1, 1))

    def near_left(self):
        self.take(3)
        self.push(4, self.half(3, 0))

    def near(self):
        self.near_right()
        self.near_left()

    def last_right(self):
        self.copies[0].wait_recv()
        self.push(2, self.half(1, 0) + self.in_z[0].astype(F32))

    def last_left(self):
        self.copies[3].wait_recv()
        self.push(5, self.half(3, 1) + self.in_z[3].astype(F32))

    def last(self):
        self.last_right()
        self.last_left()

    def result(self):
        self.take(0)
        self.copies[1].wait_recv()
        self.copies[4].wait_recv()
        self.copies[2].wait_recv()
        first = self.half(0, 0) + self.in_z[4].astype(F32) + self.in_z[2].astype(F32)
        self.copies[5].wait_recv()
        second = self.half(0, 1) + self.in_z[1].astype(F32) + self.in_z[5].astype(F32)
        return first, second

    def sent(self):
        for copy in self.swap + self.copies:
            copy.wait_send()


def line_scatter_scratch(rows, width):
    return [
        pltpu.VMEM((4, 2, 2, rows, width), BF),
        pltpu.VMEM((4, 2, rows, width), BF),
        pltpu.VMEM((6, rows, width), BF),
        pltpu.VMEM((6, rows, width), BF),
        pltpu.SemaphoreType.DMA((10,)),
        pltpu.SemaphoreType.DMA((10,)),
    ]


def to_send(w_in, gains, out):
    col = 0
    for ref, start, width in ((w_in, 0, 256), (w_in, H * HD, 128), (w_in, (H + KV) * HD, 128)):
        for j in range(8):
            out[j, :, col : col + width] = ref[:, start + j * width : start + (j + 1) * width]
        col += width
    out[:, :, col : col + 128] = jnp.zeros((8, 8, 128), F32)
    for j in range(8):
        out[j, 0:1, col : col + 18] = gains[...]


def spread_gains(gbuf):
    wide = 128 * 18
    held = gbuf[:, :, :, 0:128].reshape(128, 128)
    n = lax.broadcasted_iota(jnp.int32, (128, wide), 1)
    r = lax.broadcasted_iota(jnp.int32, (128, wide), 0)
    nf = n.astype(F32)
    within = nf - 18.0 * jnp.floor((nf + 0.5) * (1.0 / 18.0))
    pick = jnp.where(within == r.astype(F32), 1.0, 0.0)
    spread = jnp.dot(held, pick, precision=lax.Precision.HIGHEST, preferred_element_type=F32)
    first = ((r & 7) * 16 + (r >> 3)) * 18
    return jnp.sum(jnp.where((n >= first) & (n < first + 18), spread, 0.0), axis=0, keepdims=True)


def fill_order(perm):
    def block(i, carry):
        n = lax.broadcasted_iota(jnp.int32, (128, D), 0)
        k = lax.broadcasted_iota(jnp.int32, (128, D), 1)
        goal = (n >> 3) * 64 + i * 8 + (n & 7)
        perm[pl.ds(pl.multiple_of(i * 128, 128), 128), :] = jnp.where(k == goal, 1.0, 0.0).astype(BF)
        return carry

    lax.fori_loop(0, 8, block, 0)


def normed_rows(values):
    return lax.rsqrt(jnp.mean(values * values, axis=-1, keepdims=True) + norm_eps)


def token_tables(block, lengths, freq, table, q_ref, k_ref, v_ref):
    rows = block_rows(block)
    end0 = lengths[0, 0]
    end1 = end0 + lengths[0, 1]
    end2 = end1 + lengths[0, 2]
    token = block * BLOCK + lax.broadcasted_iota(jnp.int32, (BLOCK, HD), 0)
    lane = lax.broadcasted_iota(jnp.int32, (BLOCK, HD), 1)
    start = jnp.where(token >= end2, end2, jnp.where(token >= end1, end1, jnp.where(token >= end0, end0, 0)))
    angle = (token - start).astype(F32) * freq[0:1, :]
    table[rows, :] = jnp.sin(angle + jnp.where(lane < HD // 2, math.pi / 2, 0.0))
    one = lambda test: jnp.where(test, 1, 0)
    segment = one(token >= end0) + one(token >= end1) + one(token >= end2)
    same = segment == lane
    q_ref[rows, 256:384] = jnp.where(lane < 4, jnp.where(same, 0.0, -BIG), 0.0).astype(BF)
    k_ref[rows, 128:256] = jnp.where(lane < 4, jnp.where(same, 1.0, 0.0), jnp.where(lane < 7, 1.0, 0.0)).astype(BF)
    v_ref[rows, 128:256] = jnp.where(lane < 3, 1.0, 0.0).astype(BF)


def both_tables(table):
    lane = lax.broadcasted_iota(jnp.int32, table.shape, 1)
    other = pltpu.roll(table, HD // 2, 1)
    return jnp.where(lane < HD // 2, table, other), jnp.where(lane < HD // 2, -other, table)


def front_kernel(
    x_ref, w_in_ref, w_exp_ref, gains_ref, freq_ref, w_out_ref, dy_ref, lengths,
    a_out, raw_out, q_out, k_out, v_out, table_out, win_out, wout_out, dy_out, wexp_ref, gain_ref,
    xall, raw, q_ref, k_ref, v_ref, table, win_ref, wout_all, dy_all,
    wsend, wgot, esend, egot, gbuf, perm, weight,
    line_send, line_recv, cols_send, cols_recv, e_send, e_recv, win_send, win_recv, g_send, g_recv,
    o_send, o_recv, dy_send, dy_recv, out_sem, w_sem,
):
    z, core, x, y = place()
    dp = lax.axis_index("dp")
    peers = dp_peers()
    greet(peers + plane_peers())
    to_send(w_in_ref, gains_ref, wsend)
    wout_all[x, y] = w_out_ref[...].astype(BF)
    dy_all[dp] = dy_ref[:, 0 : D // 2].reshape(2, 128, D // 2)
    fill_order(perm)
    values = x_ref[...].astype(F32)
    normed = (values * normed_rows(values)).astype(BF)
    xall[dp] = dot(normed, perm[...]).astype(BF).reshape(2, 128, D)
    meet(peers + plane_peers())

    def exchange(src, dst, send, recv):
        copies = [
            remote(src.at[lax.rem(dp + k, 8)], dst.at[dp], send.at[k - 1], recv.at[k - 1], peers[k - 1])
            for k in range(1, 8)
        ]
        for copy in copies:
            copy.start()
        return copies

    cols = exchange(wsend, wgot, cols_send, cols_recv)
    line = LineGather(xall, line_send, line_recv)
    line.begin()
    wgot[dp] = wsend[dp]
    for j in range(8):
        for part in range(2):
            start = part * FF + j * 384
            esend[j, :, part * 384 : (part + 1) * 384] = w_exp_ref[:, start : start + 384]
    for copy in cols:
        copy.wait_recv()
    win_ref[x, y] = wgot[:, :, 0:IN_COLS].reshape(64, IN_COLS).astype(BF)
    own_gains = wgot[:, 0, IN_COLS:]
    gbuf[x, y, :, 0:128] = own_gains
    gbuf[x, y, :, 128:256] = own_gains
    plane_g = PlaneGather(gbuf, g_send, g_recv)
    plane_w = PlaneGather(win_ref, win_send, win_recv)
    plane_g.begin()
    plane_w.begin()
    ecols = exchange(esend, egot, e_send, e_recv)
    egot[dp] = esend[dp]

    def tables(block, carry):
        token_tables(block, lengths, freq_ref, table, q_ref, k_ref, v_ref)
        return carry

    plane_g.pass_on()
    plane_w.pass_on()
    lax.fori_loop(0, 4, tables, 0)
    line.pass_on()
    plane_g.end()
    gains = spread_gains(gbuf)
    gain_ref[0:8, :] = jnp.broadcast_to(gains, (8, 2304))
    moved = jnp.zeros((8, D), F32)
    for term in in_three(gain_ref[0:8, 0:D]):
        moved += dot(term.astype(BF), perm[...])
    gain_ref[8:16, 0:D] = moved
    first = jnp.where(lax.broadcasted_iota(jnp.int32, (8, 128), 0) == 0, 1.0, 0.0)
    column = lax.dot_general(
        moved, first, (((0,), (0,)), ((), ())), precision=lax.Precision.HIGHEST, preferred_element_type=F32
    )[:, 0:1]
    plane_w.end()
    plane_o = PlaneGather(wout_all, o_send, o_recv)
    plane_o.begin()
    weight[...] = (win_ref[...].reshape(D, IN_COLS).astype(F32) * column).astype(BF)
    keep_weight = pltpu.make_async_copy(weight, win_out, w_sem.at[0])
    keep_weight.start()
    lax.fori_loop(4, 8, tables, 0)

    def chip(offset):
        chip_at = lax.rem(z + offset, 4)
        rows = chip_rows(chip_at)
        qkv = dot(xall[pl.ds(chip_at * 2, 2)].reshape(512, D), weight[...])
        raw[rows, :] = qkv[:, 0:384]
        cos, sin = both_tables(table[rows, :])
        for part in range(3):
            u = qkv[:, part * HD : (part + 1) * HD]
            start = 2 * D + (HD if part == 2 else 0)
            u = u * normed_rows(u) * gain_ref[0:1, start : start + HD]
            u = (u * cos + pltpu.roll(u, HD // 2, 1) * sin).astype(BF)
            if part < 2:
                q_ref[rows, part * HD : (part + 1) * HD] = u
            else:
                k_ref[rows, 0:HD] = u
        v_ref[rows, 0:HD] = qkv[:, 384:512].astype(BF)

    outs = []

    def write(offset):
        chip_at = lax.rem(z + offset, 4)
        rows = pl.ds(pl.multiple_of(chip_at * 512, 512), 512)
        blocks = pl.ds(chip_at * 2, 2)
        pairs = [(xall.at[blocks], a_out.at[blocks])]
        pairs += [
            (ref.at[rows, :], out.at[rows, :])
            for ref, out in ((raw, raw_out), (q_ref, q_out), (k_ref, k_out), (v_ref, v_out), (table, table_out))
        ]
        for n, (src, dst) in enumerate(pairs):
            copy = pltpu.make_async_copy(src, dst, out_sem.at[6 * offset + n])
            copy.start()
            outs.append(copy)

    line.wait(6)
    chip(0)
    write(0)
    line.second()
    line_dy = LineGather(dy_all, dy_send, dy_recv)
    line_dy.begin()
    plane_o.pass_on()
    line.wait(7, 8, 9, 10)

    def near(t, carry):
        chip(1 + 2 * t)
        return carry

    lax.fori_loop(0, 2, near, 0)
    write(1)
    write(3)
    line.third()
    line.wait(11, 12)
    line_dy.pass_on()
    chip(2)
    write(2)
    line_dy.second()
    for copy in ecols:
        copy.wait_recv()
    wexp_ref[...] = egot[...].reshape(64, EXP_COLS).astype(BF)
    plane_o.end()
    line_dy.third()
    line_dy.wait(6, 7, 8, 9, 10, 11, 12)
    for n, (src, dst) in enumerate(((wout_all, wout_out), (dy_all, dy_out))):
        copy = pltpu.make_async_copy(src, dst, w_sem.at[1 + n])
        copy.start()
        outs.append(copy)
    line.sent()
    line_dy.sent()
    plane_o.sent()
    plane_g.sent()
    plane_w.sent()
    for copy in cols + ecols:
        copy.wait_send()
    for copy in [keep_weight] + outs:
        copy.wait()


def front(x, w_in, w_exp, gains, freq, w_out, dy, lengths):
    sh = jax.ShapeDtypeStruct
    held = [
        ((8, 2, 128, D), BF),
        ((2048, 384), F32),
        ((2048, 384), BF),
        ((2048, 256), BF),
        ((2048, 256), BF),
        ((2048, 128), F32),
    ]
    return pl.pallas_call(
        front_kernel,
        out_shape=tuple(sh(*one) for one in held)
        + (
            sh((D, IN_COLS), BF),
            sh((4, 4, 16, D), BF),
            sh((8, 2, 128, D // 2), BF),
            sh((64, EXP_COLS), BF),
            sh((16, 2304), F32),
        ),
        in_specs=[VMEM] * 7 + [pl.BlockSpec(memory_space=pltpu.SMEM)],
        out_specs=[HBM] * 9 + [VMEM] * 2,
        scratch_shapes=[pltpu.VMEM(*one) for one in held]
        + [
            pltpu.VMEM((4, 4, 64, IN_COLS), BF),
            pltpu.VMEM((4, 4, 16, D), BF),
            pltpu.VMEM((8, 2, 128, D // 2), BF),
            pltpu.VMEM((8, 8, IN_COLS + 128), F32),
            pltpu.VMEM((8, 8, IN_COLS + 128), F32),
            pltpu.VMEM((8, 8, EXP_COLS), F32),
            pltpu.VMEM((8, 8, EXP_COLS), F32),
            pltpu.VMEM((4, 4, 8, 256), F32),
            pltpu.VMEM((D, D), BF),
            pltpu.VMEM((D, IN_COLS), BF),
        ]
        + [pltpu.SemaphoreType.DMA((n,)) for n in (13, 13, 7, 7, 7, 7, 12, 12, 12, 12, 12, 12, 13, 13, 24, 3)],
        compiler_params=pltpu.CompilerParams(
            collective_id=1, has_side_effects=True, vmem_limit_bytes=56 * 2**20
        ),
        name="front",
    )(x, w_in, w_exp, gains, freq, w_out, dy, lengths)


def rope_rates():
    half = HD // 2
    rates = np.float32(rope_base) ** (-(2.0 * np.arange(half, dtype=np.float32)) / np.float32(HD))
    return jnp.asarray(np.tile(np.concatenate([rates, rates])[None], (8, 1)), F32)


def attend_block(i, q_ref, k_ref, v_ref, o_ref, lse_ref, acc, qs):
    rows = block_rows(i)
    for h in range(2):
        qs[h * BLOCK : (h + 1) * BLOCK, 0:HD] = q_ref[rows, h * HD : (h + 1) * HD]
        qs[h * BLOCK : (h + 1) * BLOCK, HD:] = q_ref[rows, 2 * HD :]

    query = lax.broadcasted_iota(jnp.int32, (2 * BLOCK, BLOCK), 0) & (BLOCK - 1)
    index = lax.broadcasted_iota(jnp.int32, (2 * BLOCK, BLOCK), 1)
    e = jnp.where(index <= query, jnp.exp2(dot_t(qs[...], k_ref[rows, :]) * SCORE), 0.0)
    acc[...] = dot(e.astype(BF), v_ref[rows, :])

    def step(kr):
        acc[...] += dot(jnp.exp2(dot_t(qs[...], k_ref[kr, :]) * SCORE).astype(BF), v_ref[kr, :])

    def wide(j, carry):
        step(wide_rows(j))
        return carry

    def narrow(j, carry):
        step(block_rows(j))
        return carry

    lax.fori_loop(0, i // 2, wide, 0)
    lax.fori_loop(i // 2 * 2, i, narrow, 0)
    total = acc[:, HD : HD + 1]
    out = acc[:, 0:HD] * (1.0 / total)
    lse = jnp.log2(total) * (1.0 / SCORE)
    for h in range(2):
        part = slice(h * BLOCK, (h + 1) * BLOCK)
        o_ref[rows, h * HD : (h + 1) * HD] = out[part].astype(BF)
        lse_ref[rows, h : h + 1] = lse[part]


def rms_back(h, r, dg):
    return r * dg - h * (r * r * r) * jnp.mean(h * dg, axis=-1, keepdims=True)


def unorder(values, perm):
    high = values.astype(BF)
    low = (values - high.astype(F32)).astype(BF)
    return dot_t(high, perm) + dot_t(low, perm)


def core_kernel(
    q_ref, k_ref, v_ref, x_ref, wout_ref, wexp_own, wred_own, dy_own, dy_left, gain_ref,
    o_out, lse_out, yparts_out, hid_ref, dhid_ref, gred_ref, gexp_ref, dgain_ref,
    o_ref, lse_ref, yparts, act_ref, wred,
    acc, qs, wexp, wred_all, dy_right, perm, ball, dgu,
    parts, took, out_z, in_z,
    e_send, e_recv, r_send, r_recv, y_send, y_recv,
    s1_send, s1_recv, b_send, b_recv, s2_send, s2_recv, out_sem,
):
    z, core, x, y = place()
    dp = lax.axis_index("dp")
    half = FF // 8
    greet(line_peers() + plane_peers())
    wexp[x, y] = wexp_own[...]
    wred_all[x, y] = jnp.concatenate([wred_own[...], jnp.zeros((8, D), F32)], axis=0).astype(BF)
    dy_right[dp] = dy_own[:, D // 2 :].reshape(2, 128, D // 2)
    meet(line_peers() + plane_peers())
    plane_e = PlaneGather(wexp, e_send, e_recv)
    plane_r = PlaneGather(wred_all, r_send, r_recv)
    line_y = LineGather(dy_right, y_send, y_recv)
    line_y.begin()
    plane_e.begin()
    plane_r.begin()
    scatter = LineScatter(parts, took, out_z, in_z, s1_send, s1_recv)
    wout = wout_ref[...].reshape(256, D)
    outs = []

    def write(src, dst):
        copy = pltpu.make_async_copy(src, dst, out_sem.at[len(outs)])
        copy.start()
        outs.append(copy)

    def attend(t, carry):
        pair = t // 2
        offset = jnp.where(pair == 0, 2, jnp.where(pair == 1, 1, jnp.where(pair == 2, 3, 0)))
        second = lax.rem(t, 2)
        block = lax.rem(z + offset, 4) * 2 + jnp.where(second == 1, core, 1 - core)
        attend_block(block, q_ref, k_ref, v_ref, o_ref, lse_ref, acc, qs)
        parts[offset, second] = dot(o_ref[block_rows(block), :], wout).astype(BF).reshape(2, 128, D)

        @pl.when(second == 0)
        def _():
            scatter.give_at(offset)

        @pl.when(t == 1)
        def _():
            scatter.far()
            plane_e.pass_on()
            plane_r.pass_on()
            line_y.pass_on()

        @pl.when(t == 3)
        def _():
            scatter.near_right()

        @pl.when(t == 4)
        def _():
            line_y.second()

        @pl.when(t == 5)
        def _():
            scatter.near_left()

        @pl.when(t == 6)
        def _():
            line_y.third()

        return carry

    lax.fori_loop(0, 8, attend, 0)
    write(o_ref, o_out)
    write(lse_ref, lse_out)
    scatter.last()
    fill_order(perm)
    plane_e.end()
    plane_r.end()
    wred[...] = wred_all[...].astype(F32)[:, :, 0:24, :].reshape(half, D).astype(BF)
    line_y.wait(6, 7, 8, 9, 10, 11, 12)
    first, second = scatter.result()
    hid_ref[...] = x_ref[...].astype(F32) + jnp.concatenate([first, second], axis=0)
    gain = gain_ref[0:1, D : 2 * D]
    hid = hid_ref[...]
    b = (hid * normed_rows(hid) * gain).astype(BF)
    ball[dp] = dot(b, perm[...]).astype(BF).reshape(2, 128, D)
    line_b = LineGather(ball, b_send, b_recv)
    line_b.begin()
    scatter.sent()
    scatter2 = LineScatter(parts, took, out_z, in_z, s2_send, s2_recv)

    def mlp(t, carry):
        offset = jnp.where(t == 0, 0, jnp.where(t == 1, 1, jnp.where(t == 2, 3, 2)))
        chip = lax.rem(z + offset, 4)
        rows = chip_rows(chip)
        both = pl.ds(chip * 2, 2)

        @pl.when(t == 0)
        def _():
            line_b.wait(6)

        @pl.when(t == 1)
        def _():
            line_b.pass_on()
            line_b.second()
            line_b.wait(7, 8, 9, 10)

        @pl.when(t == 3)
        def _():
            line_b.third()
            line_b.wait(11, 12)

        weight = wexp[...].reshape(D, EXP_COLS)
        gu = dot(ball[both].reshape(512, D), weight)
        gate, up = gu[:, :half], gu[:, half:]
        sig = 1.0 / (1.0 + jnp.exp(-gate))
        silu = gate * sig
        act_ref[rows, :] = (silu * up).astype(BF)
        d_act = dot_t(dy_left[both].reshape(512, D // 2), wred[:, 0 : D // 2])
        d_act += dot_t(dy_right[both].reshape(512, D // 2), wred[:, D // 2 :])
        dgu[rows, 0:half] = (d_act * up * (sig * (1.0 + gate * (1.0 - sig)))).astype(BF)
        dgu[rows, half:] = (d_act * silu).astype(BF)
        partial = dot_t(dgu[rows, :], weight).astype(BF).reshape(2, 2, 128, D)
        parts[offset, core] = partial[1]
        parts[offset, 1 - core] = partial[0]
        scatter2.give_at(offset)

        @pl.when(t == 1)
        def _():
            scatter2.near_right()

        @pl.when(t == 2)
        def _():
            scatter2.near_left()

        return carry

    lax.fori_loop(0, 4, mlp, 0)
    scatter2.far()
    for side, dy in ((0, dy_left), (1, dy_right)):
        cols = pl.ds(side * (D // 2), D // 2)
        gred_ref[:, :, :, cols] = jnp.concatenate(
            [
                t_dot(act_ref[...], dy[...].reshape(2048, D // 2)).reshape(4, 4, 24, D // 2),
                jnp.zeros((4, 4, 8, D // 2), F32),
            ],
            axis=2,
        ).astype(BF)

    def outcome(offset, carry):
        chip = lax.rem(z + offset, 4)
        y_part = dot(act_ref[chip_rows(chip), :], wred[...]).astype(BF).reshape(2, 2, 128, D)
        yparts[offset, core] = y_part[1]
        yparts[offset, 1 - core] = y_part[0]
        return carry

    lax.fori_loop(0, 4, outcome, 0)
    write(yparts, yparts_out)
    scatter2.last()
    gexp_ref[...] = t_dot(ball[...].reshape(2048, D), dgu[...]).astype(BF).reshape(4, 4, 64, EXP_COLS)
    first, second = scatter2.result()
    d_b = unorder(jnp.concatenate([first, second], axis=0), perm[...])
    hid = hid_ref[...]
    r = normed_rows(hid)
    dgain_ref[...] = jnp.broadcast_to(jnp.sum(d_b * hid * r, axis=0, keepdims=True), (8, D))
    dhid_ref[...] = dy_own[...].astype(F32) + rms_back(hid, r, d_b * gain)
    for one in (line_y, line_b, plane_e, plane_r, scatter2):
        one.sent()
    for copy in outs:
        copy.wait()


def core(*args):
    sh = jax.ShapeDtypeStruct
    held = [
        ((2048, 256), BF),
        ((2048, 128), F32),
        ((4, 2, 2, 128, D), BF),
    ]
    return pl.pallas_call(
        core_kernel,
        out_shape=tuple(sh(*one) for one in held)
        + (
            sh((256, D), F32),
            sh((256, D), F32),
            sh((4, 4, RED_ROWS, D), BF),
            sh((4, 4, 64, EXP_COLS), BF),
            sh((8, D), F32),
        ),
        in_specs=[VMEM] * 10,
        out_specs=[HBM] * 3 + [VMEM] * 5,
        scratch_shapes=[pltpu.VMEM(*one) for one in held]
        + [
            pltpu.VMEM((2048, FF // 8), BF),
            pltpu.VMEM((FF // 8, D), BF),
            pltpu.VMEM((2 * BLOCK, 256), F32),
            pltpu.VMEM((2 * BLOCK, 256), BF),
            pltpu.VMEM((4, 4, 64, EXP_COLS), BF),
            pltpu.VMEM((4, 4, RED_ROWS, D), BF),
            pltpu.VMEM((8, 2, 128, D // 2), BF),
            pltpu.VMEM((D, D), BF),
            pltpu.VMEM((8, 2, 128, D), BF),
            pltpu.VMEM((2048, EXP_COLS), BF),
        ]
        + line_scatter_scratch(128, D)[:4]
        + [pltpu.SemaphoreType.DMA((n,)) for n in (12, 12, 12, 12, 13, 13, 10, 10, 13, 13, 10, 10, 3)],
        compiler_params=pltpu.CompilerParams(
            collective_id=2, has_side_effects=True, vmem_limit_bytes=60 * 2**20
        ),
        name="core",
    )(*args)


def attend_back_block(
    i, q_ref, k_ref, v_ref, o_ref, lse_ref, do_ref,
    dk_ref, dv_ref, qs, dos, dqa,
):
    rows = block_rows(i)
    lane = lax.broadcasted_iota(jnp.int32, (BLOCK, HD), 1)
    for h in range(2):
        part = slice(h * BLOCK, (h + 1) * BLOCK)
        cols = slice(h * HD, (h + 1) * HD)
        qs[part, 0:HD] = q_ref[rows, cols]
        extra = q_ref[rows, 2 * HD :].astype(F32)
        for k, term in enumerate(in_three(lse_ref[rows, h : h + 1])):
            extra = jnp.where(lane == 4 + k, -term, extra)
        qs[part, HD:] = extra.astype(BF)
        d = do_ref[rows, cols]
        dos[part, 0:HD] = d
        inner = jnp.sum(d.astype(F32) * o_ref[rows, cols].astype(F32), axis=1, keepdims=True)
        extra = jnp.zeros((BLOCK, HD), F32)
        for k, term in enumerate(in_three(inner)):
            extra = jnp.where(lane == k, -term, extra)
        dos[part, HD:] = extra.astype(BF)

    def step(kr, diagonal):
        p = jnp.exp2(dot_t(k_ref[kr, :], qs[...]) * SCORE)
        if diagonal:
            index = lax.broadcasted_iota(jnp.int32, (BLOCK, 2 * BLOCK), 0)
            query = lax.broadcasted_iota(jnp.int32, (BLOCK, 2 * BLOCK), 1) & (BLOCK - 1)
            p = jnp.where(index <= query, p, 0.0)
        ds = (p * dot_t(v_ref[kr, :], dos[...])).astype(BF)
        dv_ref[kr, :] += dot(p.astype(BF), dos[:, 0:HD])
        dk_ref[kr, :] += dot(ds, qs[:, 0:HD])
        dq = t_dot(ds, k_ref[kr, 0:HD])
        if diagonal:
            dqa[...] = dq
        else:
            dqa[...] += dq

    step(rows, True)

    def wide(j, carry):
        step(wide_rows(j), False)
        return carry

    def narrow(j, carry):
        step(block_rows(j), False)
        return carry

    lax.fori_loop(0, i // 2, wide, 0)
    lax.fori_loop(i // 2 * 2, i, narrow, 0)


def from_received(got, out, parts):
    col = 0
    for start, width in parts:
        for j in range(8):
            out[:, start + j * width : start + (j + 1) * width] = got[j, :, col : col + width]
        col += width


def back_kernel(
    q_ref, k_ref, v_ref, o_ref, lse_ref, wout_ref, weight, gain_ref, pred_ref, pexp_ref, dhid, dmid_ref,
    yparts, raw_in, table_in, a_in, hid_in, x_in,
    y_ref, dx_ref, gred_ref, gout_ref, gin_out, gexp_out, dgain_ref,
    raw, table, hid, x_ref,
    qs, dos, dqa, dk_ref, dv_ref, dqkv, acc, parts, pout, perm, datt, do_ref,
    gin, gexp, csend, cgot, esend, egot, gsum, gdp, gx, gy,
    *rest,
):
    z, core, x, y = place()
    dp = lax.axis_index("dp")
    peers = dp_peers()
    greet(peers + plane_peers())
    datt[dp] = dhid[...].astype(BF).reshape(2, 128, D)
    (ykeep, ytook, y_out, y_in, ys, yr), rest = rest[:6], rest[6:]
    (d_parts, took, out_z, in_z, ss, sr), rest = rest[:6], rest[6:]
    planes = [
        PlaneScatter(part, *rest[5 * n : 5 * n + 5])
        for n, part in enumerate((pred_ref, pexp_ref, pout, parts))
    ]
    plane_out, plane_in = planes[2:]
    planes = planes[:2]
    c_send, c_recv, e_send, e_recv, g_send, g_recv, d_send, d_recv, in_sem = rest[20:]
    scatter = LineScatter(d_parts, took, out_z, in_z, ss, sr)
    y_scatter = LineScatter(yparts, ytook, y_out, y_in, ys, yr, ykeep)
    line = LineGather(datt, d_send, d_recv)
    fetched = [
        pltpu.make_async_copy(src, dst, in_sem.at[n])
        for n, (src, dst) in enumerate(
            ((raw_in, raw), (table_in, table), (yparts.at[:, 1], ykeep), (hid_in, hid), (x_in, x_ref))
        )
    ]
    again = pltpu.make_async_copy(a_in, datt, in_sem.at[5])
    wout = wout_ref[...].reshape(256, D)
    meet(peers + plane_peers())
    line.begin()
    for copy in fetched:
        copy.start()
    for plane in planes:
        plane.begin()
    dk_ref[...] = jnp.zeros_like(dk_ref)
    dv_ref[...] = jnp.zeros_like(dv_ref)
    gsum[...] = jnp.zeros_like(gsum)
    fill_order(perm)
    for copy in fetched:
        copy.wait()

    def exchange(src, dst, send, recv):
        return [
            remote(src.at[lax.rem(dp + k, 8)], dst.at[dp], send.at[k - 1], recv.at[k - 1], peers[k - 1])
            for k in range(1, 8)
        ]

    ecols = exchange(esend, egot, e_send, e_recv)

    def through_norm(rows, part, d, tables):
        cos, sin = tables
        cols = slice(part * HD, (part + 1) * HD)
        u = raw[rows, cols]
        start = 2 * D + (HD if part == 2 else 0)
        gain = gain_ref[0:1, start : start + HD]
        d = d * HD**-0.5
        d = d * cos + pltpu.roll(d * sin, HD // 2, 1)
        r = normed_rows(u)
        row = 16 + part // 2
        gsum[row : row + 1, :] += jnp.sum(d * u * r, axis=0, keepdims=True)
        dqkv[rows, cols] = rms_back(u, r, d * gain).astype(BF)

    def block(t, carry):
        pair = t // 2
        chip = lax.rem(z + jnp.where(pair == 0, 0, jnp.where(pair == 1, 1, jnp.where(pair == 2, 3, 2))), 4)
        i = chip * 2 + lax.rem(t, 2)

        @pl.when(t == 0)
        def _():
            line.wait(6)

        @pl.when(t == 2)
        def _():
            line.pass_on()
            line.second()
            line.wait(7, 8, 9, 10)
            for offset in (2, 1, 3, 0):
                y_scatter.give(offset)

        @pl.when(t == 6)
        def _():
            line.third()
            line.wait(11, 12)

        @pl.when(lax.rem(t, 2) == 0)
        def _():
            do_ref[chip_rows(chip), :] = dot_t(datt[pl.ds(chip * 2, 2)].reshape(512, D), wout).astype(BF)

        @pl.when(t == 6)
        def _():
            pout[...] = t_dot(o_ref[...], datt[...].reshape(2048, D)).astype(BF).reshape(4, 4, 16, D)
            plane_out.begin()
            line.sent()
            again.start()

        rows = block_rows(i)
        attend_back_block(i, q_ref, k_ref, v_ref, o_ref, lse_ref, do_ref, dk_ref, dv_ref, qs, dos, dqa)
        tables = both_tables(table[rows, :])
        for part in range(2):
            through_norm(rows, part, dqa[part * BLOCK : (part + 1) * BLOCK, :], tables)

        @pl.when(t == 3)
        def _():
            y_scatter.far()
            y_scatter.near()

        @pl.when(t == 4)
        def _():
            for plane in planes:
                plane.pass_on()

        @pl.when(t == 6)
        def _():
            y_scatter.last()

        @pl.when(t == 7)
        def _():
            planes[1].end(gexp)
            for j in range(8):
                esend[j] = gexp[8 * j : 8 * j + 8, :]
            egot[dp] = esend[dp]
            for copy in ecols:
                copy.start()

        return carry

    lax.fori_loop(0, 8, block, 0)

    def to_input(t, carry):
        offset = jnp.where(t == 0, 2, jnp.where(t == 1, 1, jnp.where(t == 2, 3, 0)))
        rows = chip_rows(lax.rem(z + offset, 4))
        through_norm(rows, 2, dk_ref[rows, :], both_tables(table[rows, :]))
        dqkv[rows, 384:512] = dv_ref[rows, :].astype(BF)
        partial = dot_t(dqkv[rows, :], weight[...]).astype(BF).reshape(2, 2, 128, D)
        d_parts[offset, core] = partial[1]
        d_parts[offset, 1 - core] = partial[0]
        scatter.give_at(offset)

        @pl.when(t == 0)
        def _():
            scatter.far()

        @pl.when(t == 1)
        def _():
            scatter.near_right()

        @pl.when(t == 2)
        def _():
            scatter.near_left()

        return carry

    lax.fori_loop(0, 4, to_input, 0)
    again.wait()
    acc[...] = t_dot(datt[...].reshape(2048, D), dqkv[...])
    first = jnp.where(lax.broadcasted_iota(jnp.int32, (8, 128), 0) == 0, 1.0, 0.0)
    column = lax.dot_general(
        gain_ref[8:16, 0:D],
        first,
        (((0,), (0,)), ((), ())),
        precision=lax.Precision.HIGHEST,
        preferred_element_type=F32,
    )[:, 0:1]
    parts[...] = (acc[...] * column).astype(BF).reshape(4, 4, 64, IN_COLS)
    plane_in.begin()
    inner = jnp.sum(acc[...] * weight[...].astype(F32), axis=1, keepdims=True)
    d_in = jnp.zeros((128, D), F32)
    for term in in_three(jnp.broadcast_to(inner, (D, 128))):
        d_in += lax.dot_general(
            term.astype(BF), perm[...], (((0,), (1,)), ((), ())), preferred_element_type=F32
        )
    d_in = d_in[0:1, :] * (1.0 / gain_ref[0:1, 0:D])
    for k in range(8):
        gsum[k : k + 1, :] = d_in[:, k * 128 : (k + 1) * 128]
        gsum[8 + k : 9 + k, :] = dmid_ref[0:1, k * 128 : (k + 1) * 128]
    dp_copies = [
        remote(gsum, gdp.at[k - 1], g_send.at[k - 1], g_recv.at[k - 1], peers[k - 1]) for k in range(1, 8)
    ]
    for copy in dp_copies:
        copy.start()

    scatter.last()
    plane_out.pass_on()
    first, second = y_scatter.result()
    y_ref[...] = (hid[...] + jnp.concatenate([first, second], axis=0)).astype(BF)
    planes[0].end(gred_ref)
    for copy in ecols:
        copy.wait_recv()
    from_received(egot, gexp_out, ((0, 384), (FF, 384)))
    for copy in dp_copies:
        copy.wait_recv()
    total = gsum[...]
    for k in range(7):
        total += gdp[k]
    gx[0] = total
    x_copies = [
        remote(gx.at[0], gx.at[k], g_send.at[6 + k], g_recv.at[6 + k], device(z, core, x + k, y)) for k in (1, 2, 3)
    ]
    for copy in x_copies:
        copy.start()
    plane_in.pass_on()
    for copy in x_copies:
        copy.wait_recv()
    gy[0] = gx[0] + gx[1] + gx[2] + gx[3]
    y_copies = [
        remote(gy.at[0], gy.at[k], g_send.at[9 + k], g_recv.at[9 + k], device(z, core, x, y + k)) for k in (1, 2, 3)
    ]
    for copy in y_copies:
        copy.start()
    plane_in.end(gin)
    plane_out.end(gout_ref)
    for j in range(8):
        csend[j] = gin[8 * j : 8 * j + 8, :]
    cols = exchange(csend, cgot, c_send, c_recv)
    for copy in cols:
        copy.start()
    cgot[dp] = csend[dp]
    first, second = scatter.result()
    d_a = unorder(jnp.concatenate([first, second], axis=0), perm[...])
    values = x_ref[...].astype(F32)
    dx_ref[...] = dhid[...] + rms_back(values, normed_rows(values), d_a)
    for copy in y_copies:
        copy.wait_recv()
    dgain_ref[...] = gy[0] + gy[1] + gy[2] + gy[3]
    for copy in cols:
        copy.wait_recv()
    from_received(cgot, gin_out, ((0, 256), (H * HD, 128), ((H + KV) * HD, 128)))
    for copy in dp_copies + x_copies + y_copies + cols + ecols:
        copy.wait_send()
    for one in [scatter, y_scatter, plane_in, plane_out] + planes:
        one.sent()


def back(*args):
    sh = jax.ShapeDtypeStruct
    return pl.pallas_call(
        back_kernel,
        out_shape=(
            sh((256, D), BF),
            sh((256, D), F32),
            sh((RED_ROWS, D), F32),
            sh((16, D), F32),
            sh((8, 4096), F32),
            sh((8, 2 * FF), F32),
            sh((24, 128), F32),
        ),
        in_specs=[VMEM] * 12 + [HBM] * 6,
        out_specs=[VMEM] * 7,
        scratch_shapes=[
            pltpu.VMEM((2048, 384), F32),
            pltpu.VMEM((2048, 128), F32),
            pltpu.VMEM((256, D), F32),
            pltpu.VMEM((256, D), BF),
            pltpu.VMEM((2 * BLOCK, 256), BF),
            pltpu.VMEM((2 * BLOCK, 256), BF),
            pltpu.VMEM((2 * BLOCK, HD), F32),
            pltpu.VMEM((2048, HD), F32),
            pltpu.VMEM((2048, HD), F32),
            pltpu.VMEM((2048, IN_COLS), BF),
            pltpu.VMEM((D, IN_COLS), F32),
            pltpu.VMEM((4, 4, 64, IN_COLS), BF),
            pltpu.VMEM((4, 4, 16, D), BF),
            pltpu.VMEM((D, D), BF),
            pltpu.VMEM((8, 2, 128, D), BF),
            pltpu.VMEM((2048, 256), BF),
            pltpu.VMEM((64, IN_COLS), F32),
            pltpu.VMEM((64, EXP_COLS), F32),
            pltpu.VMEM((8, 8, IN_COLS), F32),
            pltpu.VMEM((8, 8, IN_COLS), F32),
            pltpu.VMEM((8, 8, EXP_COLS), F32),
            pltpu.VMEM((8, 8, EXP_COLS), F32),
            pltpu.VMEM((24, 128), F32),
            pltpu.VMEM((7, 24, 128), F32),
            pltpu.VMEM((4, 24, 128), F32),
            pltpu.VMEM((4, 24, 128), F32),
        ]
        + [pltpu.VMEM((4, 2, 128, D), BF)]
        + line_scatter_scratch(128, D)[1:]
        + line_scatter_scratch(128, D)
        + plane_scatter_scratch(RED_ROWS, D)
        + plane_scatter_scratch(64, EXP_COLS)
        + plane_scatter_scratch(16, D)
        + plane_scatter_scratch(64, IN_COLS)
        + [pltpu.SemaphoreType.DMA((n,)) for n in (7, 7, 7, 7, 13, 13, 13, 13, 6)],
        compiler_params=pltpu.CompilerParams(
            collective_id=3, has_side_effects=True, vmem_limit_bytes=62 * 2**20
        ),
        name="back",
    )(*args)


def update_kernel(*refs):
    weights, grads, firsts, seconds, news, means, squares = (refs[5 * n : 5 * n + 5] for n in range(7))
    for k in range(5):
        rate, decay = (gain_rate, 0.0) if k == 4 else (matrix_rate, matrix_decay)
        grad = grads[k][0 : weights[k].shape[0], :]
        news[k][...], means[k][...], squares[k][...] = adam_step(
            weights[k][...], grad, firsts[k][...], seconds[k][...], rate, decay
        )


def update(weights, grads, firsts, seconds):
    like = tuple(jax.ShapeDtypeStruct(w.shape, F32) for w in weights)
    return pl.pallas_call(
        update_kernel,
        out_shape=like * 3,
        in_specs=[VMEM] * 20,
        out_specs=[VMEM] * 15,
        compiler_params=pltpu.CompilerParams(vmem_limit_bytes=40 * 2**20),
        name="update",
    )(*weights, *grads, *firsts, *seconds)


def body(
    tokens,
    cotangent,
    lengths,
    weight_input,
    weight_output,
    weight_expand,
    weight_reduce,
    gains,
    first_input,
    first_output,
    first_expand,
    first_reduce,
    first_gains,
    second_input,
    second_output,
    second_expand,
    second_reduce,
    second_gains,
):
    a, raw, q, k, v, table, win, wout, dy_left, wexp, gain = front(
        tokens[0],
        weight_input,
        weight_expand,
        gains[None],
        rope_rates(),
        weight_output,
        cotangent[0],
        lengths,
    )
    o, lse, y_parts, hid, d_hid, part_red, part_exp, d_gain_mid = core(
        q, k, v, tokens[0], wout, wexp, weight_reduce, cotangent[0], dy_left, gain
    )
    block_out, input_grad, grad_reduce, grad_output, grad_input, grad_expand, grad_gains = back(
        q, k, v, o, lse, wout, win, gain, part_red, part_exp, d_hid, d_gain_mid,
        y_parts, raw, table, a, hid, tokens[0],
    )
    own = gains.shape[0]
    index = lax.axis_index("dp") * lax.axis_size("shard") + lax.axis_index("shard")
    grad_gains = lax.dynamic_slice_in_dim(grad_gains.reshape(-1), index * own, own)
    done = update(
        (weight_input, weight_output, weight_expand, weight_reduce, gains[None]),
        (grad_input, grad_output, grad_expand, grad_reduce, grad_gains[None]),
        (first_input, first_output, first_expand, first_reduce, first_gains[None]),
        (second_input, second_output, second_expand, second_reduce, second_gains[None]),
    )
    done = [one[0] if n % 5 == 4 else one for n, one in enumerate(done)]
    return (block_out[None], input_grad[None], *done)


def solution(mesh):
    placed = (
        P("shard", "dp", None),
        P("shard", "dp", None),
        P("shard", None),
        P(("dp", "shard"), None),
        P(("dp", "shard"), None),
        P(("dp", "shard"), None),
        P(("dp", "shard"), None),
        P(("dp", "shard")),
        P(("dp", "shard"), None),
        P(("dp", "shard"), None),
        P(("dp", "shard"), None),
        P(("dp", "shard"), None),
        P(("dp", "shard")),
        P(("dp", "shard"), None),
        P(("dp", "shard"), None),
        P(("dp", "shard"), None),
        P(("dp", "shard"), None),
        P(("dp", "shard")),
    )
    return jax.shard_map(
        body,
        mesh=mesh,
        in_specs=placed,
        out_specs=(
            P("shard", "dp", None),
            P("shard", "dp", None),
            P(("dp", "shard"), None),
            P(("dp", "shard"), None),
            P(("dp", "shard"), None),
            P(("dp", "shard"), None),
            P(("dp", "shard")),
            P(("dp", "shard"), None),
            P(("dp", "shard"), None),
            P(("dp", "shard"), None),
            P(("dp", "shard"), None),
            P(("dp", "shard")),
            P(("dp", "shard"), None),
            P(("dp", "shard"), None),
            P(("dp", "shard"), None),
            P(("dp", "shard"), None),
            P(("dp", "shard")),
        ),
        check_vma=False,
    )
```

```python
import math

import jax
import jax.numpy as jnp
import numpy as np
from jax import lax
from jax.experimental import pallas as pl
from jax.experimental.pallas import tpu as pltpu
from jax.sharding import PartitionSpec as P

D = 1024
H = 16
KV = 8
HD = 128
FF = 3072
STEP = 10


norm_eps = 1e-06
rope_base = 1000000.0
beta_one = 0.9
beta_two = 0.95
adam_eps = 1e-08
matrix_rate = 0.1
gain_rate = 0.5
matrix_decay = 0.1
masked_score = -1e30


def adam_step(weight, grad, first, second, rate, decay):
    first_new = beta_one * first + (1.0 - beta_one) * grad
    second_new = beta_two * second + (1.0 - beta_two) * grad * grad
    fix_one = 1.0 - beta_one**STEP
    fix_two = 1.0 - beta_two**STEP
    direction = first_new / fix_one / (jnp.sqrt(second_new / fix_two) + adam_eps)
    return (weight - rate * (direction + decay * weight), first_new, second_new)


MESH = pl.DeviceIdType.MESH
F32 = jnp.float32
BF = jnp.bfloat16
VMEM = pl.BlockSpec(memory_space=pltpu.VMEM)
HBM = pl.BlockSpec(memory_space=pl.ANY)
SCORE = HD**-0.5 * math.log2(math.e)
BLOCK = 256
BIG = 30000.0
IN_COLS = (H + 2 * KV) * HD // 8
EXP_COLS = 2 * FF // 8
RED_ROWS = 32


def dot(a, b):
    return jnp.dot(a, b, preferred_element_type=F32)


def dot_t(a, b):
    return lax.dot_general(a, b, (((1,), (1,)), ((), ())), preferred_element_type=F32)


def t_dot(a, b):
    return lax.dot_general(a, b, (((0,), (0,)), ((), ())), preferred_element_type=F32)


def in_three(values):
    high = values.astype(BF)
    rest = values - high.astype(F32)
    middle = rest.astype(BF)
    return high.astype(F32), middle.astype(F32), (rest - middle.astype(F32)).astype(BF).astype(F32)


def block_rows(i):
    return pl.ds(pl.multiple_of(i * BLOCK, BLOCK), BLOCK)


def wide_rows(i):
    return pl.ds(pl.multiple_of(i * 2 * BLOCK, 2 * BLOCK), 2 * BLOCK)


def chip_rows(i):
    return pl.ds(pl.multiple_of(i * 2 * BLOCK, 2 * BLOCK), 2 * BLOCK)


def place():
    dp = lax.axis_index("dp")
    shard = lax.axis_index("shard")
    return dp // 2, lax.rem(dp, 2), shard // 4, lax.rem(shard, 4)


def device(z, core, x, y):
    return (lax.rem(z, 4) * 2 + core, lax.rem(x, 4) * 4 + lax.rem(y, 4))


def line_peers():
    z, core, x, y = place()
    return [device(z, 1 - core, x, y), device(z + 1, core, x, y), device(z + 3, core, x, y)]


def plane_peers():
    z, core, x, y = place()
    return [device(z, core, x + k, y) for k in (1, 2, 3)] + [
        device(z, core, x, y + k) for k in (1, 2, 3)
    ]


def dp_peers():
    dp = lax.axis_index("dp")
    shard = lax.axis_index("shard")
    return [(lax.rem(dp + k, 8), shard) for k in range(1, 8)]


def greet(peers):
    for peer in peers:
        pl.semaphore_signal(
            pltpu.get_barrier_semaphore(), inc=1, device_id=peer, device_id_type=MESH
        )


def meet(peers):
    pl.semaphore_wait(pltpu.get_barrier_semaphore(), len(peers))


def remote(src, dst, send, recv, peer):
    return pltpu.make_async_remote_copy(
        src_ref=src, dst_ref=dst, send_sem=send, recv_sem=recv, device_id=peer, device_id_type=MESH
    )


class LineGather:
    sems = 13

    def __init__(self, buf, send, recv):
        z, core, x, y = place()
        me, right, far, left = (lax.rem(z + k, 4) * 2 + core for k in range(4))
        to_right, to_left = device(z + 1, core, x, y), device(z + 3, core, x, y)
        sibling = device(z, 1 - core, x, y)
        plan = [
            (me, 0, to_right),
            (me, 1, to_right),
            (left, 0, to_right),
            (me, 1, to_left),
            (me, 0, to_left),
            (right, 1, to_left),
            (me, None, sibling),
            (left, 0, sibling),
            (right, 1, sibling),
            (left, 1, sibling),
            (right, 0, sibling),
            (far, 0, sibling),
            (far, 1, sibling),
        ]
        self.copies = []
        for k, (slot, half, peer) in enumerate(plan):
            ref = buf.at[slot] if half is None else buf.at[slot, half]
            self.copies.append(remote(ref, ref, send.at[k], recv.at[k], peer))

    def start(self, *which):
        for k in which:
            self.copies[k].start()

    def wait(self, *which):
        for k in which:
            self.copies[k].wait_recv()

    def begin(self):
        self.start(6, 0, 3, 1, 4)

    def pass_on(self):
        self.wait(0)
        self.start(2, 7)
        self.wait(3)
        self.start(5, 8)

    def second(self):
        self.wait(1)
        self.start(9)
        self.wait(4)
        self.start(10)

    def third(self):
        self.wait(2)
        self.start(11)
        self.wait(5)
        self.start(12)

    def sent(self):
        for copy in self.copies:
            copy.wait_send()


class PlaneGather:
    sems = 12

    def __init__(self, buf, send, recv):
        z, core, x, y = place()
        half = buf.shape[3] // 2
        low, high = pl.ds(0, half), pl.ds(half, half)
        self.copies = []
        refs = (
            (buf.at[x, y, :, low], 0),
            (buf.at[x, y, :, high], 1),
            (buf.at[:, y, :, low], 1),
            (buf.at[x, :, :, high], 0),
        )
        k = 0
        for ref, along_y in refs:
            for step in (1, 2, 3):
                peer = device(z, core, x, y + step) if along_y else device(z, core, x + step, y)
                self.copies.append(remote(ref, ref, send.at[k], recv.at[k], peer))
                k += 1

    def begin(self):
        for k in (0, 3, 1, 4, 2, 5):
            self.copies[k].start()

    def pass_on(self):
        for k in (0, 1, 2):
            self.copies[k].wait_recv()
        for k in (6, 7, 8):
            self.copies[k].start()
        for k in (3, 4, 5):
            self.copies[k].wait_recv()
        for k in (9, 10, 11):
            self.copies[k].start()

    def end(self):
        for k in range(6, 12):
            self.copies[k].wait_recv()

    def sent(self):
        for copy in self.copies:
            copy.wait_send()


class PlaneScatter:
    sems = 12

    def __init__(self, parts, got1, mid, got2, send, recv):
        z, core, x, y = place()
        self.parts, self.got1, self.mid, self.got2 = parts, got1, mid, got2
        half = parts.shape[3] // 2
        self.cols = (pl.ds(0, half), pl.ds(half, half))
        self.x, self.y = x, y
        self.copies = []
        k = 0
        for side in (0, 1):
            for step in (1, 2, 3):
                if side == 0:
                    ref = parts.at[:, lax.rem(y + step, 4), :, self.cols[0]]
                    peer = device(z, core, x, y + step)
                else:
                    ref = parts.at[lax.rem(x + step, 4), :, :, self.cols[1]]
                    peer = device(z, core, x + step, y)
                self.copies.append(remote(ref, got1.at[side, step - 1], send.at[k], recv.at[k], peer))
                k += 1
        for side in (0, 1):
            for step in (1, 2, 3):
                if side == 0:
                    ref = mid.at[0, lax.rem(x + step, 4)]
                    peer = device(z, core, x + step, y)
                else:
                    ref = mid.at[1, lax.rem(y + step, 4)]
                    peer = device(z, core, x, y + step)
                self.copies.append(remote(ref, got2.at[side, step - 1], send.at[k], recv.at[k], peer))
                k += 1

    def begin(self):
        for k in (0, 3, 1, 4, 2, 5):
            self.copies[k].start()

    def pass_on(self):
        for side in (0, 1):
            for k in range(3 * side, 3 * side + 3):
                self.copies[k].wait_recv()
            for j in range(4):
                if side == 0:
                    own = self.parts[j, self.y, :, self.cols[0]]
                else:
                    own = self.parts[self.x, j, :, self.cols[1]]
                total = own.astype(F32)
                for k in range(3):
                    total += self.got1[side, k, j].astype(F32)
                self.mid[side, j] = total.astype(BF)
            for k in range(6 + 3 * side, 9 + 3 * side):
                self.copies[k].start()

    def end(self, out):
        for side in (0, 1):
            for k in range(6 + 3 * side, 9 + 3 * side):
                self.copies[k].wait_recv()
            total = self.mid[side, self.x if side == 0 else self.y].astype(F32)
            for k in range(3):
                total += self.got2[side, k].astype(F32)
            out[:, self.cols[side]] = total

    def sent(self):
        for copy in self.copies:
            copy.wait_send()


def plane_scatter_scratch(rows, width):
    half = width // 2
    return [
        pltpu.VMEM((2, 3, 4, rows, half), BF),
        pltpu.VMEM((2, 4, rows, half), BF),
        pltpu.VMEM((2, 3, rows, half), BF),
        pltpu.SemaphoreType.DMA((12,)),
        pltpu.SemaphoreType.DMA((12,)),
    ]


class LineScatter:
    def __init__(self, parts, took, out_z, in_z, send, recv, kept=None):
        z, core, x, y = place()
        self.parts, self.kept, self.took, self.out_z, self.in_z = parts, kept, took, out_z, in_z
        to_right, to_left = device(z + 1, core, x, y), device(z + 3, core, x, y)
        sibling = device(z, 1 - core, x, y)
        self.exchange = lambda k: remote(parts.at[k, 0], took.at[k], send.at[k], recv.at[k], sibling)
        self.swap = [self.exchange(k) for k in range(4)]
        self.copies = [
            remote(
                out_z.at[k], in_z.at[k], send.at[4 + k], recv.at[4 + k], to_right if k < 3 else to_left
            )
            for k in range(6)
        ]

    def give(self, offset):
        self.swap[offset].start()

    def give_at(self, offset):
        self.exchange(offset).start()

    def take(self, offset):
        self.swap[offset].wait_recv()

    def half(self, offset, part):
        own = self.parts[offset, 1, part] if self.kept is None else self.kept[offset, part]
        return own.astype(F32) + self.took[offset, part].astype(F32)

    def push(self, k, value):
        self.out_z[k] = value.astype(BF)
        self.copies[k].start()

    def far(self):
        self.take(2)
        self.push(0, self.half(2, 0))
        self.push(3, self.half(2, 1))

    def near_right(self):
        self.take(1)
        self.push(1, self.half(1, 1))

    def near_left(self):
        self.take(3)
        self.push(4, self.half(3, 0))

    def near(self):
        self.near_right()
        self.near_left()

    def last_right(self):
        self.copies[0].wait_recv()
        self.push(2, self.half(1, 0) + self.in_z[0].astype(F32))

    def last_left(self):
        self.copies[3].wait_recv()
        self.push(5, self.half(3, 1) + self.in_z[3].astype(F32))

    def last(self):
        self.last_right()
        self.last_left()

    def result(self):
        self.take(0)
        self.copies[1].wait_recv()
        self.copies[4].wait_recv()
        self.copies[2].wait_recv()
        first = self.half(0, 0) + self.in_z[4].astype(F32) + self.in_z[2].astype(F32)
        self.copies[5].wait_recv()
        second = self.half(0, 1) + self.in_z[1].astype(F32) + self.in_z[5].astype(F32)
        return first, second

    def sent(self):
        for copy in self.swap + self.copies:
            copy.wait_send()


def line_scatter_scratch(rows, width):
    return [
        pltpu.VMEM((4, 2, 2, rows, width), BF),
        pltpu.VMEM((4, 2, rows, width), BF),
        pltpu.VMEM((6, rows, width), BF),
        pltpu.VMEM((6, rows, width), BF),
        pltpu.SemaphoreType.DMA((10,)),
        pltpu.SemaphoreType.DMA((10,)),
    ]


def to_send(w_in, gains, out):
    col = 0
    for ref, start, width in ((w_in, 0, 256), (w_in, H * HD, 128), (w_in, (H + KV) * HD, 128)):
        for j in range(8):
            out[j, :, col : col + width] = ref[:, start + j * width : start + (j + 1) * width]
        col += width
    out[:, :, col : col + 128] = jnp.zeros((8, 8, 128), F32)
    for j in range(8):
        out[j, 0:1, col : col + 18] = gains[...]


def spread_gains(gbuf):
    wide = 128 * 18
    held = gbuf[:, :, :, 0:128].reshape(128, 128)
    n = lax.broadcasted_iota(jnp.int32, (128, wide), 1)
    r = lax.broadcasted_iota(jnp.int32, (128, wide), 0)
    nf = n.astype(F32)
    within = nf - 18.0 * jnp.floor((nf + 0.5) * (1.0 / 18.0))
    pick = jnp.where(within == r.astype(F32), 1.0, 0.0)
    spread = jnp.dot(held, pick, precision=lax.Precision.HIGHEST, preferred_element_type=F32)
    first = ((r & 7) * 16 + (r >> 3)) * 18
    return jnp.sum(jnp.where((n >= first) & (n < first + 18), spread, 0.0), axis=0, keepdims=True)


def fill_order(perm):
    def block(i, carry):
        n = lax.broadcasted_iota(jnp.int32, (128, D), 0)
        k = lax.broadcasted_iota(jnp.int32, (128, D), 1)
        goal = (n >> 3) * 64 + i * 8 + (n & 7)
        perm[pl.ds(pl.multiple_of(i * 128, 128), 128), :] = jnp.where(k == goal, 1.0, 0.0).astype(BF)
        return carry

    lax.fori_loop(0, 8, block, 0)


def normed_rows(values):
    return lax.rsqrt(jnp.mean(values * values, axis=-1, keepdims=True) + norm_eps)


def token_tables(block, lengths, freq, table, q_ref, k_ref, v_ref):
    rows = block_rows(block)
    end0 = lengths[0, 0]
    end1 = end0 + lengths[0, 1]
    end2 = end1 + lengths[0, 2]
    token = block * BLOCK + lax.broadcasted_iota(jnp.int32, (BLOCK, HD), 0)
    lane = lax.broadcasted_iota(jnp.int32, (BLOCK, HD), 1)
    start = jnp.where(token >= end2, end2, jnp.where(token >= end1, end1, jnp.where(token >= end0, end0, 0)))
    angle = (token - start).astype(F32) * freq[0:1, :]
    table[rows, :] = jnp.sin(angle + jnp.where(lane < HD // 2, math.pi / 2, 0.0))
    one = lambda test: jnp.where(test, 1, 0)
    segment = one(token >= end0) + one(token >= end1) + one(token >= end2)
    same = segment == lane
    q_ref[rows, 256:384] = jnp.where(lane < 4, jnp.where(same, 0.0, -BIG), 0.0).astype(BF)
    k_ref[rows, 128:256] = jnp.where(lane < 4, jnp.where(same, 1.0, 0.0), jnp.where(lane < 7, 1.0, 0.0)).astype(BF)
    v_ref[rows, 128:256] = jnp.where(lane < 3, 1.0, 0.0).astype(BF)


def both_tables(table):
    lane = lax.broadcasted_iota(jnp.int32, table.shape, 1)
    other = pltpu.roll(table, HD // 2, 1)
    return jnp.where(lane < HD // 2, table, other), jnp.where(lane < HD // 2, -other, table)


def rope_rates():
    half = HD // 2
    rates = np.float32(rope_base) ** (-(2.0 * np.arange(half, dtype=np.float32)) / np.float32(HD))
    return jnp.asarray(np.tile(np.concatenate([rates, rates])[None], (8, 1)), F32)


def attend_block(i, q_ref, k_ref, v_ref, o_ref, lse_ref, acc, qs):
    rows = block_rows(i)
    for h in range(2):
        qs[h * BLOCK : (h + 1) * BLOCK, 0:HD] = q_ref[rows, h * HD : (h + 1) * HD]
        qs[h * BLOCK : (h + 1) * BLOCK, HD:] = q_ref[rows, 2 * HD :]

    query = lax.broadcasted_iota(jnp.int32, (2 * BLOCK, BLOCK), 0) & (BLOCK - 1)
    index = lax.broadcasted_iota(jnp.int32, (2 * BLOCK, BLOCK), 1)
    e = jnp.where(index <= query, jnp.exp2(dot_t(qs[...], k_ref[rows, :]) * SCORE), 0.0)
    acc[...] = dot(e.astype(BF), v_ref[rows, :])

    def step(kr):
        acc[...] += dot(jnp.exp2(dot_t(qs[...], k_ref[kr, :]) * SCORE).astype(BF), v_ref[kr, :])

    def wide(j, carry):
        step(wide_rows(j))
        return carry

    def narrow(j, carry):
        step(block_rows(j))
        return carry

    lax.fori_loop(0, i // 2, wide, 0)
    lax.fori_loop(i // 2 * 2, i, narrow, 0)
    total = acc[:, HD : HD + 1]
    out = acc[:, 0:HD] * (1.0 / total)
    lse = jnp.log2(total) * (1.0 / SCORE)
    for h in range(2):
        part = slice(h * BLOCK, (h + 1) * BLOCK)
        o_ref[rows, h * HD : (h + 1) * HD] = out[part].astype(BF)
        lse_ref[rows, h : h + 1] = lse[part]


def rms_back(h, r, dg):
    return r * dg - h * (r * r * r) * jnp.mean(h * dg, axis=-1, keepdims=True)


def unorder(values, perm):
    high = values.astype(BF)
    low = (values - high.astype(F32)).astype(BF)
    return dot_t(high, perm) + dot_t(low, perm)


def first_kernel(
    x_ref, w_in_ref, w_exp_ref, gains_ref, freq_ref, w_out_ref, w_red_ref, dy_own, lengths,
    a_out, raw_out, q_out, k_out, v_out, table_out, win_out, wout_out, o_out, lse_out, yparts_out,
    gain_ref, hid_ref, dhid_ref, gred_ref, gexp_ref, dgain_ref,
    xall, raw, q_ref, k_ref, v_ref, table, win_ref, wout_all, weight, o_ref, lse_ref, act_ref, wred, dy_all,
    wsend, wgot, esend, egot, gbuf, perm, acc, qs, wexp, wred_all, ball, dgu,
    parts, took, out_z, in_z,
    line_send, line_recv, cols_send, cols_recv, ec_send, ec_recv, win_send, win_recv, g_send, g_recv,
    o_send, o_recv, y_send, y_recv, e_send, e_recv, r_send, r_recv,
    s1_send, s1_recv, b_send, b_recv, s2_send, s2_recv, out_sem, w_sem,
):
    z, core, x, y = place()
    dp = lax.axis_index("dp")
    half = FF // 8
    peers = dp_peers()
    greet(peers + plane_peers())
    to_send(w_in_ref, gains_ref, wsend)
    fill_order(perm)
    values = x_ref[...].astype(F32)
    normed = (values * normed_rows(values)).astype(BF)
    xall[dp] = dot(normed, perm[...]).astype(BF).reshape(2, 128, D)
    dy_all[dp] = dy_own[...].reshape(2, 128, D)
    wout_all[x, y] = w_out_ref[...].astype(BF)
    wred_all[x, y] = jnp.concatenate([w_red_ref[...], jnp.zeros((8, D), F32)], axis=0).astype(BF)
    meet(peers + plane_peers())

    def exchange(src, dst, send, recv):
        copies = [
            remote(src.at[lax.rem(dp + k, 8)], dst.at[dp], send.at[k - 1], recv.at[k - 1], peers[k - 1])
            for k in range(1, 8)
        ]
        for copy in copies:
            copy.start()
        return copies

    cols = exchange(wsend, wgot, cols_send, cols_recv)
    line = LineGather(xall, line_send, line_recv)
    line.begin()
    wgot[dp] = wsend[dp]
    for j in range(8):
        for part in range(2):
            start = part * FF + j * 384
            esend[j, :, part * 384 : (part + 1) * 384] = w_exp_ref[:, start : start + 384]
    for copy in cols:
        copy.wait_recv()
    win_ref[x, y] = wgot[:, :, 0:IN_COLS].reshape(64, IN_COLS).astype(BF)
    own_gains = wgot[:, 0, IN_COLS:]
    gbuf[x, y, :, 0:128] = own_gains
    gbuf[x, y, :, 128:256] = own_gains
    plane_g = PlaneGather(gbuf, g_send, g_recv)
    plane_w = PlaneGather(win_ref, win_send, win_recv)
    plane_o = PlaneGather(wout_all, o_send, o_recv)
    plane_e = PlaneGather(wexp, e_send, e_recv)
    plane_r = PlaneGather(wred_all, r_send, r_recv)
    plane_g.begin()
    plane_w.begin()
    ecols = exchange(esend, egot, ec_send, ec_recv)
    egot[dp] = esend[dp]

    def tables(block, carry):
        token_tables(block, lengths, freq_ref, table, q_ref, k_ref, v_ref)
        return carry

    plane_g.pass_on()
    plane_w.pass_on()
    plane_o.begin()
    lax.fori_loop(0, 4, tables, 0)
    line.pass_on()
    line_y = LineGather(dy_all, y_send, y_recv)
    line_y.begin()
    plane_g.end()
    gains = spread_gains(gbuf)
    gain_ref[0:8, :] = jnp.broadcast_to(gains, (8, 2304))
    moved = jnp.zeros((8, D), F32)
    for term in in_three(gain_ref[0:8, 0:D]):
        moved += dot(term.astype(BF), perm[...])
    gain_ref[8:16, 0:D] = moved
    first = jnp.where(lax.broadcasted_iota(jnp.int32, (8, 128), 0) == 0, 1.0, 0.0)
    column = lax.dot_general(
        moved, first, (((0,), (0,)), ((), ())), precision=lax.Precision.HIGHEST, preferred_element_type=F32
    )[:, 0:1]
    plane_w.end()
    weight[...] = (win_ref[...].reshape(D, IN_COLS).astype(F32) * column).astype(BF)
    outs = []

    def write(src, dst, sem):
        copy = pltpu.make_async_copy(src, dst, sem)
        copy.start()
        outs.append(copy)

    write(weight, win_out, w_sem.at[0])
    lax.fori_loop(4, 8, tables, 0)

    def chip(offset):
        chip_at = lax.rem(z + offset, 4)
        rows = chip_rows(chip_at)
        qkv = dot(xall[pl.ds(chip_at * 2, 2)].reshape(512, D), weight[...])
        raw[rows, :] = qkv[:, 0:384]
        cos, sin = both_tables(table[rows, :])
        for part in range(3):
            u = qkv[:, part * HD : (part + 1) * HD]
            start = 2 * D + (HD if part == 2 else 0)
            u = u * normed_rows(u) * gain_ref[0:1, start : start + HD]
            u = (u * cos + pltpu.roll(u, HD // 2, 1) * sin).astype(BF)
            if part < 2:
                q_ref[rows, part * HD : (part + 1) * HD] = u
            else:
                k_ref[rows, 0:HD] = u
        v_ref[rows, 0:HD] = qkv[:, 384:512].astype(BF)

    def write_chip(offset):
        chip_at = lax.rem(z + offset, 4)
        rows = chip_rows(chip_at)
        blocks = pl.ds(chip_at * 2, 2)
        write(xall.at[blocks], a_out.at[blocks], out_sem.at[6 * offset])
        for n, (ref, out) in enumerate(
            ((raw, raw_out), (q_ref, q_out), (k_ref, k_out), (v_ref, v_out), (table, table_out))
        ):
            write(ref.at[rows, :], out.at[rows, :], out_sem.at[6 * offset + 1 + n])

    line.second()
    line.wait(6)
    chip(0)
    write_chip(0)
    for copy in ecols:
        copy.wait_recv()
    wexp[x, y] = egot[...].reshape(64, EXP_COLS).astype(BF)
    plane_o.pass_on()
    plane_e.begin()
    plane_r.begin()
    line.wait(7, 8, 9, 10)

    def near(t, carry):
        chip(1 + 2 * t)
        return carry

    lax.fori_loop(0, 2, near, 0)
    write_chip(1)
    write_chip(3)
    line.third()
    line_y.pass_on()
    line.wait(11, 12)
    chip(2)
    write_chip(2)
    plane_o.end()
    write(wout_all, wout_out, w_sem.at[1])
    scatter = LineScatter(parts, took, out_z, in_z, s1_send, s1_recv)
    wout = wout_all[...].reshape(256, D)

    def attend(t, carry):
        pair = t // 2
        offset = jnp.where(pair == 0, 2, jnp.where(pair == 1, 1, jnp.where(pair == 2, 3, 0)))
        second = lax.rem(t, 2)
        block = lax.rem(z + offset, 4) * 2 + jnp.where(second == 1, core, 1 - core)
        attend_block(block, q_ref, k_ref, v_ref, o_ref, lse_ref, acc, qs)
        parts[offset, second] = dot(o_ref[block_rows(block), :], wout).astype(BF).reshape(2, 128, D)

        @pl.when(second == 0)
        def _():
            scatter.give_at(offset)

        @pl.when(t == 1)
        def _():
            scatter.far()
            plane_e.pass_on()
            plane_r.pass_on()

        @pl.when(t == 0)
        def _():
            line_y.second()

        @pl.when(t == 3)
        def _():
            scatter.near_right()
            line_y.third()

        @pl.when(t == 5)
        def _():
            scatter.near_left()

        return carry

    lax.fori_loop(0, 8, attend, 0)
    line_y.wait(6, 7, 8, 9, 10, 11, 12)
    write(o_ref, o_out, w_sem.at[2])
    write(lse_ref, lse_out, w_sem.at[3])
    scatter.last()
    plane_e.end()
    plane_r.end()
    wred[...] = wred_all[...].astype(F32)[:, :, 0:24, :].reshape(half, D).astype(BF)
    first, second = scatter.result()
    hid_ref[...] = x_ref[...].astype(F32) + jnp.concatenate([first, second], axis=0)
    gain = gain_ref[0:1, D : 2 * D]
    hid = hid_ref[...]
    b = (hid * normed_rows(hid) * gain).astype(BF)
    ball[dp] = dot(b, perm[...]).astype(BF).reshape(2, 128, D)
    line_b = LineGather(ball, b_send, b_recv)
    line_b.begin()
    scatter.sent()
    scatter2 = LineScatter(parts, took, out_z, in_z, s2_send, s2_recv)

    def mlp(t, carry):
        offset = jnp.where(t == 0, 0, jnp.where(t == 1, 1, jnp.where(t == 2, 3, 2)))
        chip = lax.rem(z + offset, 4)
        rows = chip_rows(chip)
        both = pl.ds(chip * 2, 2)

        @pl.when(t == 0)
        def _():
            line_b.wait(6)

        @pl.when(t == 1)
        def _():
            line_b.pass_on()
            line_b.second()
            line_b.wait(7, 8, 9, 10)

        @pl.when(t == 3)
        def _():
            line_b.third()
            line_b.wait(11, 12)

        weight = wexp[...].reshape(D, EXP_COLS)
        gu = dot(ball[both].reshape(512, D), weight)
        gate, up = gu[:, :half], gu[:, half:]
        sig = 1.0 / (1.0 + jnp.exp(-gate))
        silu = gate * sig
        act_ref[rows, :] = (silu * up).astype(BF)
        d_act = dot_t(dy_all[both].reshape(512, D), wred[...])
        dgu[rows, 0:half] = (d_act * up * (sig * (1.0 + gate * (1.0 - sig)))).astype(BF)
        dgu[rows, half:] = (d_act * silu).astype(BF)
        partial = dot_t(dgu[rows, :], weight).astype(BF).reshape(2, 2, 128, D)
        parts[offset, core] = partial[1]
        parts[offset, 1 - core] = partial[0]
        scatter2.give_at(offset)

        @pl.when(t == 1)
        def _():
            scatter2.near_right()

        @pl.when(t == 2)
        def _():
            scatter2.near_left()

        return carry

    lax.fori_loop(0, 4, mlp, 0)
    scatter2.far()
    gred_ref[...] = jnp.concatenate(
        [
            t_dot(act_ref[...], dy_all[...].reshape(2048, D)).reshape(4, 4, 24, D),
            jnp.zeros((4, 4, 8, D), F32),
        ],
        axis=2,
    ).astype(BF)

    line.sent()
    for copy in outs:
        copy.wait()
    outs.clear()

    def outcome(offset, carry):
        chip = lax.rem(z + offset, 4)
        y_part = dot(act_ref[chip_rows(chip), :], wred[...]).astype(BF).reshape(2, 2, 128, D)
        xall[offset * 2 + core] = y_part[1]
        xall[offset * 2 + 1 - core] = y_part[0]
        return carry

    lax.fori_loop(0, 4, outcome, 0)
    write(xall, yparts_out, w_sem.at[4])
    scatter2.last()
    gexp_ref[...] = t_dot(ball[...].reshape(2048, D), dgu[...]).astype(BF).reshape(4, 4, 64, EXP_COLS)
    first, second = scatter2.result()
    d_b = unorder(jnp.concatenate([first, second], axis=0), perm[...])
    hid = hid_ref[...]
    r = normed_rows(hid)
    dgain_ref[...] = jnp.broadcast_to(jnp.sum(d_b * hid * r, axis=0, keepdims=True), (8, D))
    dhid_ref[...] = dy_own[...].astype(F32) + rms_back(hid, r, d_b * gain)
    for one in (line_y, line_b, plane_g, plane_w, plane_o, plane_e, plane_r, scatter2):
        one.sent()
    for copy in cols + ecols:
        copy.wait_send()
    for copy in outs:
        copy.wait()


def first(*args):
    sh = jax.ShapeDtypeStruct
    held = [
        ((8, 2, 128, D), BF),
        ((2048, 384), F32),
        ((2048, 384), BF),
        ((2048, 256), BF),
        ((2048, 256), BF),
        ((2048, 128), F32),
    ]
    weight = ((D, IN_COLS), BF)
    wout = ((4, 4, 16, D), BF)
    later = [((2048, 256), BF), ((2048, 128), F32)]
    return pl.pallas_call(
        first_kernel,
        out_shape=tuple(sh(*one) for one in held + [weight, wout] + later + held[:1])
        + (
            sh((16, 2304), F32),
            sh((256, D), F32),
            sh((256, D), F32),
            sh((4, 4, RED_ROWS, D), BF),
            sh((4, 4, 64, EXP_COLS), BF),
            sh((8, D), F32),
        ),
        in_specs=[VMEM] * 8 + [pl.BlockSpec(memory_space=pltpu.SMEM)],
        out_specs=[HBM] * 11 + [VMEM] * 6,
        scratch_shapes=[
            pltpu.VMEM(*one) for one in held + [((4, 4, 64, IN_COLS), BF), wout, weight] + later
        ]
        + [
            pltpu.VMEM((2048, FF // 8), BF),
            pltpu.VMEM((FF // 8, D), BF),
            pltpu.VMEM((8, 2, 128, D), BF),
            pltpu.VMEM((8, 8, IN_COLS + 128), F32),
            pltpu.VMEM((8, 8, IN_COLS + 128), F32),
            pltpu.VMEM((8, 8, EXP_COLS), F32),
            pltpu.VMEM((8, 8, EXP_COLS), F32),
            pltpu.VMEM((4, 4, 8, 256), F32),
            pltpu.VMEM((D, D), BF),
            pltpu.VMEM((2 * BLOCK, 256), F32),
            pltpu.VMEM((2 * BLOCK, 256), BF),
            pltpu.VMEM((4, 4, 64, EXP_COLS), BF),
            pltpu.VMEM((4, 4, RED_ROWS, D), BF),
            pltpu.VMEM((8, 2, 128, D), BF),
            pltpu.VMEM((2048, EXP_COLS), BF),
        ]
        + line_scatter_scratch(128, D)[:4]
        + [
            pltpu.SemaphoreType.DMA((n,))
            for n in (13, 13, 7, 7, 7, 7, 12, 12, 12, 12, 12, 12, 13, 13, 12, 12, 12, 12, 10, 10, 13, 13, 10, 10, 24, 5)
        ],
        compiler_params=pltpu.CompilerParams(
            collective_id=1, has_side_effects=True, vmem_limit_bytes=60 * 2**20
        ),
        name="first",
    )(*args)


def attend_back_block(
    i, q_ref, k_ref, v_ref, o_ref, lse_ref, do_ref,
    dk_ref, dv_ref, qs, dos, dqa,
):
    rows = block_rows(i)
    lane = lax.broadcasted_iota(jnp.int32, (BLOCK, HD), 1)
    for h in range(2):
        part = slice(h * BLOCK, (h + 1) * BLOCK)
        cols = slice(h * HD, (h + 1) * HD)
        qs[part, 0:HD] = q_ref[rows, cols]
        extra = q_ref[rows, 2 * HD :].astype(F32)
        for k, term in enumerate(in_three(lse_ref[rows, h : h + 1])):
            extra = jnp.where(lane == 4 + k, -term, extra)
        qs[part, HD:] = extra.astype(BF)
        d = do_ref[:, cols]
        dos[part, 0:HD] = d
        inner = jnp.sum(d.astype(F32) * o_ref[rows, cols].astype(F32), axis=1, keepdims=True)
        extra = jnp.zeros((BLOCK, HD), F32)
        for k, term in enumerate(in_three(inner)):
            extra = jnp.where(lane == k, -term, extra)
        dos[part, HD:] = extra.astype(BF)

    def step(kr, diagonal):
        p = jnp.exp2(dot_t(k_ref[kr, :], qs[...]) * SCORE)
        if diagonal:
            index = lax.broadcasted_iota(jnp.int32, (BLOCK, 2 * BLOCK), 0)
            query = lax.broadcasted_iota(jnp.int32, (BLOCK, 2 * BLOCK), 1) & (BLOCK - 1)
            p = jnp.where(index <= query, p, 0.0)
        ds = (p * dot_t(v_ref[kr, :], dos[...])).astype(BF)
        dv_ref[kr, :] += dot(p.astype(BF), dos[:, 0:HD])
        dk_ref[kr, :] += dot(ds, qs[:, 0:HD])
        dq = t_dot(ds, k_ref[kr, 0:HD])
        if diagonal:
            dqa[...] = dq
        else:
            dqa[...] += dq

    step(rows, True)

    def wide(j, carry):
        step(wide_rows(j), False)
        return carry

    def narrow(j, carry):
        step(block_rows(j), False)
        return carry

    lax.fori_loop(0, i // 2, wide, 0)
    lax.fori_loop(i // 2 * 2, i, narrow, 0)


def from_received(got, out, parts):
    col = 0
    for start, width in parts:
        for j in range(8):
            out[:, start + j * width : start + (j + 1) * width] = got[j, :, col : col + width]
        col += width


def back_kernel(
    wout_ref, gain_ref, pred_ref, pexp_ref, dhid, dmid_ref,
    q_in, k_in, v_in, o_in, lse_in, weight_in, yparts, raw_in, table_in, a_in, hid_in, x_in,
    y_ref, dx_ref, gred_ref, gout_ref, gin_out, gexp_out, dgain_ref,
    q_ref, k_ref, v_ref, o_ref, lse_ref, weight, raw, table, hid, x_ref,
    qs, dos, dqa, dk_ref, dv_ref, dqkv, acc, column, parts_q, parts_kv, pout, perm, datt, do_ref,
    gin, gexp, csend, cgot, esend, egot, gsum, gdp, gx, gy,
    *rest,
):
    z, core, x, y = place()
    dp = lax.axis_index("dp")
    peers = dp_peers()
    greet(peers + plane_peers())
    parts = (parts_q, parts_kv)
    datt[dp] = dhid[...].astype(BF).reshape(2, 128, D)
    (ykeep, ytook, y_out, y_in, ys, yr), rest = rest[:6], rest[6:]
    (d_parts, took, out_z, in_z, ss, sr), rest = rest[:6], rest[6:]
    planes = [
        PlaneScatter(part, *rest[5 * n : 5 * n + 5])
        for n, part in enumerate((pred_ref, pexp_ref, pout, *parts))
    ]
    plane_out, plane_q, plane_kv = planes[2:]
    planes = planes[:2]
    c_send, c_recv, e_send, e_recv, g_send, g_recv, d_send, d_recv, in_sem = rest[25:]
    scatter = LineScatter(d_parts, took, out_z, in_z, ss, sr)
    y_scatter = LineScatter(yparts, ytook, y_out, y_in, ys, yr, ykeep)
    line = LineGather(datt, d_send, d_recv)
    fetched = [
        pltpu.make_async_copy(src, dst, in_sem.at[n])
        for n, (src, dst) in enumerate(
            (
                (q_in, q_ref),
                (k_in, k_ref),
                (v_in, v_ref),
                (o_in, o_ref),
                (lse_in, lse_ref),
                (raw_in, raw),
                (table_in, table),
                (weight_in, weight),
                (yparts.at[:, 1], ykeep),
                (hid_in, hid),
                (x_in, x_ref),
            )
        )
    ]
    again = pltpu.make_async_copy(a_in, datt, in_sem.at[11])
    wout = wout_ref[...].reshape(256, D)
    for copy in fetched:
        copy.start()
    meet(peers + plane_peers())
    line.begin()
    for plane in planes:
        plane.begin()
    dk_ref[...] = jnp.zeros_like(dk_ref)
    dv_ref[...] = jnp.zeros_like(dv_ref)
    gsum[...] = jnp.zeros_like(gsum)
    fill_order(perm)
    for copy in fetched[:5]:
        copy.wait()

    def exchange(src, dst, send, recv):
        return [
            remote(src.at[lax.rem(dp + k, 8)], dst.at[dp], send.at[k - 1], recv.at[k - 1], peers[k - 1])
            for k in range(1, 8)
        ]

    ecols = exchange(esend, egot, e_send, e_recv)

    def through_norm(rows, part, d, tables):
        cos, sin = tables
        cols = slice(part * HD, (part + 1) * HD)
        u = raw[rows, cols]
        start = 2 * D + (HD if part == 2 else 0)
        gain = gain_ref[0:1, start : start + HD]
        d = d * HD**-0.5
        d = d * cos + pltpu.roll(d * sin, HD // 2, 1)
        r = normed_rows(u)
        row = 16 + part // 2
        gsum[row : row + 1, :] += jnp.sum(d * u * r, axis=0, keepdims=True)
        dqkv[rows, cols] = rms_back(u, r, d * gain).astype(BF)

    first = jnp.where(lax.broadcasted_iota(jnp.int32, (8, 128), 0) == 0, 1.0, 0.0)
    column[...] = lax.dot_general(
        gain_ref[8:16, 0:D],
        first,
        (((0,), (0,)), ((), ())),
        precision=lax.Precision.HIGHEST,
        preferred_element_type=F32,
    )

    def block(t, carry):
        offset = jnp.where(t < 2, 0, jnp.where(t < 4, 1, jnp.where(t < 6, 3, 2)))
        i = lax.rem(z + offset, 4) * 2 + jnp.where(lax.rem(t, 2) == 0, core, 1 - core)

        @pl.when(t == 1)
        def _():
            line.wait(6)

        @pl.when(t == 2)
        def _():
            line.pass_on()
            line.second()
            line.wait(7, 8, 9, 10)
            for k in (2, 1, 3, 0):
                y_scatter.give(k)

        @pl.when(t == 6)
        def _():
            line.third()
            line.wait(11, 12)
            pout[...] = t_dot(o_ref[...], datt[...].reshape(2048, D)).astype(BF).reshape(4, 4, 16, D)
            plane_out.begin()

        rows = block_rows(i)
        do_ref[...] = dot_t(datt[i].reshape(256, D), wout).astype(BF)

        @pl.when(t == 7)
        def _():
            line.sent()
            again.start()

        attend_back_block(i, q_ref, k_ref, v_ref, o_ref, lse_ref, do_ref, dk_ref, dv_ref, qs, dos, dqa)
        @pl.when(t == 0)
        def _():
            for copy in fetched[5:]:
                copy.wait()

        tables = both_tables(table[rows, :])
        for part in range(2):
            through_norm(rows, part, dqa[part * BLOCK : (part + 1) * BLOCK, :], tables)

        @pl.when(t == 4)
        def _():
            y_scatter.far()
            y_scatter.near()

        @pl.when(t == 6)
        def _():
            y_scatter.last()
            for plane in planes:
                plane.pass_on()

        @pl.when(t == 7)
        def _():
            again.wait()
            grad_columns(0)
            plane_q.begin()

        return carry

    def grad_columns(side):
        cols = slice(side * 256, side * 256 + 256)
        acc[...] = t_dot(datt[...].reshape(2048, D), dqkv[:, cols])
        parts[side][...] = (acc[...] * column[:, 0:1]).astype(BF).reshape(4, 4, 64, 256)
        inner = jnp.sum(acc[...] * weight[:, cols].astype(F32), axis=1, keepdims=True)
        if side == 0:
            column[:, 1:2] = inner
        return inner

    lax.fori_loop(0, 8, block, 0)

    def to_input(t, carry):
        offset = jnp.where(t == 0, 2, jnp.where(t == 1, 1, jnp.where(t == 2, 3, 0)))
        rows = chip_rows(lax.rem(z + offset, 4))
        through_norm(rows, 2, dk_ref[rows, :], both_tables(table[rows, :]))
        dqkv[rows, 384:512] = dv_ref[rows, :].astype(BF)
        partial = dot_t(dqkv[rows, :], weight[...]).astype(BF).reshape(2, 2, 128, D)
        d_parts[offset, core] = partial[1]
        d_parts[offset, 1 - core] = partial[0]
        scatter.give_at(offset)

        @pl.when(t == 0)
        def _():
            scatter.far()

        @pl.when(t == 1)
        def _():
            scatter.near_right()

        @pl.when(t == 2)
        def _():
            scatter.near_left()

        return carry

    lax.fori_loop(0, 4, to_input, 0)
    planes[1].end(gexp)
    for j in range(8):
        esend[j] = gexp[8 * j : 8 * j + 8, :]
    egot[dp] = esend[dp]
    for copy in ecols:
        copy.start()
    plane_q.pass_on()
    inner = grad_columns(1) + column[:, 1:2]
    plane_kv.begin()
    d_in = jnp.zeros((128, D), F32)
    for term in in_three(jnp.broadcast_to(inner, (D, 128))):
        d_in += lax.dot_general(
            term.astype(BF), perm[...], (((0,), (1,)), ((), ())), preferred_element_type=F32
        )
    d_in = d_in[0:1, :] * (1.0 / gain_ref[0:1, 0:D])
    for k in range(8):
        gsum[k : k + 1, :] = d_in[:, k * 128 : (k + 1) * 128]
        gsum[8 + k : 9 + k, :] = dmid_ref[0:1, k * 128 : (k + 1) * 128]
    dp_copies = [
        remote(gsum, gdp.at[k - 1], g_send.at[k - 1], g_recv.at[k - 1], peers[k - 1]) for k in range(1, 8)
    ]
    for copy in dp_copies:
        copy.start()

    plane_out.pass_on()
    scatter.last()

    def send_columns(plane, side):
        plane.end(gin)
        for j in range(8):
            csend[side, j] = gin[8 * j : 8 * j + 8, :]
        copies = exchange(csend.at[side], cgot.at[side], c_send.at[side], c_recv.at[side])
        for copy in copies:
            copy.start()
        cgot[side, dp] = csend[side, dp]
        return copies

    cols = send_columns(plane_q, 0)
    for copy in dp_copies:
        copy.wait_recv()
    total = gsum[...]
    for k in range(7):
        total += gdp[k]
    gx[0] = total
    x_copies = [
        remote(gx.at[0], gx.at[k], g_send.at[6 + k], g_recv.at[6 + k], device(z, core, x + k, y)) for k in (1, 2, 3)
    ]
    for copy in x_copies:
        copy.start()
    first, second = y_scatter.result()
    y_ref[...] = (hid[...] + jnp.concatenate([first, second], axis=0)).astype(BF)
    planes[0].end(gred_ref)
    plane_kv.pass_on()
    for copy in x_copies:
        copy.wait_recv()
    gy[0] = gx[0] + gx[1] + gx[2] + gx[3]
    y_copies = [
        remote(gy.at[0], gy.at[k], g_send.at[9 + k], g_recv.at[9 + k], device(z, core, x, y + k)) for k in (1, 2, 3)
    ]
    for copy in y_copies:
        copy.start()
    plane_out.end(gout_ref)
    for copy in ecols:
        copy.wait_recv()
    from_received(egot, gexp_out, ((0, 384), (FF, 384)))
    cols += send_columns(plane_kv, 1)
    first, second = scatter.result()
    d_a = unorder(jnp.concatenate([first, second], axis=0), perm[...])
    values = x_ref[...].astype(F32)
    dx_ref[...] = dhid[...] + rms_back(values, normed_rows(values), d_a)
    for copy in y_copies:
        copy.wait_recv()
    dgain_ref[...] = gy[0] + gy[1] + gy[2] + gy[3]
    for copy in cols:
        copy.wait_recv()
    from_received(cgot.at[0], gin_out, ((0, 256),))
    from_received(cgot.at[1], gin_out, ((H * HD, 128), ((H + KV) * HD, 128)))
    for copy in dp_copies + x_copies + y_copies + cols + ecols:
        copy.wait_send()
    for one in [scatter, y_scatter, plane_q, plane_kv, plane_out] + planes:
        one.sent()


def back(*args):
    sh = jax.ShapeDtypeStruct
    return pl.pallas_call(
        back_kernel,
        out_shape=(
            sh((256, D), BF),
            sh((256, D), F32),
            sh((RED_ROWS, D), F32),
            sh((16, D), F32),
            sh((8, 4096), F32),
            sh((8, 2 * FF), F32),
            sh((24, 128), F32),
        ),
        in_specs=[VMEM] * 6 + [HBM] * 12,
        out_specs=[VMEM] * 7,
        scratch_shapes=[
            pltpu.VMEM((2048, 384), BF),
            pltpu.VMEM((2048, 256), BF),
            pltpu.VMEM((2048, 256), BF),
            pltpu.VMEM((2048, 256), BF),
            pltpu.VMEM((2048, 128), F32),
            pltpu.VMEM((D, IN_COLS), BF),
            pltpu.VMEM((2048, 384), F32),
            pltpu.VMEM((2048, 128), F32),
            pltpu.VMEM((256, D), F32),
            pltpu.VMEM((256, D), BF),
            pltpu.VMEM((2 * BLOCK, 256), BF),
            pltpu.VMEM((2 * BLOCK, 256), BF),
            pltpu.VMEM((2 * BLOCK, HD), F32),
            pltpu.VMEM((2048, HD), F32),
            pltpu.VMEM((2048, HD), F32),
            pltpu.VMEM((2048, IN_COLS), BF),
            pltpu.VMEM((D, 256), F32),
            pltpu.VMEM((D, 128), F32),
            pltpu.VMEM((4, 4, 64, 256), BF),
            pltpu.VMEM((4, 4, 64, 256), BF),
            pltpu.VMEM((4, 4, 16, D), BF),
            pltpu.VMEM((D, D), BF),
            pltpu.VMEM((8, 2, 128, D), BF),
            pltpu.VMEM((BLOCK, 256), BF),
            pltpu.VMEM((64, 256), F32),
            pltpu.VMEM((64, EXP_COLS), F32),
            pltpu.VMEM((2, 8, 8, 256), F32),
            pltpu.VMEM((2, 8, 8, 256), F32),
            pltpu.VMEM((8, 8, EXP_COLS), F32),
            pltpu.VMEM((8, 8, EXP_COLS), F32),
            pltpu.VMEM((24, 128), F32),
            pltpu.VMEM((7, 24, 128), F32),
            pltpu.VMEM((4, 24, 128), F32),
            pltpu.VMEM((4, 24, 128), F32),
        ]
        + [pltpu.VMEM((4, 2, 128, D), BF)]
        + line_scatter_scratch(128, D)[1:]
        + line_scatter_scratch(128, D)
        + plane_scatter_scratch(RED_ROWS, D)
        + plane_scatter_scratch(64, EXP_COLS)
        + plane_scatter_scratch(16, D)
        + plane_scatter_scratch(64, 256)
        + plane_scatter_scratch(64, 256)
        + [pltpu.SemaphoreType.DMA((2, 7)), pltpu.SemaphoreType.DMA((2, 7))]
        + [pltpu.SemaphoreType.DMA((n,)) for n in (7, 7, 13, 13, 13, 13, 12)],
        compiler_params=pltpu.CompilerParams(
            collective_id=3, has_side_effects=True, vmem_limit_bytes=60 * 2**20
        ),
        name="back",
    )(*args)


def update_kernel(*refs):
    weights, grads, firsts, seconds = (refs[5 * n : 5 * n + 5] for n in range(4))
    y_ref, dx_ref, y_out, dx_out = refs[20:24]
    news, means, squares = (refs[24 + 5 * n : 29 + 5 * n] for n in range(3))
    y_out[...] = y_ref[...]
    dx_out[...] = dx_ref[...]
    for k in range(4):
        news[k][...], means[k][...], squares[k][...] = adam_step(
            weights[k][...],
            grads[k][0 : weights[k].shape[0], :],
            firsts[k][...],
            seconds[k][...],
            matrix_rate,
            matrix_decay,
        )
    own = weights[4].shape[1]
    first = (lax.axis_index("dp") * 16 + lax.axis_index("shard")) * own
    row, col = first // 128, lax.rem(first, 128)
    lane = lax.broadcasted_iota(jnp.int32, (8, 128), 1)
    here = pltpu.roll(jnp.broadcast_to(grads[4][pl.ds(row, 1), :], (8, 128)), lax.rem(128 - col, 128), 1)
    after = pltpu.roll(jnp.broadcast_to(grads[4][pl.ds(row + 1, 1), :], (8, 128)), lax.rem(128 - col, 128), 1)
    grad = jnp.where(lane < 128 - col, here, after)[0:1, 0:own]
    news[4][...], means[4][...], squares[4][...] = adam_step(
        weights[4][...], grad, firsts[4][...], seconds[4][...], gain_rate, 0.0
    )


def update(weights, grads, firsts, seconds, y, dx):
    like = tuple(jax.ShapeDtypeStruct(w.shape, F32) for w in weights)
    return pl.pallas_call(
        update_kernel,
        out_shape=(jax.ShapeDtypeStruct(y.shape, BF), jax.ShapeDtypeStruct(dx.shape, F32)) + like * 3,
        in_specs=[VMEM] * 22,
        out_specs=[VMEM] * 17,
        compiler_params=pltpu.CompilerParams(vmem_limit_bytes=60 * 2**20),
        name="update",
    )(*weights, *grads, *firsts, *seconds, y, dx)


def body(
    tokens,
    cotangent,
    lengths,
    weight_input,
    weight_output,
    weight_expand,
    weight_reduce,
    gains,
    first_input,
    first_output,
    first_expand,
    first_reduce,
    first_gains,
    second_input,
    second_output,
    second_expand,
    second_reduce,
    second_gains,
):
    a, raw, q, k, v, table, win, wout, o, lse, y_parts, gain, hid, d_hid, part_red, part_exp, d_gain_mid = first(
        tokens[0],
        weight_input,
        weight_expand,
        gains[None],
        rope_rates(),
        weight_output,
        weight_reduce,
        cotangent[0],
        lengths,
    )
    block_out, input_grad, grad_reduce, grad_output, grad_input, grad_expand, grad_gains = back(
        wout, gain, part_red, part_exp, d_hid, d_gain_mid,
        q, k, v, o, lse, win, y_parts.reshape(4, 2, 2, 128, D), raw, table, a, hid, tokens[0],
    )
    block_out, input_grad, *done = update(
        (weight_input, weight_output, weight_expand, weight_reduce, gains[None]),
        (grad_input, grad_output, grad_expand, grad_reduce, grad_gains),
        (first_input, first_output, first_expand, first_reduce, first_gains[None]),
        (second_input, second_output, second_expand, second_reduce, second_gains[None]),
        block_out,
        input_grad,
    )
    done = [one[0] if n % 5 == 4 else one for n, one in enumerate(done)]
    return (block_out[None], input_grad[None], *done)


def solution(mesh):
    placed = (
        P("shard", "dp", None),
        P("shard", "dp", None),
        P("shard", None),
        P(("dp", "shard"), None),
        P(("dp", "shard"), None),
        P(("dp", "shard"), None),
        P(("dp", "shard"), None),
        P(("dp", "shard")),
        P(("dp", "shard"), None),
        P(("dp", "shard"), None),
        P(("dp", "shard"), None),
        P(("dp", "shard"), None),
        P(("dp", "shard")),
        P(("dp", "shard"), None),
        P(("dp", "shard"), None),
        P(("dp", "shard"), None),
        P(("dp", "shard"), None),
        P(("dp", "shard")),
    )
    return jax.shard_map(
        body,
        mesh=mesh,
        in_specs=placed,
        out_specs=(
            P("shard", "dp", None),
            P("shard", "dp", None),
            P(("dp", "shard"), None),
            P(("dp", "shard"), None),
            P(("dp", "shard"), None),
            P(("dp", "shard"), None),
            P(("dp", "shard")),
            P(("dp", "shard"), None),
            P(("dp", "shard"), None),
            P(("dp", "shard"), None),
            P(("dp", "shard"), None),
            P(("dp", "shard")),
            P(("dp", "shard"), None),
            P(("dp", "shard"), None),
            P(("dp", "shard"), None),
            P(("dp", "shard"), None),
            P(("dp", "shard")),
        ),
        check_vma=False,
    )
```

```python
import math

import jax
import jax.numpy as jnp
import numpy as np
from jax import lax
from jax.experimental import pallas as pl
from jax.experimental.pallas import tpu as pltpu
from jax.sharding import PartitionSpec as P

D = 1024
H = 16
KV = 8
HD = 128
FF = 3072
STEP = 10


norm_eps = 1e-06
rope_base = 1000000.0
beta_one = 0.9
beta_two = 0.95
adam_eps = 1e-08
matrix_rate = 0.1
gain_rate = 0.5
matrix_decay = 0.1
masked_score = -1e30


def adam_step(weight, grad, first, second, rate, decay):
    first_new = beta_one * first + (1.0 - beta_one) * grad
    second_new = beta_two * second + (1.0 - beta_two) * grad * grad
    fix_one = 1.0 - beta_one**STEP
    fix_two = 1.0 - beta_two**STEP
    direction = first_new / fix_one / (jnp.sqrt(second_new / fix_two) + adam_eps)
    return (weight - rate * (direction + decay * weight), first_new, second_new)


MESH = pl.DeviceIdType.MESH
F32 = jnp.float32
BF = jnp.bfloat16
VMEM = pl.BlockSpec(memory_space=pltpu.VMEM)
HBM = pl.BlockSpec(memory_space=pl.ANY)
SCORE = HD**-0.5 * math.log2(math.e)
BLOCK = 256
BIG = 30000.0
IN_COLS = (H + 2 * KV) * HD // 8
EXP_COLS = 2 * FF // 8
RED_ROWS = 32


def dot(a, b):
    return jnp.dot(a, b, preferred_element_type=F32)


def dot_t(a, b):
    return lax.dot_general(a, b, (((1,), (1,)), ((), ())), preferred_element_type=F32)


def t_dot(a, b):
    return lax.dot_general(a, b, (((0,), (0,)), ((), ())), preferred_element_type=F32)


def in_three(values):
    high = values.astype(BF)
    rest = values - high.astype(F32)
    middle = rest.astype(BF)
    return high.astype(F32), middle.astype(F32), (rest - middle.astype(F32)).astype(BF).astype(F32)


def block_rows(i):
    return pl.ds(pl.multiple_of(i * BLOCK, BLOCK), BLOCK)


def wide_rows(i):
    return pl.ds(pl.multiple_of(i * 2 * BLOCK, 2 * BLOCK), 2 * BLOCK)


def chip_rows(i):
    return pl.ds(pl.multiple_of(i * 2 * BLOCK, 2 * BLOCK), 2 * BLOCK)


def place():
    dp = lax.axis_index("dp")
    shard = lax.axis_index("shard")
    return dp // 2, lax.rem(dp, 2), shard // 4, lax.rem(shard, 4)


def device(z, core, x, y):
    return (lax.rem(z, 4) * 2 + core, lax.rem(x, 4) * 4 + lax.rem(y, 4))


def line_peers():
    z, core, x, y = place()
    return [device(z, 1 - core, x, y), device(z + 1, core, x, y), device(z + 3, core, x, y)]


def plane_peers():
    z, core, x, y = place()
    return [device(z, core, x + k, y) for k in (1, 2, 3)] + [
        device(z, core, x, y + k) for k in (1, 2, 3)
    ]


def dp_peers():
    dp = lax.axis_index("dp")
    shard = lax.axis_index("shard")
    return [(lax.rem(dp + k, 8), shard) for k in range(1, 8)]


def greet(peers):
    for peer in peers:
        pl.semaphore_signal(
            pltpu.get_barrier_semaphore(), inc=1, device_id=peer, device_id_type=MESH
        )


def meet(peers):
    pl.semaphore_wait(pltpu.get_barrier_semaphore(), len(peers))


def remote(src, dst, send, recv, peer):
    return pltpu.make_async_remote_copy(
        src_ref=src, dst_ref=dst, send_sem=send, recv_sem=recv, device_id=peer, device_id_type=MESH
    )


class LineGather:
    sems = 13

    def __init__(self, buf, send, recv):
        z, core, x, y = place()
        me, right, far, left = (lax.rem(z + k, 4) * 2 + core for k in range(4))
        to_right, to_left = device(z + 1, core, x, y), device(z + 3, core, x, y)
        sibling = device(z, 1 - core, x, y)
        plan = [
            (me, 0, to_right),
            (me, 1, to_right),
            (left, 0, to_right),
            (me, 1, to_left),
            (me, 0, to_left),
            (right, 1, to_left),
            (me, None, sibling),
            (left, 0, sibling),
            (right, 1, sibling),
            (left, 1, sibling),
            (right, 0, sibling),
            (far, 0, sibling),
            (far, 1, sibling),
        ]
        self.copies = []
        for k, (slot, half, peer) in enumerate(plan):
            ref = buf.at[slot] if half is None else buf.at[slot, half]
            self.copies.append(remote(ref, ref, send.at[k], recv.at[k], peer))

    def start(self, *which):
        for k in which:
            self.copies[k].start()

    def wait(self, *which):
        for k in which:
            self.copies[k].wait_recv()

    def begin(self):
        self.start(6, 0, 3, 1, 4)

    def pass_on(self):
        self.wait(0)
        self.start(2, 7)
        self.wait(3)
        self.start(5, 8)

    def second(self):
        self.wait(1)
        self.start(9)
        self.wait(4)
        self.start(10)

    def third(self):
        self.wait(2)
        self.start(11)
        self.wait(5)
        self.start(12)

    def sent(self):
        for copy in self.copies:
            copy.wait_send()


class ChipGather:
    sems = 13

    def __init__(self, buf, send, recv):
        z, core, x, y = place()
        self.core = core
        chips = [lax.rem(z + k, 4) * 2 for k in range(4)]
        me, right, far, left = chips
        to_right, to_left = device(z + 1, core, x, y), device(z + 3, core, x, y)
        onward = device(z + 1 + 2 * core, core, x, y)
        behind = lax.rem(z + 3 - 2 * core, 4) * 2
        sibling = device(z, 1 - core, x, y)
        plan = [(buf.at[me + core], sibling)]
        for block in (0, 1):
            plan += [(buf.at[me + block, core], to_right), (buf.at[me + block, core], to_left)]
        plan += [(buf.at[behind + block, core], onward) for block in (0, 1)]
        for block in (0, 1):
            plan += [(buf.at[left + block, core], sibling), (buf.at[right + block, core], sibling)]
        plan += [(buf.at[far + block, core], sibling) for block in (0, 1)]
        self.copies = [remote(ref, ref, send.at[k], recv.at[k], peer) for k, (ref, peer) in enumerate(plan)]

    def start(self, *which):
        for k in which:
            self.copies[k].start()

    def wait(self, *which):
        for k in which:
            self.copies[k].wait_recv()

    def begin(self):
        self.start(0)

        @pl.when(self.core == 0)
        def _():
            self.start(1, 2)

        self.wait(0)

        @pl.when(self.core == 1)
        def _():
            self.start(1, 2)

        self.start(3, 4)

    def neighbours(self, block):
        for side in (0, 1):
            self.wait(1 + 2 * block + side)
            self.start(7 + 2 * block + side)

            @pl.when(self.core == side)
            def _():
                self.start(5 + block)

        self.wait(7 + 2 * block, 8 + 2 * block)

    def first(self):
        self.neighbours(0)

    def second(self):
        self.neighbours(1)

    def third(self):
        for block in (0, 1):
            self.wait(5 + block)
            self.start(11 + block)
        self.wait(11, 12)

    def sent(self):
        for copy in self.copies:
            copy.wait_send()


class PlaneGather:
    sems = 12

    def __init__(self, buf, send, recv):
        z, core, x, y = place()
        half = buf.shape[3] // 2
        low, high = pl.ds(0, half), pl.ds(half, half)
        self.copies = []
        refs = (
            (buf.at[x, y, :, low], 0),
            (buf.at[x, y, :, high], 1),
            (buf.at[:, y, :, low], 1),
            (buf.at[x, :, :, high], 0),
        )
        k = 0
        for ref, along_y in refs:
            for step in (1, 2, 3):
                peer = device(z, core, x, y + step) if along_y else device(z, core, x + step, y)
                self.copies.append(remote(ref, ref, send.at[k], recv.at[k], peer))
                k += 1

    def begin(self):
        for k in (0, 3, 1, 4, 2, 5):
            self.copies[k].start()

    def pass_on(self):
        for k in (0, 1, 2):
            self.copies[k].wait_recv()
        for k in (6, 7, 8):
            self.copies[k].start()
        for k in (3, 4, 5):
            self.copies[k].wait_recv()
        for k in (9, 10, 11):
            self.copies[k].start()

    def end(self):
        for k in range(6, 12):
            self.copies[k].wait_recv()

    def sent(self):
        for copy in self.copies:
            copy.wait_send()


class PlaneScatter:
    sems = 12

    def __init__(self, parts, got1, mid, got2, send, recv):
        z, core, x, y = place()
        self.parts, self.got1, self.mid, self.got2 = parts, got1, mid, got2
        half = parts.shape[3] // 2
        self.cols = (pl.ds(0, half), pl.ds(half, half))
        self.x, self.y = x, y
        self.copies = []
        k = 0
        for side in (0, 1):
            for step in (1, 2, 3):
                if side == 0:
                    ref = parts.at[:, lax.rem(y + step, 4), :, self.cols[0]]
                    peer = device(z, core, x, y + step)
                else:
                    ref = parts.at[lax.rem(x + step, 4), :, :, self.cols[1]]
                    peer = device(z, core, x + step, y)
                self.copies.append(remote(ref, got1.at[side, step - 1], send.at[k], recv.at[k], peer))
                k += 1
        for side in (0, 1):
            for step in (1, 2, 3):
                if side == 0:
                    ref = mid.at[0, lax.rem(x + step, 4)]
                    peer = device(z, core, x + step, y)
                else:
                    ref = mid.at[1, lax.rem(y + step, 4)]
                    peer = device(z, core, x, y + step)
                self.copies.append(remote(ref, got2.at[side, step - 1], send.at[k], recv.at[k], peer))
                k += 1

    def begin(self):
        for k in (0, 3, 1, 4, 2, 5):
            self.copies[k].start()

    def pass_on(self):
        for side in (0, 1):
            for k in range(3 * side, 3 * side + 3):
                self.copies[k].wait_recv()
            for j in range(4):
                if side == 0:
                    own = self.parts[j, self.y, :, self.cols[0]]
                else:
                    own = self.parts[self.x, j, :, self.cols[1]]
                total = own.astype(F32)
                for k in range(3):
                    total += self.got1[side, k, j].astype(F32)
                self.mid[side, j] = total.astype(BF)
            for k in range(6 + 3 * side, 9 + 3 * side):
                self.copies[k].start()

    def end(self, out):
        for side in (0, 1):
            for k in range(6 + 3 * side, 9 + 3 * side):
                self.copies[k].wait_recv()
            total = self.mid[side, self.x if side == 0 else self.y].astype(F32)
            for k in range(3):
                total += self.got2[side, k].astype(F32)
            out[:, self.cols[side]] = total

    def sent(self):
        for copy in self.copies:
            copy.wait_send()


def plane_scatter_scratch(rows, width):
    half = width // 2
    return [
        pltpu.VMEM((2, 3, 4, rows, half), BF),
        pltpu.VMEM((2, 4, rows, half), BF),
        pltpu.VMEM((2, 3, rows, half), BF),
        pltpu.SemaphoreType.DMA((12,)),
        pltpu.SemaphoreType.DMA((12,)),
    ]


class LineScatter:
    def __init__(self, parts, took, out_z, in_z, send, recv, kept=None):
        z, core, x, y = place()
        self.parts, self.kept, self.took, self.out_z, self.in_z = parts, kept, took, out_z, in_z
        to_right, to_left = device(z + 1, core, x, y), device(z + 3, core, x, y)
        sibling = device(z, 1 - core, x, y)
        self.exchange = lambda k: remote(parts.at[k, 0], took.at[k], send.at[k], recv.at[k], sibling)
        self.swap = [self.exchange(k) for k in range(4)]
        self.copies = [
            remote(
                out_z.at[k], in_z.at[k], send.at[4 + k], recv.at[4 + k], to_right if k < 3 else to_left
            )
            for k in range(6)
        ]

    def give(self, offset):
        self.swap[offset].start()

    def give_at(self, offset):
        self.exchange(offset).start()

    def take(self, offset):
        self.swap[offset].wait_recv()

    def half(self, offset, part):
        own = self.parts[offset, 1, part] if self.kept is None else self.kept[offset, part]
        return own.astype(F32) + self.took[offset, part].astype(F32)

    def push(self, k, value):
        self.out_z[k] = value.astype(BF)
        self.copies[k].start()

    def far(self):
        self.take(2)
        self.push(0, self.half(2, 0))
        self.push(3, self.half(2, 1))

    def near_right(self):
        self.take(1)
        self.push(1, self.half(1, 1))

    def near_left(self):
        self.take(3)
        self.push(4, self.half(3, 0))

    def near(self):
        self.near_right()
        self.near_left()

    def last_right(self):
        self.copies[0].wait_recv()
        self.push(2, self.half(1, 0) + self.in_z[0].astype(F32))

    def last_left(self):
        self.copies[3].wait_recv()
        self.push(5, self.half(3, 1) + self.in_z[3].astype(F32))

    def last(self):
        self.last_right()
        self.last_left()

    def result(self):
        self.take(0)
        self.copies[1].wait_recv()
        self.copies[4].wait_recv()
        self.copies[2].wait_recv()
        first = self.half(0, 0) + self.in_z[4].astype(F32) + self.in_z[2].astype(F32)
        self.copies[5].wait_recv()
        second = self.half(0, 1) + self.in_z[1].astype(F32) + self.in_z[5].astype(F32)
        return first, second

    def sent(self):
        for copy in self.swap + self.copies:
            copy.wait_send()


def line_scatter_scratch(rows, width):
    return [
        pltpu.VMEM((4, 2, 2, rows, width), BF),
        pltpu.VMEM((4, 2, rows, width), BF),
        pltpu.VMEM((6, rows, width), BF),
        pltpu.VMEM((6, rows, width), BF),
        pltpu.SemaphoreType.DMA((10,)),
        pltpu.SemaphoreType.DMA((10,)),
    ]


def to_send(w_in, gains, out):
    col = 0
    for ref, start, width in ((w_in, 0, 256), (w_in, H * HD, 128), (w_in, (H + KV) * HD, 128)):
        for j in range(8):
            out[j, :, col : col + width] = ref[:, start + j * width : start + (j + 1) * width]
        col += width
    out[:, :, col : col + 128] = jnp.zeros((8, 8, 128), F32)
    for j in range(8):
        out[j, 0:1, col : col + 18] = gains[...]


def spread_gains(gbuf):
    wide = 128 * 18
    held = gbuf[:, :, :, 0:128].reshape(128, 128)
    n = lax.broadcasted_iota(jnp.int32, (128, wide), 1)
    r = lax.broadcasted_iota(jnp.int32, (128, wide), 0)
    nf = n.astype(F32)
    within = nf - 18.0 * jnp.floor((nf + 0.5) * (1.0 / 18.0))
    pick = jnp.where(within == r.astype(F32), 1.0, 0.0)
    spread = jnp.dot(held, pick, precision=lax.Precision.HIGHEST, preferred_element_type=F32)
    first = ((r & 7) * 16 + (r >> 3)) * 18
    return jnp.sum(jnp.where((n >= first) & (n < first + 18), spread, 0.0), axis=0, keepdims=True)


def fill_order(perm):
    def block(i, carry):
        n = lax.broadcasted_iota(jnp.int32, (128, D), 0)
        k = lax.broadcasted_iota(jnp.int32, (128, D), 1)
        goal = (n >> 3) * 64 + i * 8 + (n & 7)
        perm[pl.ds(pl.multiple_of(i * 128, 128), 128), :] = jnp.where(k == goal, 1.0, 0.0).astype(BF)
        return carry

    lax.fori_loop(0, 8, block, 0)


def normed_rows(values):
    return lax.rsqrt(jnp.mean(values * values, axis=-1, keepdims=True) + norm_eps)


def token_tables(block, lengths, freq, table, q_ref, k_ref, v_ref):
    rows = block_rows(block)
    end0 = lengths[0, 0]
    end1 = end0 + lengths[0, 1]
    end2 = end1 + lengths[0, 2]
    token = block * BLOCK + lax.broadcasted_iota(jnp.int32, (BLOCK, HD), 0)
    lane = lax.broadcasted_iota(jnp.int32, (BLOCK, HD), 1)
    start = jnp.where(token >= end2, end2, jnp.where(token >= end1, end1, jnp.where(token >= end0, end0, 0)))
    angle = (token - start).astype(F32) * freq[0:1, :]
    table[rows, :] = jnp.sin(angle + jnp.where(lane < HD // 2, math.pi / 2, 0.0))
    one = lambda test: jnp.where(test, 1, 0)
    segment = one(token >= end0) + one(token >= end1) + one(token >= end2)
    same = segment == lane
    q_ref[rows, 256:384] = jnp.where(lane < 4, jnp.where(same, 0.0, -BIG), 0.0).astype(BF)
    k_ref[rows, 128:256] = jnp.where(lane < 4, jnp.where(same, 1.0, 0.0), jnp.where(lane < 7, 1.0, 0.0)).astype(BF)
    v_ref[rows, 128:256] = jnp.where(lane < 3, 1.0, 0.0).astype(BF)


def both_tables(table):
    lane = lax.broadcasted_iota(jnp.int32, table.shape, 1)
    other = pltpu.roll(table, HD // 2, 1)
    return jnp.where(lane < HD // 2, table, other), jnp.where(lane < HD // 2, -other, table)


def rope_rates():
    half = HD // 2
    rates = np.float32(rope_base) ** (-(2.0 * np.arange(half, dtype=np.float32)) / np.float32(HD))
    return jnp.asarray(np.tile(np.concatenate([rates, rates])[None], (8, 1)), F32)


def attend_block(i, q_ref, k_ref, v_ref, o_ref, lse_ref, acc, qs):
    rows = block_rows(i)
    for h in range(2):
        qs[h * BLOCK : (h + 1) * BLOCK, 0:HD] = q_ref[rows, h * HD : (h + 1) * HD]
        qs[h * BLOCK : (h + 1) * BLOCK, HD:] = q_ref[rows, 2 * HD :]

    query = lax.broadcasted_iota(jnp.int32, (2 * BLOCK, BLOCK), 0) & (BLOCK - 1)
    index = lax.broadcasted_iota(jnp.int32, (2 * BLOCK, BLOCK), 1)
    e = jnp.where(index <= query, jnp.exp2(dot_t(qs[...], k_ref[rows, :]) * SCORE), 0.0)
    acc[...] = dot(e.astype(BF), v_ref[rows, :])

    def step(kr):
        acc[...] += dot(jnp.exp2(dot_t(qs[...], k_ref[kr, :]) * SCORE).astype(BF), v_ref[kr, :])

    def wide(j, carry):
        step(wide_rows(j))
        return carry

    def narrow(j, carry):
        step(block_rows(j))
        return carry

    lax.fori_loop(0, i // 2, wide, 0)
    lax.fori_loop(i // 2 * 2, i, narrow, 0)
    total = acc[:, HD : HD + 1]
    out = acc[:, 0:HD] * (1.0 / total)
    lse = jnp.log2(total) * (1.0 / SCORE)
    for h in range(2):
        part = slice(h * BLOCK, (h + 1) * BLOCK)
        o_ref[rows, h * HD : (h + 1) * HD] = out[part].astype(BF)
        lse_ref[rows, h : h + 1] = lse[part]


def rms_back(h, r, dg):
    return r * dg - h * (r * r * r) * jnp.mean(h * dg, axis=-1, keepdims=True)


def unorder(values, perm):
    high = values.astype(BF)
    low = (values - high.astype(F32)).astype(BF)
    return dot_t(high, perm) + dot_t(low, perm)


def first_kernel(
    x_ref, w_in_ref, w_exp_ref, gains_ref, freq_ref, w_out_ref, w_red_ref, dy_own, lengths,
    a_out, raw_out, q_out, k_out, v_out, table_out, win_out, wout_out, o_out, lse_out, yparts_out,
    hid_out, gred_out, gexp_out, gain_ref, dhid_ref, dgain_ref,
    hid_ref, gred_ref, gexp_ref, xall, raw, q_ref, k_ref, v_ref, table, win_ref, wout_all, weight, o_ref, lse_ref, act_ref, wred, dy_all,
    wsend, wgot, esend, egot, gbuf, perm, acc, qs, wexp, wred_all, ball, dgu,
    parts, took, out_z, in_z,
    line_send, line_recv, cols_send, cols_recv, ec_send, ec_recv, win_send, win_recv, g_send, g_recv,
    o_send, o_recv, y_send, y_recv, e_send, e_recv, r_send, r_recv,
    s1_send, s1_recv, b_send, b_recv, s2_send, s2_recv, out_sem, w_sem,
):
    z, core, x, y = place()
    dp = lax.axis_index("dp")
    half = FF // 8
    peers = dp_peers()
    greet(peers + plane_peers())
    to_send(w_in_ref, gains_ref, wsend)
    fill_order(perm)
    values = x_ref[...].astype(F32)
    normed = (values * normed_rows(values)).astype(BF)
    xall[dp] = dot(normed, perm[...]).astype(BF).reshape(2, 128, D)
    dy_all[dp] = dy_own[...].reshape(2, 128, D)
    wout_all[x, y] = w_out_ref[...].astype(BF)
    wred_all[x, y] = jnp.concatenate([w_red_ref[...], jnp.zeros((8, D), F32)], axis=0).astype(BF)
    meet(peers + plane_peers())

    def exchange(src, dst, send, recv):
        copies = [
            remote(src.at[lax.rem(dp + k, 8)], dst.at[dp], send.at[k - 1], recv.at[k - 1], peers[k - 1])
            for k in range(1, 8)
        ]
        for copy in copies:
            copy.start()
        return copies

    cols = exchange(wsend, wgot, cols_send, cols_recv)
    line = LineGather(xall, line_send, line_recv)
    line.begin()
    wgot[dp] = wsend[dp]
    for j in range(8):
        for part in range(2):
            start = part * FF + j * 384
            esend[j, :, part * 384 : (part + 1) * 384] = w_exp_ref[:, start : start + 384]
    for copy in cols:
        copy.wait_recv()
    win_ref[x, y] = wgot[:, :, 0:IN_COLS].reshape(64, IN_COLS).astype(BF)
    own_gains = wgot[:, 0, IN_COLS:]
    gbuf[x, y, :, 0:128] = own_gains
    gbuf[x, y, :, 128:256] = own_gains
    plane_g = PlaneGather(gbuf, g_send, g_recv)
    plane_w = PlaneGather(win_ref, win_send, win_recv)
    plane_o = PlaneGather(wout_all, o_send, o_recv)
    plane_e = PlaneGather(wexp, e_send, e_recv)
    plane_r = PlaneGather(wred_all, r_send, r_recv)
    plane_g.begin()
    plane_w.begin()
    ecols = exchange(esend, egot, ec_send, ec_recv)
    egot[dp] = esend[dp]

    def tables(block, carry):
        token_tables(block, lengths, freq_ref, table, q_ref, k_ref, v_ref)
        return carry

    plane_g.pass_on()
    plane_w.pass_on()
    plane_o.begin()
    plane_r.begin()
    lax.fori_loop(0, 4, tables, 0)
    line.pass_on()
    line_y = LineGather(dy_all, y_send, y_recv)
    line_y.begin()
    plane_g.end()
    gains = spread_gains(gbuf)
    gain_ref[0:8, :] = jnp.broadcast_to(gains, (8, 2304))
    moved = jnp.zeros((8, D), F32)
    for term in in_three(gain_ref[0:8, 0:D]):
        moved += dot(term.astype(BF), perm[...])
    gain_ref[8:16, 0:D] = moved
    first = jnp.where(lax.broadcasted_iota(jnp.int32, (8, 128), 0) == 0, 1.0, 0.0)
    column = lax.dot_general(
        moved, first, (((0,), (0,)), ((), ())), precision=lax.Precision.HIGHEST, preferred_element_type=F32
    )[:, 0:1]
    plane_w.end()
    weight[...] = (win_ref[...].reshape(D, IN_COLS).astype(F32) * column).astype(BF)
    outs = []

    def write(src, dst, sem):
        copy = pltpu.make_async_copy(src, dst, sem)
        copy.start()
        outs.append(copy)

    write(weight, win_out, w_sem.at[0])
    lax.fori_loop(4, 8, tables, 0)

    def chip(offset):
        chip_at = lax.rem(z + offset, 4)
        rows = chip_rows(chip_at)
        qkv = dot(xall[pl.ds(chip_at * 2, 2)].reshape(512, D), weight[...])
        raw[rows, :] = qkv[:, 0:384]
        cos, sin = both_tables(table[rows, :])
        for part in range(3):
            u = qkv[:, part * HD : (part + 1) * HD]
            start = 2 * D + (HD if part == 2 else 0)
            u = u * normed_rows(u) * gain_ref[0:1, start : start + HD]
            u = (u * cos + pltpu.roll(u, HD // 2, 1) * sin).astype(BF)
            if part < 2:
                q_ref[rows, part * HD : (part + 1) * HD] = u
            else:
                k_ref[rows, 0:HD] = u
        v_ref[rows, 0:HD] = qkv[:, 384:512].astype(BF)

    def write_chip(offset):
        chip_at = lax.rem(z + offset, 4)
        rows = chip_rows(chip_at)
        blocks = pl.ds(chip_at * 2, 2)
        write(xall.at[blocks], a_out.at[blocks], out_sem.at[6 * offset])
        for n, (ref, out) in enumerate(
            ((raw, raw_out), (q_ref, q_out), (k_ref, k_out), (v_ref, v_out), (table, table_out))
        ):
            write(ref.at[rows, :], out.at[rows, :], out_sem.at[6 * offset + 1 + n])

    line.second()
    line.wait(6)
    chip(0)
    write_chip(0)
    for copy in ecols:
        copy.wait_recv()
    wexp[x, y] = egot[...].reshape(64, EXP_COLS).astype(BF)
    plane_o.pass_on()
    plane_e.begin()
    plane_r.pass_on()
    line.wait(7, 8, 9, 10)

    def near(t, carry):
        chip(1 + 2 * t)
        return carry

    lax.fori_loop(0, 2, near, 0)
    write_chip(1)
    write_chip(3)
    line.third()
    line_y.pass_on()
    line.wait(11, 12)
    chip(2)
    write_chip(2)
    plane_o.end()
    write(wout_all, wout_out, w_sem.at[1])
    scatter = LineScatter(parts, took, out_z, in_z, s1_send, s1_recv)
    wout = wout_all[...].reshape(256, D)

    def attend(t, carry):
        pair = t // 2
        offset = jnp.where(pair == 0, 2, jnp.where(pair == 1, 1, jnp.where(pair == 2, 3, 0)))
        second = lax.rem(t, 2)
        block = lax.rem(z + offset, 4) * 2 + jnp.where(second == 1, core, 1 - core)
        attend_block(block, q_ref, k_ref, v_ref, o_ref, lse_ref, acc, qs)
        parts[offset, second] = dot(o_ref[block_rows(block), :], wout).astype(BF).reshape(2, 128, D)

        @pl.when(second == 0)
        def _():
            scatter.give_at(offset)

        @pl.when(t == 0)
        def _():
            line_y.second()
            plane_e.pass_on()

        @pl.when(t == 1)
        def _():
            scatter.far()

        @pl.when(t == 3)
        def _():
            scatter.near_right()
            line_y.third()

        @pl.when(t == 5)
        def _():
            scatter.near_left()
            scatter.last_right()

        @pl.when(t == 6)
        def _():
            scatter.last_left()

        return carry

    lax.fori_loop(0, 8, attend, 0)
    write(o_ref, o_out, w_sem.at[2])
    write(lse_ref, lse_out, w_sem.at[3])
    first, second = scatter.result()
    hid_ref[...] = x_ref[...].astype(F32) + jnp.concatenate([first, second], axis=0)
    gain = gain_ref[0:1, D : 2 * D]
    write(hid_ref, hid_out, w_sem.at[5])
    hid = hid_ref[...]
    b = (hid * normed_rows(hid) * gain).astype(BF)
    ball[dp] = dot(b, perm[...]).astype(BF).reshape(2, 128, D)
    line_b = LineGather(ball, b_send, b_recv)
    line_b.begin()
    plane_r.end()
    wred[...] = wred_all[...].astype(F32)[:, :, 0:24, :].reshape(half, D).astype(BF)
    plane_e.end()
    line_y.wait(6, 7, 8, 9, 10, 11, 12)
    scatter.sent()
    scatter2 = LineScatter(parts, took, out_z, in_z, s2_send, s2_recv)

    def mlp(t, carry):
        offset = jnp.where(t == 0, 0, jnp.where(t == 1, 1, jnp.where(t == 2, 3, 2)))
        chip = lax.rem(z + offset, 4)
        rows = chip_rows(chip)
        both = pl.ds(chip * 2, 2)

        @pl.when(t == 0)
        def _():
            line_b.wait(6)

        @pl.when(t == 1)
        def _():
            line_b.pass_on()
            line_b.second()
            line_b.wait(7, 8, 9, 10)

        @pl.when(t == 3)
        def _():
            line_b.third()
            line_b.wait(11, 12)

        weight = wexp[...].reshape(D, EXP_COLS)
        gu = dot(ball[both].reshape(512, D), weight)
        gate, up = gu[:, :half], gu[:, half:]
        sig = 1.0 / (1.0 + jnp.exp(-gate))
        silu = gate * sig
        act_ref[rows, :] = (silu * up).astype(BF)

        @pl.when(t == 2)
        def _():
            scatter2.near_right()

        @pl.when(t == 3)
        def _():
            scatter2.near_left()

        d_act = dot_t(dy_all[both].reshape(512, D), wred[...])
        dgu[rows, 0:half] = (d_act * up * (sig * (1.0 + gate * (1.0 - sig)))).astype(BF)
        dgu[rows, half:] = (d_act * silu).astype(BF)
        for own in (0, 1):
            mine = block_rows(chip * 2 + (core if own else 1 - core))
            parts[offset, own] = dot_t(dgu[mine, :], weight).astype(BF).reshape(2, 128, D)
            if not own:
                scatter2.give_at(offset)
        return carry

    lax.fori_loop(0, 4, mlp, 0)
    scatter2.far()
    gred_ref[...] = jnp.concatenate(
        [
            t_dot(act_ref[...], dy_all[...].reshape(2048, D)).reshape(4, 4, 24, D),
            jnp.zeros((4, 4, 8, D), F32),
        ],
        axis=2,
    ).astype(BF)

    line.sent()
    for copy in outs:
        copy.wait()
    outs.clear()
    write(gred_ref, gred_out, w_sem.at[6])

    def outcome(offset, carry):
        chip = lax.rem(z + offset, 4)
        y_part = dot(act_ref[chip_rows(chip), :], wred[...]).astype(BF).reshape(2, 2, 128, D)
        xall[offset * 2 + core] = y_part[1]
        xall[offset * 2 + 1 - core] = y_part[0]
        return carry

    lax.fori_loop(0, 4, outcome, 0)
    write(xall, yparts_out, w_sem.at[4])
    scatter2.last()
    gexp_ref[...] = t_dot(ball[...].reshape(2048, D), dgu[...]).astype(BF).reshape(4, 4, 64, EXP_COLS)
    write(gexp_ref, gexp_out, w_sem.at[7])
    first, second = scatter2.result()
    d_b = unorder(jnp.concatenate([first, second], axis=0), perm[...])
    hid = hid_ref[...]
    r = normed_rows(hid)
    dgain_ref[...] = jnp.broadcast_to(jnp.sum(d_b * hid * r, axis=0, keepdims=True), (8, D))
    dhid_ref[...] = dy_own[...].astype(F32) + rms_back(hid, r, d_b * gain)
    for one in (line_y, line_b, plane_g, plane_w, plane_o, plane_e, plane_r, scatter2):
        one.sent()
    for copy in cols + ecols:
        copy.wait_send()
    for copy in outs:
        copy.wait()


def first(*args):
    sh = jax.ShapeDtypeStruct
    held = [
        ((8, 2, 128, D), BF),
        ((2048, 384), F32),
        ((2048, 384), BF),
        ((2048, 256), BF),
        ((2048, 256), BF),
        ((2048, 128), F32),
    ]
    weight = ((D, IN_COLS), BF)
    wout = ((4, 4, 16, D), BF)
    early = [((256, D), F32), ((4, 4, RED_ROWS, D), BF), ((4, 4, 64, EXP_COLS), BF)]
    later = [((2048, 256), BF), ((2048, 128), F32)]
    return pl.pallas_call(
        first_kernel,
        out_shape=tuple(sh(*one) for one in held + [weight, wout] + later + held[:1])
        + tuple(sh(*one) for one in early)
        + (sh((16, 2304), F32), sh((256, D), F32), sh((8, D), F32)),
        in_specs=[VMEM] * 8 + [pl.BlockSpec(memory_space=pltpu.SMEM)],
        out_specs=[HBM] * 14 + [VMEM] * 3,
        scratch_shapes=[
            pltpu.VMEM(*one) for one in early + held + [((4, 4, 64, IN_COLS), BF), wout, weight] + later
        ]
        + [
            pltpu.VMEM((2048, FF // 8), BF),
            pltpu.VMEM((FF // 8, D), BF),
            pltpu.VMEM((8, 2, 128, D), BF),
            pltpu.VMEM((8, 8, IN_COLS + 128), F32),
            pltpu.VMEM((8, 8, IN_COLS + 128), F32),
            pltpu.VMEM((8, 8, EXP_COLS), F32),
            pltpu.VMEM((8, 8, EXP_COLS), F32),
            pltpu.VMEM((4, 4, 8, 256), F32),
            pltpu.VMEM((D, D), BF),
            pltpu.VMEM((2 * BLOCK, 256), F32),
            pltpu.VMEM((2 * BLOCK, 256), BF),
            pltpu.VMEM((4, 4, 64, EXP_COLS), BF),
            pltpu.VMEM((4, 4, RED_ROWS, D), BF),
            pltpu.VMEM((8, 2, 128, D), BF),
            pltpu.VMEM((2048, EXP_COLS), BF),
        ]
        + line_scatter_scratch(128, D)[:4]
        + [
            pltpu.SemaphoreType.DMA((n,))
            for n in (13, 13, 7, 7, 7, 7, 12, 12, 12, 12, 12, 12, 13, 13, 12, 12, 12, 12, 10, 10, 13, 13, 10, 10, 24, 8)
        ],
        compiler_params=pltpu.CompilerParams(
            collective_id=1, has_side_effects=True, vmem_limit_bytes=60 * 2**20
        ),
        name="first",
    )(*args)


def attend_back_block(
    i, q_ref, k_ref, v_ref, o_ref, lse_ref, do_ref,
    dk_ref, dv_ref, qs, dos, dqa,
):
    rows = block_rows(i)
    lane = lax.broadcasted_iota(jnp.int32, (BLOCK, HD), 1)
    for h in range(2):
        part = slice(h * BLOCK, (h + 1) * BLOCK)
        cols = slice(h * HD, (h + 1) * HD)
        qs[part, 0:HD] = q_ref[rows, cols]
        extra = q_ref[rows, 2 * HD :].astype(F32)
        for k, term in enumerate(in_three(lse_ref[rows, h : h + 1])):
            extra = jnp.where(lane == 4 + k, -term, extra)
        qs[part, HD:] = extra.astype(BF)
        d = do_ref[:, cols]
        dos[part, 0:HD] = d
        inner = jnp.sum(d.astype(F32) * o_ref[rows, cols].astype(F32), axis=1, keepdims=True)
        extra = jnp.zeros((BLOCK, HD), F32)
        for k, term in enumerate(in_three(inner)):
            extra = jnp.where(lane == k, -term, extra)
        dos[part, HD:] = extra.astype(BF)

    def step(kr, diagonal):
        p = jnp.exp2(dot_t(k_ref[kr, :], qs[...]) * SCORE)
        if diagonal:
            index = lax.broadcasted_iota(jnp.int32, (BLOCK, 2 * BLOCK), 0)
            query = lax.broadcasted_iota(jnp.int32, (BLOCK, 2 * BLOCK), 1) & (BLOCK - 1)
            p = jnp.where(index <= query, p, 0.0)
        ds = (p * dot_t(v_ref[kr, :], dos[...])).astype(BF)
        dv_ref[kr, :] += dot(p.astype(BF), dos[:, 0:HD])
        dk_ref[kr, :] += dot(ds, qs[:, 0:HD])
        dq = t_dot(ds, k_ref[kr, 0:HD])
        if diagonal:
            dqa[...] = dq
        else:
            dqa[...] += dq

    step(rows, True)

    def wide(j, carry):
        step(wide_rows(j), False)
        return carry

    def narrow(j, carry):
        step(block_rows(j), False)
        return carry

    lax.fori_loop(0, i // 2, wide, 0)
    lax.fori_loop(i // 2 * 2, i, narrow, 0)


def from_received(got, out, parts):
    col = 0
    for start, width in parts:
        for j in range(8):
            out[:, start + j * width : start + (j + 1) * width] = got[j, :, col : col + width]
        col += width


def back_kernel(
    wout_ref, gain_ref, dhid, dmid_ref,
    pred_in, pexp_in, q_in, k_in, v_in, o_in, lse_in, weight_in, yparts, raw_in, table_in, a_in, hid_in, x_in,
    y_ref, dx_ref, gred_ref, gout_ref, gin_out, gexp_out, dgain_ref,
    pred_ref, pexp_ref, q_ref, k_ref, v_ref, o_ref, lse_ref, weight, raw, table, hid, x_ref,
    qs, dos, dqa, dk_ref, dv_ref, dqkv, acc, column, parts_q, parts_kv, pout, perm, datt, do_ref,
    gin, gexp, csend, cgot, esend, egot, gsum, gdp, gx, gy,
    *rest,
):
    z, core, x, y = place()
    dp = lax.axis_index("dp")
    peers = dp_peers()
    greet(peers + plane_peers())
    parts = (parts_q, parts_kv)
    datt[dp] = dhid[...].astype(BF).reshape(2, 128, D)
    (ykeep, ytook, y_out, y_in, ys, yr), rest = rest[:6], rest[6:]
    (d_parts, took, out_z, in_z, ss, sr), rest = rest[:6], rest[6:]
    planes = [
        PlaneScatter(part, *rest[5 * n : 5 * n + 5])
        for n, part in enumerate((pred_ref, pexp_ref, pout, *parts))
    ]
    plane_out, plane_q, plane_kv = planes[2:]
    planes = planes[:2]
    c_send, c_recv, e_send, e_recv, g_send, g_recv, d_send, d_recv, in_sem = rest[25:]
    scatter = LineScatter(d_parts, took, out_z, in_z, ss, sr)
    y_scatter = LineScatter(yparts, ytook, y_out, y_in, ys, yr, ykeep)
    line = ChipGather(datt, d_send, d_recv)
    fetched = [
        pltpu.make_async_copy(src, dst, in_sem.at[n])
        for n, (src, dst) in enumerate(
            (
                (pred_in, pred_ref),
                (pexp_in, pexp_ref),
                (q_in, q_ref),
                (k_in, k_ref),
                (v_in, v_ref),
                (o_in, o_ref),
                (lse_in, lse_ref),
                (raw_in, raw),
                (table_in, table),
                (weight_in, weight),
                (yparts.at[:, 1], ykeep),
                (hid_in, hid),
                (x_in, x_ref),
            )
        )
    ]
    again = pltpu.make_async_copy(a_in, datt, in_sem.at[13])
    wout = wout_ref[...].reshape(256, D)
    for copy in fetched:
        copy.start()
    meet(peers + plane_peers())
    line.begin()
    for n in (0, 1):
        fetched[n].wait()
        planes[n].begin()
    dk_ref[...] = jnp.zeros_like(dk_ref)
    dv_ref[...] = jnp.zeros_like(dv_ref)
    gsum[...] = jnp.zeros_like(gsum)
    for copy in fetched[2:7]:
        copy.wait()

    def exchange(src, dst, send, recv):
        return [
            remote(src.at[lax.rem(dp + k, 8)], dst.at[dp], send.at[k - 1], recv.at[k - 1], peers[k - 1])
            for k in range(1, 8)
        ]

    ecols = exchange(esend, egot, e_send, e_recv)

    def through_norm(rows, part, d, tables):
        cos, sin = tables
        cols = slice(part * HD, (part + 1) * HD)
        u = raw[rows, cols]
        start = 2 * D + (HD if part == 2 else 0)
        gain = gain_ref[0:1, start : start + HD]
        d = d * HD**-0.5
        d = d * cos + pltpu.roll(d * sin, HD // 2, 1)
        r = normed_rows(u)
        row = 16 + part // 2
        gsum[row : row + 1, :] += jnp.sum(d * u * r, axis=0, keepdims=True)
        dqkv[rows, cols] = rms_back(u, r, d * gain).astype(BF)

    first = jnp.where(lax.broadcasted_iota(jnp.int32, (8, 128), 0) == 0, 1.0, 0.0)
    column[...] = lax.dot_general(
        gain_ref[8:16, 0:D],
        first,
        (((0,), (0,)), ((), ())),
        precision=lax.Precision.HIGHEST,
        preferred_element_type=F32,
    )

    def block(t, carry):
        offset = jnp.where(t < 2, 0, jnp.where(t >= 6, 2, jnp.where(lax.rem(t, 2) == 0, 1, 3)))
        second = jnp.where((t >= 2) & (t < 6), jnp.where(t >= 4, 1, 0), lax.rem(t, 2))
        i = lax.rem(z + offset, 4) * 2 + second

        @pl.when(t == 2)
        def _():
            line.first()

        @pl.when(t == 3)
        def _():
            for k in (2, 1, 3, 0):
                y_scatter.give(k)

        @pl.when(t == 4)
        def _():
            line.second()

        @pl.when(t == 6)
        def _():
            line.third()
            pout[...] = t_dot(o_ref[...], datt[...].reshape(2048, D)).astype(BF).reshape(4, 4, 16, D)
            plane_out.begin()

        rows = block_rows(i)
        do_ref[...] = dot_t(datt[i].reshape(256, D), wout).astype(BF)

        @pl.when(t == 7)
        def _():
            line.sent()
            again.start()

        attend_back_block(i, q_ref, k_ref, v_ref, o_ref, lse_ref, do_ref, dk_ref, dv_ref, qs, dos, dqa)
        @pl.when(t == 0)
        def _():
            for copy in fetched[7:]:
                copy.wait()

        tables = both_tables(table[rows, :])
        for part in range(2):
            through_norm(rows, part, dqa[part * BLOCK : (part + 1) * BLOCK, :], tables)

        @pl.when(t == 4)
        def _():
            y_scatter.far()
            y_scatter.near()

        @pl.when(t == 6)
        def _():
            y_scatter.last()

        @pl.when(t == 7)
        def _():
            again.wait()
            grad_columns(0)
            plane_q.begin()

        return carry

    def grad_columns(side):
        cols = slice(side * 256, side * 256 + 256)
        acc[...] = t_dot(datt[...].reshape(2048, D), dqkv[:, cols])
        parts[side][...] = (acc[...] * column[:, 0:1]).astype(BF).reshape(4, 4, 64, 256)
        inner = jnp.sum(acc[...] * weight[:, cols].astype(F32), axis=1, keepdims=True)
        if side == 0:
            column[:, 1:2] = inner
        return inner

    lax.fori_loop(0, 8, block, 0)

    def to_input(t, carry):
        offset = jnp.where(t == 0, 2, jnp.where(t == 1, 1, jnp.where(t == 2, 3, 0)))
        for own in (0, 1):
            rows = block_rows(lax.rem(z + offset, 4) * 2 + (core if own else 1 - core))
            through_norm(rows, 2, dk_ref[rows, :], both_tables(table[rows, :]))
            dqkv[rows, 384:512] = dv_ref[rows, :].astype(BF)
            d_parts[offset, own] = dot_t(dqkv[rows, :], weight[...]).astype(BF).reshape(2, 128, D)
            if not own:
                scatter.give_at(offset)

        @pl.when(t == 0)
        def _():
            scatter.far()

        @pl.when(t == 1)
        def _():
            scatter.near_right()

        @pl.when(t == 2)
        def _():
            scatter.near_left()

        return carry

    lax.fori_loop(0, 4, to_input, 0)
    inner = grad_columns(1) + column[:, 1:2]
    plane_kv.begin()
    plane_q.pass_on()
    for plane in planes:
        plane.pass_on()
    fill_order(perm)
    d_in = jnp.zeros((128, D), F32)
    for term in in_three(jnp.broadcast_to(inner, (D, 128))):
        d_in += lax.dot_general(
            term.astype(BF), perm[...], (((0,), (1,)), ((), ())), preferred_element_type=F32
        )
    d_in = d_in[0:1, :] * (1.0 / gain_ref[0:1, 0:D])
    for k in range(8):
        gsum[k : k + 1, :] = d_in[:, k * 128 : (k + 1) * 128]
        gsum[8 + k : 9 + k, :] = dmid_ref[0:1, k * 128 : (k + 1) * 128]
    dp_copies = [
        remote(gsum, gdp.at[k - 1], g_send.at[k - 1], g_recv.at[k - 1], peers[k - 1]) for k in range(1, 8)
    ]
    for copy in dp_copies:
        copy.start()

    scatter.last()
    plane_out.pass_on()
    planes[1].end(gexp)
    for j in range(8):
        esend[j] = gexp[8 * j : 8 * j + 8, :]
    egot[dp] = esend[dp]
    for copy in ecols:
        copy.start()

    def send_columns(plane, side):
        plane.end(gin)
        for j in range(8):
            csend[side, j] = gin[8 * j : 8 * j + 8, :]
        copies = exchange(csend.at[side], cgot.at[side], c_send.at[side], c_recv.at[side])
        for copy in copies:
            copy.start()
        cgot[side, dp] = csend[side, dp]
        return copies

    cols = send_columns(plane_q, 0)
    for copy in dp_copies:
        copy.wait_recv()
    total = gsum[...]
    for k in range(7):
        total += gdp[k]
    gx[0] = total
    x_copies = [
        remote(gx.at[0], gx.at[k], g_send.at[6 + k], g_recv.at[6 + k], device(z, core, x + k, y)) for k in (1, 2, 3)
    ]
    for copy in x_copies:
        copy.start()
    first, second = y_scatter.result()
    y_ref[...] = (hid[...] + jnp.concatenate([first, second], axis=0)).astype(BF)
    planes[0].end(gred_ref)
    plane_kv.pass_on()
    for copy in x_copies:
        copy.wait_recv()
    gy[0] = gx[0] + gx[1] + gx[2] + gx[3]
    y_copies = [
        remote(gy.at[0], gy.at[k], g_send.at[9 + k], g_recv.at[9 + k], device(z, core, x, y + k)) for k in (1, 2, 3)
    ]
    for copy in y_copies:
        copy.start()
    plane_out.end(gout_ref)
    for copy in ecols:
        copy.wait_recv()
    from_received(egot, gexp_out, ((0, 384), (FF, 384)))
    cols += send_columns(plane_kv, 1)
    first, second = scatter.result()
    d_a = unorder(jnp.concatenate([first, second], axis=0), perm[...])
    values = x_ref[...].astype(F32)
    dx_ref[...] = dhid[...] + rms_back(values, normed_rows(values), d_a)
    for copy in y_copies:
        copy.wait_recv()
    dgain_ref[...] = gy[0] + gy[1] + gy[2] + gy[3]
    for copy in cols:
        copy.wait_recv()
    from_received(cgot.at[0], gin_out, ((0, 256),))
    from_received(cgot.at[1], gin_out, ((H * HD, 128), ((H + KV) * HD, 128)))
    for copy in dp_copies + x_copies + y_copies + cols + ecols:
        copy.wait_send()
    for one in [scatter, y_scatter, plane_q, plane_kv, plane_out] + planes:
        one.sent()


def back(*args):
    sh = jax.ShapeDtypeStruct
    return pl.pallas_call(
        back_kernel,
        out_shape=(
            sh((256, D), BF),
            sh((256, D), F32),
            sh((RED_ROWS, D), F32),
            sh((16, D), F32),
            sh((8, 4096), F32),
            sh((8, 2 * FF), F32),
            sh((24, 128), F32),
        ),
        in_specs=[VMEM] * 4 + [HBM] * 14,
        out_specs=[VMEM] * 7,
        scratch_shapes=[
            pltpu.VMEM((4, 4, RED_ROWS, D), BF),
            pltpu.VMEM((4, 4, 64, EXP_COLS), BF),
            pltpu.VMEM((2048, 384), BF),
            pltpu.VMEM((2048, 256), BF),
            pltpu.VMEM((2048, 256), BF),
            pltpu.VMEM((2048, 256), BF),
            pltpu.VMEM((2048, 128), F32),
            pltpu.VMEM((D, IN_COLS), BF),
            pltpu.VMEM((2048, 384), F32),
            pltpu.VMEM((2048, 128), F32),
            pltpu.VMEM((256, D), F32),
            pltpu.VMEM((256, D), BF),
            pltpu.VMEM((2 * BLOCK, 256), BF),
            pltpu.VMEM((2 * BLOCK, 256), BF),
            pltpu.VMEM((2 * BLOCK, HD), F32),
            pltpu.VMEM((2048, HD), F32),
            pltpu.VMEM((2048, HD), F32),
            pltpu.VMEM((2048, IN_COLS), BF),
            pltpu.VMEM((D, 256), F32),
            pltpu.VMEM((D, 128), F32),
            pltpu.VMEM((4, 4, 64, 256), BF),
            pltpu.VMEM((4, 4, 64, 256), BF),
            pltpu.VMEM((4, 4, 16, D), BF),
            pltpu.VMEM((D, D), BF),
            pltpu.VMEM((8, 2, 128, D), BF),
            pltpu.VMEM((BLOCK, 256), BF),
            pltpu.VMEM((64, 256), F32),
            pltpu.VMEM((64, EXP_COLS), F32),
            pltpu.VMEM((2, 8, 8, 256), F32),
            pltpu.VMEM((2, 8, 8, 256), F32),
            pltpu.VMEM((8, 8, EXP_COLS), F32),
            pltpu.VMEM((8, 8, EXP_COLS), F32),
            pltpu.VMEM((24, 128), F32),
            pltpu.VMEM((7, 24, 128), F32),
            pltpu.VMEM((4, 24, 128), F32),
            pltpu.VMEM((4, 24, 128), F32),
        ]
        + [pltpu.VMEM((4, 2, 128, D), BF)]
        + line_scatter_scratch(128, D)[1:]
        + line_scatter_scratch(128, D)
        + plane_scatter_scratch(RED_ROWS, D)
        + plane_scatter_scratch(64, EXP_COLS)
        + plane_scatter_scratch(16, D)
        + plane_scatter_scratch(64, 256)
        + plane_scatter_scratch(64, 256)
        + [pltpu.SemaphoreType.DMA((2, 7)), pltpu.SemaphoreType.DMA((2, 7))]
        + [pltpu.SemaphoreType.DMA((n,)) for n in (7, 7, 13, 13, 13, 13, 14)],
        compiler_params=pltpu.CompilerParams(
            collective_id=3, has_side_effects=True, vmem_limit_bytes=60 * 2**20
        ),
        name="back",
    )(*args)


def update_kernel(*refs):
    weights, grads, firsts, seconds = (refs[5 * n : 5 * n + 5] for n in range(4))
    y_ref, dx_ref, y_out, dx_out = refs[20:24]
    news, means, squares = (refs[24 + 5 * n : 29 + 5 * n] for n in range(3))
    y_out[...] = y_ref[...]
    dx_out[...] = dx_ref[...]
    for k in range(4):
        news[k][...], means[k][...], squares[k][...] = adam_step(
            weights[k][...],
            grads[k][0 : weights[k].shape[0], :],
            firsts[k][...],
            seconds[k][...],
            matrix_rate,
            matrix_decay,
        )
    own = weights[4].shape[1]
    first = (lax.axis_index("dp") * 16 + lax.axis_index("shard")) * own
    row, col = first // 128, lax.rem(first, 128)
    lane = lax.broadcasted_iota(jnp.int32, (8, 128), 1)
    here = pltpu.roll(jnp.broadcast_to(grads[4][pl.ds(row, 1), :], (8, 128)), lax.rem(128 - col, 128), 1)
    after = pltpu.roll(jnp.broadcast_to(grads[4][pl.ds(row + 1, 1), :], (8, 128)), lax.rem(128 - col, 128), 1)
    grad = jnp.where(lane < 128 - col, here, after)[0:1, 0:own]
    news[4][...], means[4][...], squares[4][...] = adam_step(
        weights[4][...], grad, firsts[4][...], seconds[4][...], gain_rate, 0.0
    )


def update(weights, grads, firsts, seconds, y, dx):
    like = tuple(jax.ShapeDtypeStruct(w.shape, F32) for w in weights)
    return pl.pallas_call(
        update_kernel,
        out_shape=(jax.ShapeDtypeStruct(y.shape, BF), jax.ShapeDtypeStruct(dx.shape, F32)) + like * 3,
        in_specs=[VMEM] * 22,
        out_specs=[VMEM] * 17,
        compiler_params=pltpu.CompilerParams(vmem_limit_bytes=60 * 2**20),
        name="update",
    )(*weights, *grads, *firsts, *seconds, y, dx)


def body(
    tokens,
    cotangent,
    lengths,
    weight_input,
    weight_output,
    weight_expand,
    weight_reduce,
    gains,
    first_input,
    first_output,
    first_expand,
    first_reduce,
    first_gains,
    second_input,
    second_output,
    second_expand,
    second_reduce,
    second_gains,
):
    a, raw, q, k, v, table, win, wout, o, lse, y_parts, hid, part_red, part_exp, gain, d_hid, d_gain_mid = first(
        tokens[0],
        weight_input,
        weight_expand,
        gains[None],
        rope_rates(),
        weight_output,
        weight_reduce,
        cotangent[0],
        lengths,
    )
    block_out, input_grad, grad_reduce, grad_output, grad_input, grad_expand, grad_gains = back(
        wout, gain, d_hid, d_gain_mid, part_red, part_exp,
        q, k, v, o, lse, win, y_parts.reshape(4, 2, 2, 128, D), raw, table, a, hid, tokens[0],
    )
    block_out, input_grad, *done = update(
        (weight_input, weight_output, weight_expand, weight_reduce, gains[None]),
        (grad_input, grad_output, grad_expand, grad_reduce, grad_gains),
        (first_input, first_output, first_expand, first_reduce, first_gains[None]),
        (second_input, second_output, second_expand, second_reduce, second_gains[None]),
        block_out,
        input_grad,
    )
    done = [one[0] if n % 5 == 4 else one for n, one in enumerate(done)]
    return (block_out[None], input_grad[None], *done)


def solution(mesh):
    placed = (
        P("shard", "dp", None),
        P("shard", "dp", None),
        P("shard", None),
        P(("dp", "shard"), None),
        P(("dp", "shard"), None),
        P(("dp", "shard"), None),
        P(("dp", "shard"), None),
        P(("dp", "shard")),
        P(("dp", "shard"), None),
        P(("dp", "shard"), None),
        P(("dp", "shard"), None),
        P(("dp", "shard"), None),
        P(("dp", "shard")),
        P(("dp", "shard"), None),
        P(("dp", "shard"), None),
        P(("dp", "shard"), None),
        P(("dp", "shard"), None),
        P(("dp", "shard")),
    )
    return jax.shard_map(
        body,
        mesh=mesh,
        in_specs=placed,
        out_specs=(
            P("shard", "dp", None),
            P("shard", "dp", None),
            P(("dp", "shard"), None),
            P(("dp", "shard"), None),
            P(("dp", "shard"), None),
            P(("dp", "shard"), None),
            P(("dp", "shard")),
            P(("dp", "shard"), None),
            P(("dp", "shard"), None),
            P(("dp", "shard"), None),
            P(("dp", "shard"), None),
            P(("dp", "shard")),
            P(("dp", "shard"), None),
            P(("dp", "shard"), None),
            P(("dp", "shard"), None),
            P(("dp", "shard"), None),
            P(("dp", "shard")),
        ),
        check_vma=False,
    )
```

```python
import math

import jax
import jax.numpy as jnp
import numpy as np
from jax import lax
from jax.experimental import pallas as pl
from jax.experimental.pallas import tpu as pltpu
from jax.sharding import PartitionSpec as P

D = 1024
H = 16
KV = 8
HD = 128
FF = 3072
STEP = 10


norm_eps = 1e-06
rope_base = 1000000.0
beta_one = 0.9
beta_two = 0.95
adam_eps = 1e-08
matrix_rate = 0.1
gain_rate = 0.5
matrix_decay = 0.1
masked_score = -1e30


def adam_step(weight, grad, first, second, rate, decay):
    first_new = beta_one * first + (1.0 - beta_one) * grad
    second_new = beta_two * second + (1.0 - beta_two) * grad * grad
    fix_one = 1.0 - beta_one**STEP
    fix_two = 1.0 - beta_two**STEP
    direction = first_new / fix_one / (jnp.sqrt(second_new / fix_two) + adam_eps)
    return (weight - rate * (direction + decay * weight), first_new, second_new)


MESH = pl.DeviceIdType.MESH
F32 = jnp.float32
BF = jnp.bfloat16
VMEM = pl.BlockSpec(memory_space=pltpu.VMEM)
HBM = pl.BlockSpec(memory_space=pl.ANY)
SCORE = HD**-0.5 * math.log2(math.e)
BLOCK = 256
BIG = 30000.0
IN_COLS = (H + 2 * KV) * HD // 8
EXP_COLS = 2 * FF // 8
RED_ROWS = 32


def dot(a, b):
    return jnp.dot(a, b, preferred_element_type=F32)


def dot_t(a, b):
    return lax.dot_general(a, b, (((1,), (1,)), ((), ())), preferred_element_type=F32)


def t_dot(a, b):
    return lax.dot_general(a, b, (((0,), (0,)), ((), ())), preferred_element_type=F32)


def in_three(values):
    high = values.astype(BF)
    rest = values - high.astype(F32)
    middle = rest.astype(BF)
    return high.astype(F32), middle.astype(F32), (rest - middle.astype(F32)).astype(BF).astype(F32)


def block_rows(i):
    return pl.ds(pl.multiple_of(i * BLOCK, BLOCK), BLOCK)


def wide_rows(i):
    return pl.ds(pl.multiple_of(i * 2 * BLOCK, 2 * BLOCK), 2 * BLOCK)


def chip_rows(i):
    return pl.ds(pl.multiple_of(i * 2 * BLOCK, 2 * BLOCK), 2 * BLOCK)


def place():
    dp = lax.axis_index("dp")
    shard = lax.axis_index("shard")
    return dp // 2, lax.rem(dp, 2), shard // 4, lax.rem(shard, 4)


def device(z, core, x, y):
    return (lax.rem(z, 4) * 2 + core, lax.rem(x, 4) * 4 + lax.rem(y, 4))


def line_peers():
    z, core, x, y = place()
    return [device(z, 1 - core, x, y), device(z + 1, core, x, y), device(z + 3, core, x, y)]


def plane_peers():
    z, core, x, y = place()
    return [device(z, core, x + k, y) for k in (1, 2, 3)] + [
        device(z, core, x, y + k) for k in (1, 2, 3)
    ]


def dp_peers():
    dp = lax.axis_index("dp")
    shard = lax.axis_index("shard")
    return [(lax.rem(dp + k, 8), shard) for k in range(1, 8)]


def greet(peers):
    for peer in peers:
        pl.semaphore_signal(
            pltpu.get_barrier_semaphore(), inc=1, device_id=peer, device_id_type=MESH
        )


def meet(peers):
    pl.semaphore_wait(pltpu.get_barrier_semaphore(), len(peers))


def remote(src, dst, send, recv, peer):
    return pltpu.make_async_remote_copy(
        src_ref=src, dst_ref=dst, send_sem=send, recv_sem=recv, device_id=peer, device_id_type=MESH
    )


class LineGather:
    sems = 13

    def __init__(self, buf, send, recv):
        z, core, x, y = place()
        me, right, far, left = (lax.rem(z + k, 4) * 2 + core for k in range(4))
        to_right, to_left = device(z + 1, core, x, y), device(z + 3, core, x, y)
        sibling = device(z, 1 - core, x, y)
        plan = [
            (me, 0, to_right),
            (me, 1, to_right),
            (left, 0, to_right),
            (me, 1, to_left),
            (me, 0, to_left),
            (right, 1, to_left),
            (me, None, sibling),
            (left, 0, sibling),
            (right, 1, sibling),
            (left, 1, sibling),
            (right, 0, sibling),
            (far, 0, sibling),
            (far, 1, sibling),
        ]
        self.copies = []
        for k, (slot, half, peer) in enumerate(plan):
            ref = buf.at[slot] if half is None else buf.at[slot, half]
            self.copies.append(remote(ref, ref, send.at[k], recv.at[k], peer))

    def start(self, *which):
        for k in which:
            self.copies[k].start()

    def wait(self, *which):
        for k in which:
            self.copies[k].wait_recv()

    def begin(self):
        self.start(6, 0, 3, 1, 4)

    def pass_on(self):
        self.wait(0)
        self.start(2, 7)
        self.wait(3)
        self.start(5, 8)

    def second(self):
        self.wait(1)
        self.start(9)
        self.wait(4)
        self.start(10)

    def third(self):
        self.wait(2)
        self.start(11)
        self.wait(5)
        self.start(12)

    def sent(self):
        for copy in self.copies:
            copy.wait_send()


class ChipGather:
    sems = 13

    def __init__(self, buf, send, recv):
        z, core, x, y = place()
        self.core = core
        chips = [lax.rem(z + k, 4) * 2 for k in range(4)]
        me, right, far, left = chips
        to_right, to_left = device(z + 1, core, x, y), device(z + 3, core, x, y)
        onward = device(z + 1 + 2 * core, core, x, y)
        behind = lax.rem(z + 3 - 2 * core, 4) * 2
        sibling = device(z, 1 - core, x, y)
        plan = [(buf.at[me + core], sibling)]
        for block in (0, 1):
            plan += [(buf.at[me + block, core], to_right), (buf.at[me + block, core], to_left)]
        plan += [(buf.at[behind + block, core], onward) for block in (0, 1)]
        for block in (0, 1):
            plan += [(buf.at[left + block, core], sibling), (buf.at[right + block, core], sibling)]
        plan += [(buf.at[far + block, core], sibling) for block in (0, 1)]
        self.copies = [remote(ref, ref, send.at[k], recv.at[k], peer) for k, (ref, peer) in enumerate(plan)]

    def start(self, *which):
        for k in which:
            self.copies[k].start()

    def wait(self, *which):
        for k in which:
            self.copies[k].wait_recv()

    def begin(self):
        self.start(0)

        @pl.when(self.core == 0)
        def _():
            self.start(1, 2)

        self.wait(0)

        @pl.when(self.core == 1)
        def _():
            self.start(1, 2)

        self.start(3, 4)

    def neighbours(self, block):
        for side in (0, 1):
            self.wait(1 + 2 * block + side)
            self.start(7 + 2 * block + side)

            @pl.when(self.core == side)
            def _():
                self.start(5 + block)

        self.wait(7 + 2 * block, 8 + 2 * block)

    def first(self):
        self.neighbours(0)

    def second(self):
        self.neighbours(1)

    def third(self):
        for block in (0, 1):
            self.wait(5 + block)
            self.start(11 + block)
        self.wait(11, 12)

    def sent(self):
        for copy in self.copies:
            copy.wait_send()


class PlaneGather:
    sems = 12

    def __init__(self, buf, send, recv):
        z, core, x, y = place()
        half = buf.shape[3] // 2
        low, high = pl.ds(0, half), pl.ds(half, half)
        self.copies = []
        refs = (
            (buf.at[x, y, :, low], 0),
            (buf.at[x, y, :, high], 1),
            (buf.at[:, y, :, low], 1),
            (buf.at[x, :, :, high], 0),
        )
        k = 0
        for ref, along_y in refs:
            for step in (1, 2, 3):
                peer = device(z, core, x, y + step) if along_y else device(z, core, x + step, y)
                self.copies.append(remote(ref, ref, send.at[k], recv.at[k], peer))
                k += 1

    def begin(self):
        for k in (0, 3, 1, 4, 2, 5):
            self.copies[k].start()

    def pass_on(self):
        for k in (0, 1, 2):
            self.copies[k].wait_recv()
        for k in (6, 7, 8):
            self.copies[k].start()
        for k in (3, 4, 5):
            self.copies[k].wait_recv()
        for k in (9, 10, 11):
            self.copies[k].start()

    def end(self):
        for k in range(6, 12):
            self.copies[k].wait_recv()

    def sent(self):
        for copy in self.copies:
            copy.wait_send()


class PlaneScatter:
    sems = 12

    def __init__(self, parts, got1, mid, got2, send, recv):
        z, core, x, y = place()
        self.parts, self.got1, self.mid, self.got2 = parts, got1, mid, got2
        half = parts.shape[3] // 2
        self.cols = (pl.ds(0, half), pl.ds(half, half))
        self.x, self.y = x, y
        self.copies = []
        k = 0
        for side in (0, 1):
            for step in (1, 2, 3):
                if side == 0:
                    ref = parts.at[:, lax.rem(y + step, 4), :, self.cols[0]]
                    peer = device(z, core, x, y + step)
                else:
                    ref = parts.at[lax.rem(x + step, 4), :, :, self.cols[1]]
                    peer = device(z, core, x + step, y)
                self.copies.append(remote(ref, got1.at[side, step - 1], send.at[k], recv.at[k], peer))
                k += 1
        for side in (0, 1):
            for step in (1, 2, 3):
                if side == 0:
                    ref = mid.at[0, lax.rem(x + step, 4)]
                    peer = device(z, core, x + step, y)
                else:
                    ref = mid.at[1, lax.rem(y + step, 4)]
                    peer = device(z, core, x, y + step)
                self.copies.append(remote(ref, got2.at[side, step - 1], send.at[k], recv.at[k], peer))
                k += 1

    def begin(self):
        for k in (0, 3, 1, 4, 2, 5):
            self.copies[k].start()

    def pass_on(self):
        for side in (0, 1):
            for k in range(3 * side, 3 * side + 3):
                self.copies[k].wait_recv()
            for j in range(4):
                if side == 0:
                    own = self.parts[j, self.y, :, self.cols[0]]
                else:
                    own = self.parts[self.x, j, :, self.cols[1]]
                total = own.astype(F32)
                for k in range(3):
                    total += self.got1[side, k, j].astype(F32)
                self.mid[side, j] = total.astype(BF)
            for k in range(6 + 3 * side, 9 + 3 * side):
                self.copies[k].start()

    def end(self, out):
        for side in (0, 1):
            for k in range(6 + 3 * side, 9 + 3 * side):
                self.copies[k].wait_recv()
            total = self.mid[side, self.x if side == 0 else self.y].astype(F32)
            for k in range(3):
                total += self.got2[side, k].astype(F32)
            out[:, self.cols[side]] = total

    def sent(self):
        for copy in self.copies:
            copy.wait_send()


def plane_scatter_scratch(rows, width):
    half = width // 2
    return [
        pltpu.VMEM((2, 3, 4, rows, half), BF),
        pltpu.VMEM((2, 4, rows, half), BF),
        pltpu.VMEM((2, 3, rows, half), BF),
        pltpu.SemaphoreType.DMA((12,)),
        pltpu.SemaphoreType.DMA((12,)),
    ]


class LineScatter:
    def __init__(self, parts, took, out_z, in_z, send, recv, kept=None):
        z, core, x, y = place()
        self.parts, self.kept, self.took, self.out_z, self.in_z = parts, kept, took, out_z, in_z
        to_right, to_left = device(z + 1, core, x, y), device(z + 3, core, x, y)
        sibling = device(z, 1 - core, x, y)
        self.exchange = lambda k: remote(parts.at[k, 0], took.at[k], send.at[k], recv.at[k], sibling)
        self.swap = [self.exchange(k) for k in range(4)]
        self.copies = [
            remote(
                out_z.at[k], in_z.at[k], send.at[4 + k], recv.at[4 + k], to_right if k < 3 else to_left
            )
            for k in range(6)
        ]

    def give(self, offset):
        self.swap[offset].start()

    def give_at(self, offset):
        self.exchange(offset).start()

    def take(self, offset):
        self.swap[offset].wait_recv()

    def half(self, offset, part):
        own = self.parts[offset, 1, part] if self.kept is None else self.kept[offset, part]
        return own.astype(F32) + self.took[offset, part].astype(F32)

    def push(self, k, value):
        self.out_z[k] = value.astype(BF)
        self.copies[k].start()

    def far(self):
        self.take(2)
        self.push(0, self.half(2, 0))
        self.push(3, self.half(2, 1))

    def near_right(self):
        self.take(1)
        self.push(1, self.half(1, 1))

    def near_left(self):
        self.take(3)
        self.push(4, self.half(3, 0))

    def near(self):
        self.near_right()
        self.near_left()

    def last_right(self):
        self.copies[0].wait_recv()
        self.push(2, self.half(1, 0) + self.in_z[0].astype(F32))

    def last_left(self):
        self.copies[3].wait_recv()
        self.push(5, self.half(3, 1) + self.in_z[3].astype(F32))

    def last(self):
        self.last_right()
        self.last_left()

    def result(self):
        self.take(0)
        self.copies[1].wait_recv()
        self.copies[4].wait_recv()
        self.copies[2].wait_recv()
        first = self.half(0, 0) + self.in_z[4].astype(F32) + self.in_z[2].astype(F32)
        self.copies[5].wait_recv()
        second = self.half(0, 1) + self.in_z[1].astype(F32) + self.in_z[5].astype(F32)
        return first, second

    def sent(self):
        for copy in self.swap + self.copies:
            copy.wait_send()


def line_scatter_scratch(rows, width):
    return [
        pltpu.VMEM((4, 2, 2, rows, width), BF),
        pltpu.VMEM((4, 2, rows, width), BF),
        pltpu.VMEM((6, rows, width), BF),
        pltpu.VMEM((6, rows, width), BF),
        pltpu.SemaphoreType.DMA((10,)),
        pltpu.SemaphoreType.DMA((10,)),
    ]


def to_send(w_in, gains, out):
    col = 0
    for ref, start, width in ((w_in, 0, 256), (w_in, H * HD, 128), (w_in, (H + KV) * HD, 128)):
        for j in range(8):
            out[j, :, col : col + width] = ref[:, start + j * width : start + (j + 1) * width]
        col += width
    out[:, :, col : col + 128] = jnp.zeros((8, 8, 128), F32)
    for j in range(8):
        out[j, 0:1, col : col + 18] = gains[...]


def spread_gains(gbuf):
    wide = 128 * 18
    held = gbuf[:, :, :, 0:128].reshape(128, 128)
    n = lax.broadcasted_iota(jnp.int32, (128, wide), 1)
    r = lax.broadcasted_iota(jnp.int32, (128, wide), 0)
    nf = n.astype(F32)
    within = nf - 18.0 * jnp.floor((nf + 0.5) * (1.0 / 18.0))
    pick = jnp.where(within == r.astype(F32), 1.0, 0.0)
    spread = jnp.dot(held, pick, precision=lax.Precision.HIGHEST, preferred_element_type=F32)
    first = ((r & 7) * 16 + (r >> 3)) * 18
    return jnp.sum(jnp.where((n >= first) & (n < first + 18), spread, 0.0), axis=0, keepdims=True)


def fill_order(perm):
    def block(i, carry):
        n = lax.broadcasted_iota(jnp.int32, (128, D), 0)
        k = lax.broadcasted_iota(jnp.int32, (128, D), 1)
        goal = (n >> 3) * 64 + i * 8 + (n & 7)
        perm[pl.ds(pl.multiple_of(i * 128, 128), 128), :] = jnp.where(k == goal, 1.0, 0.0).astype(BF)
        return carry

    lax.fori_loop(0, 8, block, 0)


def normed_rows(values):
    return lax.rsqrt(jnp.mean(values * values, axis=-1, keepdims=True) + norm_eps)


def token_tables(block, lengths, freq, table, q_ref, k_ref, v_ref):
    rows = block_rows(block)
    end0 = lengths[0, 0]
    end1 = end0 + lengths[0, 1]
    end2 = end1 + lengths[0, 2]
    token = block * BLOCK + lax.broadcasted_iota(jnp.int32, (BLOCK, HD), 0)
    lane = lax.broadcasted_iota(jnp.int32, (BLOCK, HD), 1)
    start = jnp.where(token >= end2, end2, jnp.where(token >= end1, end1, jnp.where(token >= end0, end0, 0)))
    angle = (token - start).astype(F32) * freq[0:1, :]
    table[rows, :] = jnp.sin(angle + jnp.where(lane < HD // 2, math.pi / 2, 0.0))
    one = lambda test: jnp.where(test, 1, 0)
    segment = one(token >= end0) + one(token >= end1) + one(token >= end2)
    same = segment == lane
    q_ref[rows, 256:384] = jnp.where(lane < 4, jnp.where(same, 0.0, -BIG), 0.0).astype(BF)
    k_ref[rows, 128:256] = jnp.where(lane < 4, jnp.where(same, 1.0, 0.0), jnp.where(lane < 7, 1.0, 0.0)).astype(BF)
    v_ref[rows, 128:256] = jnp.where(lane < 3, 1.0, 0.0).astype(BF)


def both_tables(table):
    lane = lax.broadcasted_iota(jnp.int32, table.shape, 1)
    other = pltpu.roll(table, HD // 2, 1)
    return jnp.where(lane < HD // 2, table, other), jnp.where(lane < HD // 2, -other, table)


def rope_rates():
    half = HD // 2
    rates = np.float32(rope_base) ** (-(2.0 * np.arange(half, dtype=np.float32)) / np.float32(HD))
    return jnp.asarray(np.tile(np.concatenate([rates, rates])[None], (8, 1)), F32)


def attend_block(i, q_ref, k_ref, v_ref, o_ref, lse_ref, acc, qs):
    rows = block_rows(i)
    for h in range(2):
        qs[h * BLOCK : (h + 1) * BLOCK, 0:HD] = q_ref[rows, h * HD : (h + 1) * HD]
        qs[h * BLOCK : (h + 1) * BLOCK, HD:] = q_ref[rows, 2 * HD :]

    query = lax.broadcasted_iota(jnp.int32, (2 * BLOCK, BLOCK), 0) & (BLOCK - 1)
    index = lax.broadcasted_iota(jnp.int32, (2 * BLOCK, BLOCK), 1)
    e = jnp.where(index <= query, jnp.exp2(dot_t(qs[...], k_ref[rows, :]) * SCORE), 0.0)
    acc[...] = dot(e.astype(BF), v_ref[rows, :])

    def step(kr):
        acc[...] += dot(jnp.exp2(dot_t(qs[...], k_ref[kr, :]) * SCORE).astype(BF), v_ref[kr, :])

    def wide(j, carry):
        step(wide_rows(j))
        return carry

    def narrow(j, carry):
        step(block_rows(j))
        return carry

    lax.fori_loop(0, i // 2, wide, 0)
    lax.fori_loop(i // 2 * 2, i, narrow, 0)
    total = acc[:, HD : HD + 1]
    out = acc[:, 0:HD] * (1.0 / total)
    lse = jnp.log2(total) * (1.0 / SCORE)
    for h in range(2):
        part = slice(h * BLOCK, (h + 1) * BLOCK)
        o_ref[rows, h * HD : (h + 1) * HD] = out[part].astype(BF)
        lse_ref[rows, h : h + 1] = lse[part]


def rms_back(h, r, dg):
    return r * dg - h * (r * r * r) * jnp.mean(h * dg, axis=-1, keepdims=True)


def unorder(values, perm):
    high = values.astype(BF)
    low = (values - high.astype(F32)).astype(BF)
    return dot_t(high, perm) + dot_t(low, perm)


def first_kernel(
    x_ref, w_in_ref, w_exp_ref, gains_ref, freq_ref, w_out_ref, w_red_ref, dy_own, lengths,
    a_out, raw_out, q_out, k_out, v_out, table_out, win_out, wout_out, o_out, lse_out, yparts_out,
    hid_out, gred_out, gexp_out, gain_ref, dhid_ref, dgain_ref,
    hid_ref, gred_ref, gexp_ref, xall, raw, q_ref, k_ref, v_ref, table, win_ref, wout_all, weight, o_ref, lse_ref, act_ref, wred, dy_all,
    wsend, wgot, esend, egot, gbuf, perm, acc, qs, wexp, wred_all, ball, dgu,
    parts, took, out_z, in_z,
    line_send, line_recv, cols_send, cols_recv, ec_send, ec_recv, win_send, win_recv, g_send, g_recv,
    o_send, o_recv, y_send, y_recv, e_send, e_recv, r_send, r_recv,
    s1_send, s1_recv, b_send, b_recv, s2_send, s2_recv, out_sem, w_sem,
):
    z, core, x, y = place()
    dp = lax.axis_index("dp")
    half = FF // 8
    peers = dp_peers()
    greet(peers + plane_peers())
    to_send(w_in_ref, gains_ref, wsend)
    fill_order(perm)
    values = x_ref[...].astype(F32)
    normed = (values * normed_rows(values)).astype(BF)
    xall[dp] = dot(normed, perm[...]).astype(BF).reshape(2, 128, D)
    dy_all[dp] = dy_own[...].reshape(2, 128, D)
    wout_all[x, y] = w_out_ref[...].astype(BF)
    wred_all[x, y] = jnp.concatenate([w_red_ref[...], jnp.zeros((8, D), F32)], axis=0).astype(BF)
    meet(peers + plane_peers())

    def exchange(src, dst, send, recv):
        copies = [
            remote(src.at[lax.rem(dp + k, 8)], dst.at[dp], send.at[k - 1], recv.at[k - 1], peers[k - 1])
            for k in range(1, 8)
        ]
        for copy in copies:
            copy.start()
        return copies

    cols = exchange(wsend, wgot, cols_send, cols_recv)
    line = LineGather(xall, line_send, line_recv)
    line.begin()
    wgot[dp] = wsend[dp]
    for j in range(8):
        for part in range(2):
            start = part * FF + j * 384
            esend[j, :, part * 384 : (part + 1) * 384] = w_exp_ref[:, start : start + 384]
    for copy in cols:
        copy.wait_recv()
    win_ref[x, y] = wgot[:, :, 0:IN_COLS].reshape(64, IN_COLS).astype(BF)
    own_gains = wgot[:, 0, IN_COLS:]
    gbuf[x, y, :, 0:128] = own_gains
    gbuf[x, y, :, 128:256] = own_gains
    plane_g = PlaneGather(gbuf, g_send, g_recv)
    plane_w = PlaneGather(win_ref, win_send, win_recv)
    plane_o = PlaneGather(wout_all, o_send, o_recv)
    plane_e = PlaneGather(wexp, e_send, e_recv)
    plane_r = PlaneGather(wred_all, r_send, r_recv)
    plane_g.begin()
    plane_w.begin()
    ecols = exchange(esend, egot, ec_send, ec_recv)
    egot[dp] = esend[dp]

    def tables(block, carry):
        token_tables(block, lengths, freq_ref, table, q_ref, k_ref, v_ref)
        return carry

    plane_g.pass_on()
    plane_w.pass_on()
    plane_o.begin()
    plane_r.begin()
    lax.fori_loop(0, 4, tables, 0)
    line.pass_on()
    line_y = LineGather(dy_all, y_send, y_recv)
    line_y.begin()
    plane_g.end()
    gains = spread_gains(gbuf)
    gain_ref[0:8, :] = jnp.broadcast_to(gains, (8, 2304))
    moved = jnp.zeros((8, D), F32)
    for term in in_three(gain_ref[0:8, 0:D]):
        moved += dot(term.astype(BF), perm[...])
    gain_ref[8:16, 0:D] = moved
    first = jnp.where(lax.broadcasted_iota(jnp.int32, (8, 128), 0) == 0, 1.0, 0.0)
    column = lax.dot_general(
        moved, first, (((0,), (0,)), ((), ())), precision=lax.Precision.HIGHEST, preferred_element_type=F32
    )[:, 0:1]
    plane_w.end()
    weight[...] = (win_ref[...].reshape(D, IN_COLS).astype(F32) * column).astype(BF)
    outs = []

    def write(src, dst, sem):
        copy = pltpu.make_async_copy(src, dst, sem)
        copy.start()
        outs.append(copy)

    write(weight, win_out, w_sem.at[0])
    lax.fori_loop(4, 8, tables, 0)

    def chip(offset):
        chip_at = lax.rem(z + offset, 4)
        rows = chip_rows(chip_at)
        qkv = dot(xall[pl.ds(chip_at * 2, 2)].reshape(512, D), weight[...])
        cos, sin = both_tables(table[rows, :])
        for part in range(3):
            u = qkv[:, part * HD : (part + 1) * HD]
            start = 2 * D + (HD if part == 2 else 0)
            r = normed_rows(u)
            lse_ref[rows, 2 + part : 3 + part] = r
            u = u * r
            raw[rows, part * HD : (part + 1) * HD] = u
            u = u * gain_ref[0:1, start : start + HD]
            u = (u * cos + pltpu.roll(u, HD // 2, 1) * sin).astype(BF)
            if part < 2:
                q_ref[rows, part * HD : (part + 1) * HD] = u
            else:
                k_ref[rows, 0:HD] = u
        v_ref[rows, 0:HD] = qkv[:, 384:512].astype(BF)

    def write_chip(offset):
        chip_at = lax.rem(z + offset, 4)
        rows = chip_rows(chip_at)
        blocks = pl.ds(chip_at * 2, 2)
        write(xall.at[blocks], a_out.at[blocks], out_sem.at[6 * offset])
        for n, (ref, out) in enumerate(
            ((raw, raw_out), (q_ref, q_out), (k_ref, k_out), (v_ref, v_out), (table, table_out))
        ):
            write(ref.at[rows, :], out.at[rows, :], out_sem.at[6 * offset + 1 + n])

    line.second()
    line.wait(6)
    chip(0)
    write_chip(0)
    for copy in ecols:
        copy.wait_recv()
    wexp[x, y] = egot[...].reshape(64, EXP_COLS).astype(BF)
    plane_o.pass_on()
    plane_e.begin()
    plane_r.pass_on()
    line.wait(7, 8, 9, 10)

    def near(t, carry):
        chip(1 + 2 * t)
        return carry

    lax.fori_loop(0, 2, near, 0)
    write_chip(1)
    write_chip(3)
    line.third()
    line_y.pass_on()
    line.wait(11, 12)
    chip(2)
    write_chip(2)
    plane_o.end()
    write(wout_all, wout_out, w_sem.at[1])
    scatter = LineScatter(parts, took, out_z, in_z, s1_send, s1_recv)
    wout = wout_all[...].reshape(256, D)

    def attend(t, carry):
        pair = t // 2
        offset = jnp.where(pair == 0, 2, jnp.where(pair == 1, 1, jnp.where(pair == 2, 3, 0)))
        second = lax.rem(t, 2)
        block = lax.rem(z + offset, 4) * 2 + jnp.where(second == 1, core, 1 - core)
        attend_block(block, q_ref, k_ref, v_ref, o_ref, lse_ref, acc, qs)
        parts[offset, second] = dot(o_ref[block_rows(block), :], wout).astype(BF).reshape(2, 128, D)

        @pl.when(second == 0)
        def _():
            scatter.give_at(offset)

        @pl.when(t == 0)
        def _():
            line_y.second()
            plane_e.pass_on()

        @pl.when(t == 1)
        def _():
            scatter.far()

        @pl.when(t == 3)
        def _():
            scatter.near_right()
            line_y.third()

        @pl.when(t == 5)
        def _():
            scatter.near_left()
            scatter.last_right()

        @pl.when(t == 6)
        def _():
            scatter.last_left()

        return carry

    lax.fori_loop(0, 8, attend, 0)
    write(o_ref, o_out, w_sem.at[2])
    write(lse_ref, lse_out, w_sem.at[3])
    first, second = scatter.result()
    hid_ref[...] = x_ref[...].astype(F32) + jnp.concatenate([first, second], axis=0)
    gain = gain_ref[0:1, D : 2 * D]
    write(hid_ref, hid_out, w_sem.at[5])
    hid = hid_ref[...]
    b = (hid * normed_rows(hid) * gain).astype(BF)
    ball[dp] = dot(b, perm[...]).astype(BF).reshape(2, 128, D)
    line_b = LineGather(ball, b_send, b_recv)
    line_b.begin()
    plane_r.end()
    wred[...] = wred_all[...].astype(F32)[:, :, 0:24, :].reshape(half, D).astype(BF)
    plane_e.end()
    line_y.wait(6, 7, 8, 9, 10, 11, 12)
    scatter.sent()
    scatter2 = LineScatter(parts, took, out_z, in_z, s2_send, s2_recv)

    def mlp(t, carry):
        offset = jnp.where(t == 0, 0, jnp.where(t == 1, 1, jnp.where(t == 2, 3, 2)))
        chip = lax.rem(z + offset, 4)
        rows = chip_rows(chip)
        both = pl.ds(chip * 2, 2)

        @pl.when(t == 0)
        def _():
            line_b.wait(6)

        @pl.when(t == 1)
        def _():
            line_b.pass_on()
            line_b.second()
            line_b.wait(7, 8, 9, 10)

        @pl.when(t == 3)
        def _():
            line_b.third()
            line_b.wait(11, 12)

        weight = wexp[...].reshape(D, EXP_COLS)
        gu = dot(ball[both].reshape(512, D), weight)
        gate, up = gu[:, :half], gu[:, half:]
        sig = 1.0 / (1.0 + jnp.exp(-gate))
        silu = gate * sig
        act_ref[rows, :] = (silu * up).astype(BF)

        @pl.when(t == 2)
        def _():
            scatter2.near_right()

        @pl.when(t == 3)
        def _():
            scatter2.near_left()

        d_act = dot_t(dy_all[both].reshape(512, D), wred[...])
        dgu[rows, 0:half] = (d_act * up * (sig * (1.0 + gate * (1.0 - sig)))).astype(BF)
        dgu[rows, half:] = (d_act * silu).astype(BF)
        for own in (0, 1):
            mine = block_rows(chip * 2 + (core if own else 1 - core))
            parts[offset, own] = dot_t(dgu[mine, :], weight).astype(BF).reshape(2, 128, D)
            if not own:
                scatter2.give_at(offset)
        return carry

    lax.fori_loop(0, 4, mlp, 0)
    scatter2.far()
    gred_ref[...] = jnp.concatenate(
        [
            t_dot(act_ref[...], dy_all[...].reshape(2048, D)).reshape(4, 4, 24, D),
            jnp.zeros((4, 4, 8, D), F32),
        ],
        axis=2,
    ).astype(BF)

    line.sent()
    for copy in outs:
        copy.wait()
    outs.clear()
    write(gred_ref, gred_out, w_sem.at[6])

    def outcome(offset, carry):
        chip = lax.rem(z + offset, 4)
        y_part = dot(act_ref[chip_rows(chip), :], wred[...]).astype(BF).reshape(2, 2, 128, D)
        xall[offset * 2 + core] = y_part[1]
        xall[offset * 2 + 1 - core] = y_part[0]
        return carry

    lax.fori_loop(0, 4, outcome, 0)
    write(xall, yparts_out, w_sem.at[4])
    scatter2.last()
    gexp_ref[...] = t_dot(ball[...].reshape(2048, D), dgu[...]).astype(BF).reshape(4, 4, 64, EXP_COLS)
    write(gexp_ref, gexp_out, w_sem.at[7])
    first, second = scatter2.result()
    d_b = unorder(jnp.concatenate([first, second], axis=0), perm[...])
    hid = hid_ref[...]
    r = normed_rows(hid)
    dgain_ref[...] = jnp.broadcast_to(jnp.sum(d_b * hid * r, axis=0, keepdims=True), (8, D))
    dhid_ref[...] = dy_own[...].astype(F32) + rms_back(hid, r, d_b * gain)
    for one in (line_y, line_b, plane_g, plane_w, plane_o, plane_e, plane_r, scatter2):
        one.sent()
    for copy in cols + ecols:
        copy.wait_send()
    for copy in outs:
        copy.wait()


def first(*args):
    sh = jax.ShapeDtypeStruct
    held = [
        ((8, 2, 128, D), BF),
        ((2048, 384), F32),
        ((2048, 384), BF),
        ((2048, 256), BF),
        ((2048, 256), BF),
        ((2048, 128), F32),
    ]
    weight = ((D, IN_COLS), BF)
    wout = ((4, 4, 16, D), BF)
    early = [((256, D), F32), ((4, 4, RED_ROWS, D), BF), ((4, 4, 64, EXP_COLS), BF)]
    later = [((2048, 256), BF), ((2048, 128), F32)]
    return pl.pallas_call(
        first_kernel,
        out_shape=tuple(sh(*one) for one in held + [weight, wout] + later + held[:1])
        + tuple(sh(*one) for one in early)
        + (sh((16, 2304), F32), sh((256, D), F32), sh((8, D), F32)),
        in_specs=[VMEM] * 8 + [pl.BlockSpec(memory_space=pltpu.SMEM)],
        out_specs=[HBM] * 14 + [VMEM] * 3,
        scratch_shapes=[
            pltpu.VMEM(*one) for one in early + held + [((4, 4, 64, IN_COLS), BF), wout, weight] + later
        ]
        + [
            pltpu.VMEM((2048, FF // 8), BF),
            pltpu.VMEM((FF // 8, D), BF),
            pltpu.VMEM((8, 2, 128, D), BF),
            pltpu.VMEM((8, 8, IN_COLS + 128), F32),
            pltpu.VMEM((8, 8, IN_COLS + 128), F32),
            pltpu.VMEM((8, 8, EXP_COLS), F32),
            pltpu.VMEM((8, 8, EXP_COLS), F32),
            pltpu.VMEM((4, 4, 8, 256), F32),
            pltpu.VMEM((D, D), BF),
            pltpu.VMEM((2 * BLOCK, 256), F32),
            pltpu.VMEM((2 * BLOCK, 256), BF),
            pltpu.VMEM((4, 4, 64, EXP_COLS), BF),
            pltpu.VMEM((4, 4, RED_ROWS, D), BF),
            pltpu.VMEM((8, 2, 128, D), BF),
            pltpu.VMEM((2048, EXP_COLS), BF),
        ]
        + line_scatter_scratch(128, D)[:4]
        + [
            pltpu.SemaphoreType.DMA((n,))
            for n in (13, 13, 7, 7, 7, 7, 12, 12, 12, 12, 12, 12, 13, 13, 12, 12, 12, 12, 10, 10, 13, 13, 10, 10, 24, 8)
        ],
        compiler_params=pltpu.CompilerParams(
            collective_id=1, has_side_effects=True, vmem_limit_bytes=60 * 2**20
        ),
        name="first",
    )(*args)


def attend_back_block(
    i, q_ref, k_ref, v_ref, o_ref, lse_ref, do_ref,
    dk_ref, dv_ref, qs, dos, dqa,
):
    rows = block_rows(i)
    lane = lax.broadcasted_iota(jnp.int32, (BLOCK, HD), 1)
    for h in range(2):
        part = slice(h * BLOCK, (h + 1) * BLOCK)
        cols = slice(h * HD, (h + 1) * HD)
        qs[part, 0:HD] = q_ref[rows, cols]
        extra = q_ref[rows, 2 * HD :].astype(F32)
        for k, term in enumerate(in_three(lse_ref[rows, h : h + 1])):
            extra = jnp.where(lane == 4 + k, -term, extra)
        qs[part, HD:] = extra.astype(BF)
        d = do_ref[:, cols]
        dos[part, 0:HD] = d
        inner = jnp.sum(d.astype(F32) * o_ref[rows, cols].astype(F32), axis=1, keepdims=True)
        extra = jnp.zeros((BLOCK, HD), F32)
        for k, term in enumerate(in_three(inner)):
            extra = jnp.where(lane == k, -term, extra)
        dos[part, HD:] = extra.astype(BF)

    def step(kr, diagonal):
        p = jnp.exp2(dot_t(k_ref[kr, :], qs[...]) * SCORE)
        if diagonal:
            index = lax.broadcasted_iota(jnp.int32, (BLOCK, 2 * BLOCK), 0)
            query = lax.broadcasted_iota(jnp.int32, (BLOCK, 2 * BLOCK), 1) & (BLOCK - 1)
            p = jnp.where(index <= query, p, 0.0)
        ds = (p * dot_t(v_ref[kr, :], dos[...])).astype(BF)
        dv_ref[kr, :] += dot(p.astype(BF), dos[:, 0:HD])
        dk_ref[kr, :] += dot(ds, qs[:, 0:HD])
        dq = t_dot(ds, k_ref[kr, 0:HD])
        if diagonal:
            dqa[...] = dq
        else:
            dqa[...] += dq

    step(rows, True)

    def wide(j, carry):
        step(wide_rows(j), False)
        return carry

    def narrow(j, carry):
        step(block_rows(j), False)
        return carry

    lax.fori_loop(0, i // 2, wide, 0)
    lax.fori_loop(i // 2 * 2, i, narrow, 0)


def from_received(got, out, parts):
    col = 0
    for start, width in parts:
        for j in range(8):
            out[:, start + j * width : start + (j + 1) * width] = got[j, :, col : col + width]
        col += width


def back_kernel(
    wout_ref, gain_ref, dhid, dmid_ref,
    pred_in, pexp_in, q_in, k_in, v_in, o_in, lse_in, weight_in, yparts, raw_in, table_in, a_in, hid_in, x_in,
    y_ref, dx_ref, gred_ref, gout_ref, gin_out, gexp_out, dgain_ref,
    pred_ref, pexp_ref, q_ref, k_ref, v_ref, o_ref, lse_ref, weight, raw, table, hid, x_ref,
    qs, dos, dqa, dk_ref, dv_ref, dqkv, acc, column, parts_q, parts_kv, pout, perm, datt, do_ref,
    gin, gexp, csend, cgot, esend, egot, gsum, gdp, gx, gy,
    *rest,
):
    z, core, x, y = place()
    dp = lax.axis_index("dp")
    peers = dp_peers()
    greet(peers + plane_peers())
    parts = (parts_q, parts_kv)
    datt[dp] = dhid[...].astype(BF).reshape(2, 128, D)
    (ykeep, ytook, y_out, y_in, ys, yr), rest = rest[:6], rest[6:]
    (d_parts, took, out_z, in_z, ss, sr), rest = rest[:6], rest[6:]
    planes = [
        PlaneScatter(part, *rest[5 * n : 5 * n + 5])
        for n, part in enumerate((pred_ref, pexp_ref, pout, *parts))
    ]
    plane_out, plane_q, plane_kv = planes[2:]
    planes = planes[:2]
    c_send, c_recv, e_send, e_recv, g_send, g_recv, d_send, d_recv, in_sem = rest[25:]
    scatter = LineScatter(d_parts, took, out_z, in_z, ss, sr)
    y_scatter = LineScatter(yparts, ytook, y_out, y_in, ys, yr, ykeep)
    line = ChipGather(datt, d_send, d_recv)
    fetched = [
        pltpu.make_async_copy(src, dst, in_sem.at[n])
        for n, (src, dst) in enumerate(
            (
                (pred_in, pred_ref),
                (pexp_in, pexp_ref),
                (q_in, q_ref),
                (k_in, k_ref),
                (v_in, v_ref),
                (o_in, o_ref),
                (lse_in, lse_ref),
                (raw_in, raw),
                (table_in, table),
                (weight_in, weight),
                (yparts.at[:, 1], ykeep),
                (hid_in, hid),
                (x_in, x_ref),
            )
        )
    ]
    again = pltpu.make_async_copy(a_in, datt, in_sem.at[13])
    wout = wout_ref[...].reshape(256, D)
    for copy in fetched:
        copy.start()
    meet(peers + plane_peers())
    line.begin()
    for n in (0, 1):
        fetched[n].wait()
        planes[n].begin()
    dk_ref[...] = jnp.zeros_like(dk_ref)
    dv_ref[...] = jnp.zeros_like(dv_ref)
    gsum[...] = jnp.zeros_like(gsum)
    for copy in fetched[2:7]:
        copy.wait()

    def exchange(src, dst, send, recv):
        return [
            remote(src.at[lax.rem(dp + k, 8)], dst.at[dp], send.at[k - 1], recv.at[k - 1], peers[k - 1])
            for k in range(1, 8)
        ]

    ecols = exchange(esend, egot, e_send, e_recv)

    def through_norm(rows, part, d, tables):
        cos, sin = tables
        cols = slice(part * HD, (part + 1) * HD)
        u = raw[rows, cols]
        start = 2 * D + (HD if part == 2 else 0)
        gain = gain_ref[0:1, start : start + HD]
        d = d * HD**-0.5
        d = d * cos + pltpu.roll(d * sin, HD // 2, 1)
        r = lse_ref[rows, 2 + part : 3 + part]
        row = 16 + part // 2
        gsum[row : row + 1, :] += jnp.sum(d * u, axis=0, keepdims=True)
        d = d * gain
        dqkv[rows, cols] = (r * (d - u * jnp.mean(u * d, axis=-1, keepdims=True))).astype(BF)

    first = jnp.where(lax.broadcasted_iota(jnp.int32, (8, 128), 0) == 0, 1.0, 0.0)
    column[...] = lax.dot_general(
        gain_ref[8:16, 0:D],
        first,
        (((0,), (0,)), ((), ())),
        precision=lax.Precision.HIGHEST,
        preferred_element_type=F32,
    )

    def block(t, carry):
        offset = jnp.where(t < 2, 0, jnp.where(t >= 6, 2, jnp.where(lax.rem(t, 2) == 0, 1, 3)))
        second = jnp.where((t >= 2) & (t < 6), jnp.where(t >= 4, 1, 0), lax.rem(t, 2))
        i = lax.rem(z + offset, 4) * 2 + second

        @pl.when(t == 2)
        def _():
            line.first()

        @pl.when(t == 3)
        def _():
            for k in (2, 1, 3, 0):
                y_scatter.give(k)

        @pl.when(t == 4)
        def _():
            line.second()

        @pl.when(t == 6)
        def _():
            line.third()
            pout[...] = t_dot(o_ref[...], datt[...].reshape(2048, D)).astype(BF).reshape(4, 4, 16, D)
            plane_out.begin()

        rows = block_rows(i)
        do_ref[...] = dot_t(datt[i].reshape(256, D), wout).astype(BF)

        @pl.when(t == 7)
        def _():
            line.sent()
            again.start()

        attend_back_block(i, q_ref, k_ref, v_ref, o_ref, lse_ref, do_ref, dk_ref, dv_ref, qs, dos, dqa)
        @pl.when(t == 0)
        def _():
            for copy in fetched[7:]:
                copy.wait()

        tables = both_tables(table[rows, :])
        for part in range(2):
            through_norm(rows, part, dqa[part * BLOCK : (part + 1) * BLOCK, :], tables)

        @pl.when(t == 4)
        def _():
            y_scatter.far()
            y_scatter.near()

        @pl.when(t == 6)
        def _():
            y_scatter.last()

        @pl.when(t == 7)
        def _():
            again.wait()
            grad_columns(0)
            plane_q.begin()

        return carry

    def grad_columns(side):
        cols = slice(side * 256, side * 256 + 256)
        acc[...] = t_dot(datt[...].reshape(2048, D), dqkv[:, cols])
        parts[side][...] = (acc[...] * column[:, 0:1]).astype(BF).reshape(4, 4, 64, 256)
        inner = jnp.sum(acc[...] * weight[:, cols].astype(F32), axis=1, keepdims=True)
        if side == 0:
            column[:, 1:2] = inner
        return inner

    lax.fori_loop(0, 8, block, 0)

    def to_input(t, carry):
        offset = jnp.where(t == 0, 2, jnp.where(t == 1, 1, jnp.where(t == 2, 3, 0)))
        for own in (0, 1):
            rows = block_rows(lax.rem(z + offset, 4) * 2 + (core if own else 1 - core))
            through_norm(rows, 2, dk_ref[rows, :], both_tables(table[rows, :]))
            dqkv[rows, 384:512] = dv_ref[rows, :].astype(BF)
            d_parts[offset, own] = dot_t(dqkv[rows, :], weight[...]).astype(BF).reshape(2, 128, D)
            if not own:
                scatter.give_at(offset)

        @pl.when(t == 0)
        def _():
            scatter.far()

        @pl.when(t == 1)
        def _():
            scatter.near_right()

        @pl.when(t == 2)
        def _():
            scatter.near_left()

        return carry

    lax.fori_loop(0, 4, to_input, 0)
    inner = grad_columns(1) + column[:, 1:2]
    plane_kv.begin()
    plane_q.pass_on()
    for plane in planes:
        plane.pass_on()
    fill_order(perm)
    d_in = jnp.zeros((128, D), F32)
    for term in in_three(jnp.broadcast_to(inner, (D, 128))):
        d_in += lax.dot_general(
            term.astype(BF), perm[...], (((0,), (1,)), ((), ())), preferred_element_type=F32
        )
    d_in = d_in[0:1, :] * (1.0 / gain_ref[0:1, 0:D])
    for k in range(8):
        gsum[k : k + 1, :] = d_in[:, k * 128 : (k + 1) * 128]
        gsum[8 + k : 9 + k, :] = dmid_ref[0:1, k * 128 : (k + 1) * 128]
    dp_copies = [
        remote(gsum, gdp.at[k - 1], g_send.at[k - 1], g_recv.at[k - 1], peers[k - 1]) for k in range(1, 8)
    ]
    for copy in dp_copies:
        copy.start()

    scatter.last()
    plane_out.pass_on()
    planes[1].end(gexp)
    for j in range(8):
        esend[j] = gexp[8 * j : 8 * j + 8, :]
    egot[dp] = esend[dp]
    for copy in ecols:
        copy.start()

    def send_columns(plane, side):
        plane.end(gin)
        for j in range(8):
            csend[side, j] = gin[8 * j : 8 * j + 8, :]
        copies = exchange(csend.at[side], cgot.at[side], c_send.at[side], c_recv.at[side])
        for copy in copies:
            copy.start()
        cgot[side, dp] = csend[side, dp]
        return copies

    cols = send_columns(plane_q, 0)
    for copy in dp_copies:
        copy.wait_recv()
    total = gsum[...]
    for k in range(7):
        total += gdp[k]
    gx[0] = total
    x_copies = [
        remote(gx.at[0], gx.at[k], g_send.at[6 + k], g_recv.at[6 + k], device(z, core, x + k, y)) for k in (1, 2, 3)
    ]
    for copy in x_copies:
        copy.start()
    first, second = y_scatter.result()
    y_ref[...] = (hid[...] + jnp.concatenate([first, second], axis=0)).astype(BF)
    planes[0].end(gred_ref)
    plane_kv.pass_on()
    for copy in x_copies:
        copy.wait_recv()
    gy[0] = gx[0] + gx[1] + gx[2] + gx[3]
    y_copies = [
        remote(gy.at[0], gy.at[k], g_send.at[9 + k], g_recv.at[9 + k], device(z, core, x, y + k)) for k in (1, 2, 3)
    ]
    for copy in y_copies:
        copy.start()
    plane_out.end(gout_ref)
    for copy in ecols:
        copy.wait_recv()
    from_received(egot, gexp_out, ((0, 384), (FF, 384)))
    cols += send_columns(plane_kv, 1)
    first, second = scatter.result()
    d_a = unorder(jnp.concatenate([first, second], axis=0), perm[...])
    values = x_ref[...].astype(F32)
    dx_ref[...] = dhid[...] + rms_back(values, normed_rows(values), d_a)
    for copy in y_copies:
        copy.wait_recv()
    dgain_ref[...] = gy[0] + gy[1] + gy[2] + gy[3]
    for copy in cols:
        copy.wait_recv()
    from_received(cgot.at[0], gin_out, ((0, 256),))
    from_received(cgot.at[1], gin_out, ((H * HD, 128), ((H + KV) * HD, 128)))
    for copy in dp_copies + x_copies + y_copies + cols + ecols:
        copy.wait_send()
    for one in [scatter, y_scatter, plane_q, plane_kv, plane_out] + planes:
        one.sent()


def back(*args):
    sh = jax.ShapeDtypeStruct
    return pl.pallas_call(
        back_kernel,
        out_shape=(
            sh((256, D), BF),
            sh((256, D), F32),
            sh((RED_ROWS, D), F32),
            sh((16, D), F32),
            sh((8, 4096), F32),
            sh((8, 2 * FF), F32),
            sh((24, 128), F32),
        ),
        in_specs=[VMEM] * 4 + [HBM] * 14,
        out_specs=[VMEM] * 7,
        scratch_shapes=[
            pltpu.VMEM((4, 4, RED_ROWS, D), BF),
            pltpu.VMEM((4, 4, 64, EXP_COLS), BF),
            pltpu.VMEM((2048, 384), BF),
            pltpu.VMEM((2048, 256), BF),
            pltpu.VMEM((2048, 256), BF),
            pltpu.VMEM((2048, 256), BF),
            pltpu.VMEM((2048, 128), F32),
            pltpu.VMEM((D, IN_COLS), BF),
            pltpu.VMEM((2048, 384), F32),
            pltpu.VMEM((2048, 128), F32),
            pltpu.VMEM((256, D), F32),
            pltpu.VMEM((256, D), BF),
            pltpu.VMEM((2 * BLOCK, 256), BF),
            pltpu.VMEM((2 * BLOCK, 256), BF),
            pltpu.VMEM((2 * BLOCK, HD), F32),
            pltpu.VMEM((2048, HD), F32),
            pltpu.VMEM((2048, HD), F32),
            pltpu.VMEM((2048, IN_COLS), BF),
            pltpu.VMEM((D, 256), F32),
            pltpu.VMEM((D, 128), F32),
            pltpu.VMEM((4, 4, 64, 256), BF),
            pltpu.VMEM((4, 4, 64, 256), BF),
            pltpu.VMEM((4, 4, 16, D), BF),
            pltpu.VMEM((D, D), BF),
            pltpu.VMEM((8, 2, 128, D), BF),
            pltpu.VMEM((BLOCK, 256), BF),
            pltpu.VMEM((64, 256), F32),
            pltpu.VMEM((64, EXP_COLS), F32),
            pltpu.VMEM((2, 8, 8, 256), F32),
            pltpu.VMEM((2, 8, 8, 256), F32),
            pltpu.VMEM((8, 8, EXP_COLS), F32),
            pltpu.VMEM((8, 8, EXP_COLS), F32),
            pltpu.VMEM((24, 128), F32),
            pltpu.VMEM((7, 24, 128), F32),
            pltpu.VMEM((4, 24, 128), F32),
            pltpu.VMEM((4, 24, 128), F32),
        ]
        + [pltpu.VMEM((4, 2, 128, D), BF)]
        + line_scatter_scratch(128, D)[1:]
        + line_scatter_scratch(128, D)
        + plane_scatter_scratch(RED_ROWS, D)
        + plane_scatter_scratch(64, EXP_COLS)
        + plane_scatter_scratch(16, D)
        + plane_scatter_scratch(64, 256)
        + plane_scatter_scratch(64, 256)
        + [pltpu.SemaphoreType.DMA((2, 7)), pltpu.SemaphoreType.DMA((2, 7))]
        + [pltpu.SemaphoreType.DMA((n,)) for n in (7, 7, 13, 13, 13, 13, 14)],
        compiler_params=pltpu.CompilerParams(
            collective_id=3, has_side_effects=True, vmem_limit_bytes=60 * 2**20
        ),
        name="back",
    )(*args)


def update_kernel(*refs):
    weights, grads, firsts, seconds = (refs[5 * n : 5 * n + 5] for n in range(4))
    y_ref, dx_ref, y_out, dx_out = refs[20:24]
    news, means, squares = (refs[24 + 5 * n : 29 + 5 * n] for n in range(3))
    y_out[...] = y_ref[...]
    dx_out[...] = dx_ref[...]
    for k in range(4):
        news[k][...], means[k][...], squares[k][...] = adam_step(
            weights[k][...],
            grads[k][0 : weights[k].shape[0], :],
            firsts[k][...],
            seconds[k][...],
            matrix_rate,
            matrix_decay,
        )
    own = weights[4].shape[1]
    first = (lax.axis_index("dp") * 16 + lax.axis_index("shard")) * own
    row, col = first // 128, lax.rem(first, 128)
    lane = lax.broadcasted_iota(jnp.int32, (8, 128), 1)
    here = pltpu.roll(jnp.broadcast_to(grads[4][pl.ds(row, 1), :], (8, 128)), lax.rem(128 - col, 128), 1)
    after = pltpu.roll(jnp.broadcast_to(grads[4][pl.ds(row + 1, 1), :], (8, 128)), lax.rem(128 - col, 128), 1)
    grad = jnp.where(lane < 128 - col, here, after)[0:1, 0:own]
    news[4][...], means[4][...], squares[4][...] = adam_step(
        weights[4][...], grad, firsts[4][...], seconds[4][...], gain_rate, 0.0
    )


def update(weights, grads, firsts, seconds, y, dx):
    like = tuple(jax.ShapeDtypeStruct(w.shape, F32) for w in weights)
    return pl.pallas_call(
        update_kernel,
        out_shape=(jax.ShapeDtypeStruct(y.shape, BF), jax.ShapeDtypeStruct(dx.shape, F32)) + like * 3,
        in_specs=[VMEM] * 22,
        out_specs=[VMEM] * 17,
        compiler_params=pltpu.CompilerParams(vmem_limit_bytes=60 * 2**20),
        name="update",
    )(*weights, *grads, *firsts, *seconds, y, dx)


def body(
    tokens,
    cotangent,
    lengths,
    weight_input,
    weight_output,
    weight_expand,
    weight_reduce,
    gains,
    first_input,
    first_output,
    first_expand,
    first_reduce,
    first_gains,
    second_input,
    second_output,
    second_expand,
    second_reduce,
    second_gains,
):
    a, raw, q, k, v, table, win, wout, o, lse, y_parts, hid, part_red, part_exp, gain, d_hid, d_gain_mid = first(
        tokens[0],
        weight_input,
        weight_expand,
        gains[None],
        rope_rates(),
        weight_output,
        weight_reduce,
        cotangent[0],
        lengths,
    )
    block_out, input_grad, grad_reduce, grad_output, grad_input, grad_expand, grad_gains = back(
        wout, gain, d_hid, d_gain_mid, part_red, part_exp,
        q, k, v, o, lse, win, y_parts.reshape(4, 2, 2, 128, D), raw, table, a, hid, tokens[0],
    )
    block_out, input_grad, *done = update(
        (weight_input, weight_output, weight_expand, weight_reduce, gains[None]),
        (grad_input, grad_output, grad_expand, grad_reduce, grad_gains),
        (first_input, first_output, first_expand, first_reduce, first_gains[None]),
        (second_input, second_output, second_expand, second_reduce, second_gains[None]),
        block_out,
        input_grad,
    )
    done = [one[0] if n % 5 == 4 else one for n, one in enumerate(done)]
    return (block_out[None], input_grad[None], *done)


def solution(mesh):
    placed = (
        P("shard", "dp", None),
        P("shard", "dp", None),
        P("shard", None),
        P(("dp", "shard"), None),
        P(("dp", "shard"), None),
        P(("dp", "shard"), None),
        P(("dp", "shard"), None),
        P(("dp", "shard")),
        P(("dp", "shard"), None),
        P(("dp", "shard"), None),
        P(("dp", "shard"), None),
        P(("dp", "shard"), None),
        P(("dp", "shard")),
        P(("dp", "shard"), None),
        P(("dp", "shard"), None),
        P(("dp", "shard"), None),
        P(("dp", "shard"), None),
        P(("dp", "shard")),
    )
    return jax.shard_map(
        body,
        mesh=mesh,
        in_specs=placed,
        out_specs=(
            P("shard", "dp", None),
            P("shard", "dp", None),
            P(("dp", "shard"), None),
            P(("dp", "shard"), None),
            P(("dp", "shard"), None),
            P(("dp", "shard"), None),
            P(("dp", "shard")),
            P(("dp", "shard"), None),
            P(("dp", "shard"), None),
            P(("dp", "shard"), None),
            P(("dp", "shard"), None),
            P(("dp", "shard")),
            P(("dp", "shard"), None),
            P(("dp", "shard"), None),
            P(("dp", "shard"), None),
            P(("dp", "shard"), None),
            P(("dp", "shard")),
        ),
        check_vma=False,
    )
```
